256 devices in a mesh: row: 16 (over x_hi, y, core), chan: 16 (over z, x_lo).
Axes of the slice: x: 4 (x_hi: 2, x_lo: 2; x = x_hi * 2 + x_lo), y: 4, z: 8, core: 2. Of those that a mesh axis runs over, the one named last changes fastest.
Arguments:
- frames: bfloat16 [4, 128, 256, 128], P(None, 'row', 'chan'), may hold values from -11 to 11
- cache: bfloat16 [2, 2, 128, 256, 128], P(None, None, 'row', 'chan'), may hold values from -4 to 4
- norm_gain: float32 [2, 256], P(None, 'chan'), may hold values from 0.25 to 1.75
- norm_shift: float32 [2, 256], P(None, 'chan'), may hold values from -1.5 to 1.5
- conv_weight: bfloat16 [2, 256, 27, 256], P(None, 'chan'), may hold values from -0.078125 to 0.078125
- conv_bias: float32 [2, 256], P(None, 'chan'), may hold values from -1.5 to 1.5
Outputs:
- decoded: bfloat16 [4, 128, 256, 128], P(None, 'row', 'chan')
The draws below stay inside these ranges and needn't reach their ends.
All inputs are finite; a program needn't handle non-finite values.
Results may differ from the reference program's by a relative error of at most 0.0095.
Values may be sent and summed in bfloat16 or wider, within the bound.
No kernel may reach another device: no remote copies, remote signals or barrier semaphores. Data moves between devices by JAX's collectives and lax.ppermute only.
A program may use at most 64 MiB of HBM per device.

```python
import jax
import jax.numpy as jnp
from jax import lax

CH = 256
GROUPS = 32
FRAMES = 4
CACHE = 2
BLOCKS = 1
W = 128
ROWS = 128


def draw_frames(key, part):
    key = jax.random.fold_in(key, 11)
    first_key = jax.random.fold_in(key, 0)
    extent = (FRAMES, ROWS, CH, W)
    position = jnp.arange(ROWS).astype(jnp.float32) / (ROWS - 1)
    sample = jax.random.truncated_normal(first_key, -6.0, 6.0, extent, jnp.float32)
    row_scale = 0.6 + 1.2 * position
    values = sample * row_scale[None, :, None, None]
    return values.astype(jnp.bfloat16)


def levels(key, shape, shards, least, high):
    def one(axis_at, shards_of):
        draws = jax.random.uniform(jax.random.fold_in(jax.random.fold_in(key, 6), axis_at), (shards_of,), jnp.float32, least / len(shards), high / len(shards))
        return jnp.repeat(jnp.exp(draws), shape[axis_at] // shards_of).reshape((-1,) + (1,) * (len(shape) - axis_at - 1))

    level = one(*shards[0])
    for cut in shards[1:]:
        level = level * one(*cut)
    return level


def gaussian(own_key, shape, deviation, most, cuts=(), held_as=jnp.bfloat16):
    entries = deviation * jax.random.normal(own_key, shape, jnp.float32)
    if cuts:
        entries = entries * levels(own_key, shape, cuts, -0.22, 0.18)
    return jnp.clip(entries, -most, most).astype(held_as)


def setup_inputs(seed: int = 0) -> dict:
    streams_of = jax.random.split(jax.random.key(seed), 7)
    frames = draw_frames(jax.random.fold_in(streams_of[6], 71), 0)
    cache = gaussian(streams_of[1], (2 * BLOCKS, CACHE, ROWS, CH, W), 0.7, 4.0, ((2, 16), (3, 16)))
    norm_gain = jnp.clip(1.0 + 0.15 * jax.random.normal(streams_of[2], (2 * BLOCKS, CH), jnp.float32), 0.25, 1.75)
    norm_shift = gaussian(streams_of[3], (2 * BLOCKS, CH), 0.3, 1.5, ((1, 16),), jnp.float32)
    conv_weight = gaussian(streams_of[4], (2 * BLOCKS, CH, 27, CH), (27 * CH) ** -0.5, 0.078125, ((1, 16),))
    conv_bias = gaussian(streams_of[5], (2 * BLOCKS, CH), 0.3, 1.5, ((1, 16),), jnp.float32)
    return dict(frames=frames, cache=cache, norm_gain=norm_gain, norm_shift=norm_shift, conv_weight=conv_weight, conv_bias=conv_bias)


def group_silu(values, gain, shift):
    grouped = values.reshape(FRAMES, ROWS, GROUPS, CH // GROUPS, W)
    means = lax.optimization_barrier(jnp.mean(grouped, axis=(0, 1, 3, 4), keepdims=True))
    centred = grouped - means
    spread = lax.optimization_barrier(jnp.mean(centred * centred, axis=(0, 1, 3, 4), keepdims=True))
    scaled = (centred * lax.rsqrt(spread + 1e-06)).reshape(FRAMES, ROWS, CH, W)
    shifted = scaled * gain[None, None, :, None] + shift[None, None, :, None]
    return jax.nn.silu(shifted).astype(jnp.bfloat16)

def convolve(history, normed, weights, bias):
    joined = jnp.concatenate([history, normed], axis=0).astype(jnp.float32)
    joined = jnp.transpose(joined, (2, 0, 1, 3))[None]
    kernel = weights.astype(jnp.float32).reshape(CH, 3, 3, 3, CH)
    kernel = jnp.transpose(kernel, (0, 4, 1, 2, 3))
    result = lax.conv_general_dilated(joined, kernel, (1, 1, 1), ((0, 0), (1, 1), (1, 1)), dimension_numbers=('NCDHW', 'OIDHW', 'NCDHW'), precision=lax.Precision.HIGHEST)
    return jnp.transpose(result[0], (1, 2, 0, 3)) + bias[None, None, :, None]

def reference(frames, cache, norm_gain, norm_shift, conv_weight, conv_bias):
    current = frames
    for section in range(BLOCKS):
        lower = 2 * section
        upper = 2 * section + 1
        first_act = group_silu(current.astype(jnp.float32), norm_gain[lower], norm_shift[lower])
        middle = convolve(cache[lower], first_act, conv_weight[lower], conv_bias[lower]).astype(jnp.bfloat16)
        second_act = group_silu(middle.astype(jnp.float32), norm_gain[upper], norm_shift[upper])
        branch = convolve(cache[upper], second_act, conv_weight[upper], conv_bias[upper])
        current = (current.astype(jnp.float32) + branch).astype(jnp.bfloat16)
    return current
```

```python
import jax
import jax.numpy as jnp
from jax import lax
from jax.experimental import pallas as pl
from jax.experimental.pallas import tpu as pltpu
from jax.sharding import Mesh, PartitionSpec as P

CH = 256
GROUP = 8
EPS = 1e-06
BF16 = jnp.bfloat16
F32 = jnp.float32

ROW = ("xh", "y", "core")
LINE = ("xh", "y", "core", "z")
CHAN = ("z", "xl")


def dot(a, b):
    return lax.dot_general(a, b, (((1,), (0,)), ((), ())), preferred_element_type=F32)


def silu(u):
    return u / (1.0 + jnp.exp(-u))


def call(kernel, outs, *args, smem=(), scratch=(), flops=0):
    specs = [
        pl.BlockSpec(memory_space=pltpu.SMEM if i in smem else pltpu.VMEM) for i in range(len(args))
    ]
    moved = sum(a.size * a.dtype.itemsize for a in args)
    return pl.pallas_call(
        kernel,
        out_shape=outs,
        in_specs=specs,
        out_specs=jax.tree.map(lambda _: pl.BlockSpec(memory_space=pltpu.VMEM), outs),
        scratch_shapes=list(scratch),
        compiler_params=pltpu.CompilerParams(vmem_limit_bytes=40 * 1024 * 1024),
        cost_estimate=pl.CostEstimate(flops=flops, bytes_accessed=moved, transcendentals=0),
    )(*args)


def stats_kernel(x_ref, o_ref):
    x = x_ref[...].astype(F32).reshape(32, 2, GROUP, 128)
    mean = jnp.sum(x, axis=(0, 2), keepdims=True) / (32 * GROUP)
    off = x - mean
    square = jnp.sum(off * off, axis=(0, 2))
    both = jnp.concatenate([mean.reshape(2, 128), square], axis=0)
    o_ref[...] = jnp.broadcast_to(both[None], o_ref.shape)


def pack_kernel(cache_ref, up_ref, down_ref, first_ref, second_ref):
    for layer, out_ref in ((0, first_ref), (1, second_ref)):
        for z in range(8):
            for dr in range(3):
                row = z + dr - 1
                for t in range(2):
                    if row < 0:
                        slab = up_ref[4 + 2 * layer + t]
                    elif row > 7:
                        slab = down_ref[4 + 2 * layer + t]
                    else:
                        slab = cache_ref[layer, t, row]
                    lanes = slice(128 * t, 128 * (t + 1))
                    if layer == 0:
                        out_ref[2 * z, dr, :, lanes] = slab
                        out_ref[2 * z + 1, dr, :, lanes] = slab
                    else:
                        out_ref[z, dr, :, lanes] = slab


def norm_kernel(edge_ref, x_ref, up_ref, down_ref, stats_ref, affine_ref, o_ref):
    stats = stats_ref[...]
    means = stats[:, 0:2]
    mean = jnp.mean(means, axis=(0, 2), keepdims=True)
    off = means - mean
    total = jnp.sum(stats[:, 2:4] + (32 * GROUP) * (off * off), axis=(0, 2), keepdims=True)
    number = stats.shape[0] * 128 * 32 * GROUP
    inverse = lax.rsqrt(total / number + EPS)
    mean = jnp.broadcast_to(mean.reshape(2, 1, 1), (2, GROUP, 128)).reshape(16, 128)
    inverse = jnp.broadcast_to(inverse.reshape(2, 1, 1), (2, GROUP, 128)).reshape(16, 128)
    gain = affine_ref[0] * inverse
    shift = affine_ref[1]
    for row in range(-1, 9):
        for t in range(4):
            if row < 0:
                x = up_ref[t]
            elif row > 7:
                x = down_ref[t]
            else:
                x = x_ref[t, row]
            y = silu((x.astype(F32) - mean) * gain + shift)
            if row < 0:
                y = y * edge_ref[0]
            if row > 7:
                y = y * edge_ref[1]
            y = y.astype(BF16)
            for dr in range(3):
                z = row - dr + 1
                if 0 <= z < 8:
                    for xl in range(2):
                        o_ref[2 * z + xl, dr, :, 128 * t : 128 * (t + 1)] = y


def shift_columns(left, centre, right):
    lane = lax.broadcasted_iota(jnp.int32, left.shape, left.ndim - 1)
    axis = left.ndim - 1
    left = jnp.where(lane == 0, 0.0, pltpu.roll(left, 1, axis))
    right = jnp.where(lane == 127, 0.0, pltpu.roll(right, 127, axis))
    return left + centre + right


def first_kernel(x_ref, cache_ref, w_ref, mid_ref, stats_ref, affine_ref, slab_ref, prod_ref):
    for dr in range(3):
        for c in range(16):
            rows = slice(256 * dr + 16 * c, 256 * dr + 16 * c + 16)
            slab_ref[rows, 0:256] = cache_ref[c, dr]
            slab_ref[rows, 256:768] = x_ref[c, dr]
    w = w_ref[...].reshape(384, 2432)
    prod = dot(w[:, 0:768], slab_ref[:, 0:512])
    prod += dot(w[:, 768:1536], slab_ref[:, 128:640])
    prod += dot(w[:, 1536:2304], slab_ref[:, 256:768])
    prod_ref[...] = prod.reshape(8, 3, 16, 512)
    coded = w_ref[:, 0:16, 2304:2432].reshape(128, 128).astype(F32)
    bias = coded[:, 0:1] + coded[:, 1:2] + coded[:, 2:3]
    gain = coded[:, 3:4] + coded[:, 4:5] + coded[:, 5:6]
    shift = coded[:, 6:7] + coded[:, 7:8] + coded[:, 8:9]
    affine_ref[0] = jnp.broadcast_to(gain, (128, 128))
    affine_ref[1] = jnp.broadcast_to(shift, (128, 128))
    parts = []
    for t in range(4):
        lanes = slice(128 * t, 128 * (t + 1))
        summed = shift_columns(
            prod_ref[:, 0, :, lanes].reshape(128, 128),
            prod_ref[:, 1, :, lanes].reshape(128, 128),
            prod_ref[:, 2, :, lanes].reshape(128, 128),
        )
        part = (summed + bias).astype(BF16)
        mid_ref[:, lanes] = part
        parts.append(part.astype(F32))
    mean = jnp.sum(parts[0] + parts[1] + parts[2] + parts[3], axis=1, keepdims=True) / 512
    squares = jnp.zeros((128, 128), F32)
    for part in parts:
        off = part - mean
        squares += off * off
    square = jnp.sum(squares, axis=1, keepdims=True)
    same = lax.broadcasted_iota(jnp.int32, (128, 128), 0) == lax.broadcasted_iota(
        jnp.int32, (128, 128), 1
    )
    mean = jnp.sum(jnp.where(same, mean, 0.0), axis=0, keepdims=True)
    square = jnp.sum(jnp.where(same, square, 0.0), axis=0, keepdims=True)
    both = jnp.concatenate([mean, square], axis=0)
    stats_ref[...] = jnp.broadcast_to(both[None], stats_ref.shape)


def second_kernel(
    edge_ref, mid_ref, up_ref, down_ref, stats_ref, affine_ref, cache_ref, w_ref, o_ref, slab_ref, prod_ref
):
    stats = stats_ref[...]
    peers = stats.shape[0]
    means = stats[:, 0:1]
    mean = jnp.mean(means, axis=0, keepdims=True)
    off = means - mean
    square = jnp.sum(stats[:, 1:2] + 512.0 * (off * off), axis=0)
    mean = mean.reshape(1, 128)
    same = lax.broadcasted_iota(jnp.int32, (128, 128), 0) == lax.broadcasted_iota(
        jnp.int32, (128, 128), 1
    )
    mean = jnp.sum(jnp.where(same, mean, 0.0), axis=1, keepdims=True)
    square = jnp.sum(jnp.where(same, square, 0.0), axis=1, keepdims=True)
    mean = jnp.broadcast_to(mean, (128, 128)).reshape(16, GROUP, 128)
    square = jnp.broadcast_to(square, (128, 128)).reshape(16, GROUP, 128)
    group = jnp.mean(mean, axis=1, keepdims=True)
    off = mean - group
    total = jnp.sum(square + (512.0 * peers) * (off * off), axis=1, keepdims=True)
    inverse = lax.rsqrt(total / (512.0 * peers * GROUP) + EPS)
    group = jnp.broadcast_to(group, (16, GROUP, 128)).reshape(128, 128)
    inverse = jnp.broadcast_to(inverse, (16, GROUP, 128)).reshape(128, 128)
    gain = affine_ref[0] * inverse
    shift = affine_ref[1]
    for dr, ref in ((0, up_ref), (1, mid_ref), (2, down_ref)):
        for t in range(4):
            x = ref[:, 128 * t : 128 * (t + 1)].astype(F32)
            y = silu((x - group) * gain + shift)
            if dr == 0:
                y = y * edge_ref[2]
            if dr == 2:
                y = y * edge_ref[3]
            slab_ref[128 * dr : 128 * (dr + 1), 256 + 128 * t : 384 + 128 * t] = y.astype(BF16)
        for z in range(8):
            slab_ref[128 * dr + 16 * z : 128 * dr + 16 * z + 16, 0:256] = cache_ref[z, dr]
    w = w_ref[...].reshape(768, 1152)
    prod = dot(w[:, 0:384], slab_ref[:, 0:512])
    prod += dot(w[:, 384:768], slab_ref[:, 128:640])
    prod += dot(w[:, 768:1152], slab_ref[:, 256:768])
    prod_ref[...] = prod.reshape(16, 3, 16, 512)
    for t in range(4):
        lanes = slice(128 * t, 128 * (t + 1))
        summed = shift_columns(
            prod_ref[:, 0, :, lanes].reshape(256, 128),
            prod_ref[:, 1, :, lanes].reshape(256, 128),
            prod_ref[:, 2, :, lanes].reshape(256, 128),
        )
        o_ref[:, :, lanes] = summed.astype(BF16).reshape(16, 16, 128)


def last_kernel(x_ref, part_ref, bias_ref, o_ref):
    bias = bias_ref[...]
    for z in range(8):
        for t in range(4):
            lanes = slice(128 * t, 128 * (t + 1))
            branch = part_ref[2 * z, :, lanes].astype(F32) + part_ref[2 * z + 1, :, lanes].astype(F32)
            o_ref[t, z] = (x_ref[t, z].astype(F32) + (branch + bias)).astype(BF16)


def split(value):
    high = lax.reduce_precision(value, 8, 7)
    rest = value - high
    middle = lax.reduce_precision(rest, 8, 7)
    return [part.astype(BF16) for part in (high, middle, rest - middle)]


def first_weights(weight, bias, gain, shift):
    weight = weight.reshape(16, 9, 3, CH).transpose(2, 0, 1, 3).reshape(48, 9 * CH)
    coded = jnp.stack(split(bias) + split(gain) + split(shift), axis=1)
    coded = jnp.pad(coded, ((0, 32), (0, 119)))
    return lax.all_gather(jnp.concatenate([weight, coded], axis=1), "z")


def second_weights(weight):
    me = lax.axis_index("xl")
    weight = weight.reshape(16, 9, 3, 8, 2, 16).transpose(4, 2, 0, 1, 3, 5).reshape(2, 48, 1152)
    mine = jnp.where(me == 0, weight[0], weight[1])
    other = jnp.where(me == 0, weight[1], weight[0])
    other = lax.ppermute(other, "xl", [(0, 1), (1, 0)])
    first = jnp.where(me == 0, mine, other)
    second = jnp.where(me == 0, other, mine)
    return lax.all_gather(jnp.concatenate([first, second], axis=0), "z")


def both_ways(x_up, x_down, axes):
    size = 1
    for axis in axes:
        size *= lax.axis_size(axis)
    up = [(i, i + 1) for i in range(size - 1)]
    down = [(i + 1, i) for i in range(size - 1)]
    return lax.ppermute(x_up, axes, up), lax.ppermute(x_down, axes, down)


def exchange(x, axes):
    return lax.all_to_all(x, axes, 0, 0, tiled=True)


def struct(shape, dtype=BF16):
    return jax.ShapeDtypeStruct(shape, dtype)


def local(frames, cache, norm_gain, norm_shift, conv_weight, conv_bias):
    row = lax.axis_index(ROW)
    line = lax.axis_index(LINE)
    edge = jnp.stack([row > 0, row < 15, line > 0, line < 127]).astype(F32)

    stats = call(stats_kernel, struct((16, 4, 128), F32), frames)
    stats = exchange(stats, ROW)

    joined = [frames, cache[0], cache[1]]
    last = jnp.concatenate([x[:, 7] for x in joined], axis=0)
    first = jnp.concatenate([x[:, 0] for x in joined], axis=0)
    above, below = both_ways(last, first, ROW)

    w0 = first_weights(conv_weight[0], conv_bias[0], norm_gain[1], norm_shift[1])
    w1 = second_weights(conv_weight[1])

    c0, c1 = call(
        pack_kernel, (struct((16, 3, 16, 256)), struct((8, 3, 16, 256))), cache, above, below
    )
    c0 = exchange(c0, CHAN)
    c1 = exchange(c1, "z")

    affine = jnp.broadcast_to(jnp.stack([norm_gain[0], norm_shift[0]])[:, :, None], (2, 16, 128))
    normed = call(
        norm_kernel, struct((16, 3, 16, 512)), edge, frames, above, below, stats, affine, smem=(0,)
    )
    normed = exchange(normed, CHAN)

    middle, stats, affine = call(
        first_kernel,
        (struct((128, 512)), struct((128, 2, 128), F32), struct((2, 128, 128), F32)),
        normed,
        c0,
        w0,
        scratch=(pltpu.VMEM((768, 768), BF16), pltpu.VMEM((8, 3, 16, 512), F32)),
        flops=2 * 384 * 2304 * 512,
    )
    stats = exchange(stats, LINE)
    above, below = both_ways(middle, middle, LINE)

    partial = call(
        second_kernel,
        struct((16, 16, 512)),
        edge,
        middle,
        above,
        below,
        stats,
        affine,
        c1,
        w1,
        smem=(0,),
        scratch=(pltpu.VMEM((384, 768), BF16), pltpu.VMEM((16, 3, 16, 512), F32)),
        flops=2 * 768 * 1152 * 512,
    )
    partial = exchange(partial, CHAN)
    bias = jnp.broadcast_to(conv_bias[1][:, None], (16, 128))
    return call(last_kernel, struct((4, 8, 16, 128)), frames, partial, bias)


def solution(mesh):
    fine = Mesh(mesh.devices.reshape(2, 4, 2, 8, 2), ("xh", "y", "core", "z", "xl"))
    placed = (
        P(None, ROW, CHAN, None),
        P(None, None, ROW, CHAN, None),
        P(None, CHAN),
        P(None, CHAN),
        P(None, CHAN, None, None),
        P(None, CHAN),
    )
    return jax.shard_map(
        local, mesh=fine, in_specs=placed, out_specs=P(None, ROW, CHAN, None), check_vma=False
    )
```

```python
import jax
import jax.numpy as jnp
from jax import lax
from jax.experimental import pallas as pl
from jax.experimental.pallas import tpu as pltpu
from jax.sharding import Mesh, PartitionSpec as P

GROUP = 8
EPS = 1e-06
BF16 = jnp.bfloat16
F32 = jnp.float32

ROW = ("xh", "y", "core")
CHAN = ("zh", "zl", "xl")
NEAR = ("zl", "xl")


def dot(a, b):
    return lax.dot_general(a, b, (((1,), (0,)), ((), ())), preferred_element_type=F32)


def silu(u):
    return u / (1.0 + jnp.exp(-u))


def call(kernel, outs, *args, smem=(), scratch=(), flops=0):
    specs = [
        pl.BlockSpec(memory_space=pltpu.SMEM if i in smem else pltpu.VMEM) for i in range(len(args))
    ]
    moved = sum(a.size * a.dtype.itemsize for a in args)
    return pl.pallas_call(
        kernel,
        out_shape=outs,
        in_specs=specs,
        out_specs=jax.tree.map(lambda _: pl.BlockSpec(memory_space=pltpu.VMEM), outs),
        scratch_shapes=list(scratch),
        compiler_params=pltpu.CompilerParams(vmem_limit_bytes=40 * 1024 * 1024),
        cost_estimate=pl.CostEstimate(flops=flops, bytes_accessed=moved, transcendentals=0),
    )(*args)


def put_stats(x, gain_ref, shift_ref, layer, note_ref, stats_ref):
    number = x.shape[0] * GROUP
    mean = jnp.sum(x, axis=(0, 2), keepdims=True) / number
    off = x - mean
    square = jnp.sum(off * off, axis=(0, 2))
    note_ref[...] = jnp.zeros((8, 128), F32)
    note_ref[0:2] = mean.reshape(2, 128)
    note_ref[2:4] = square
    note_ref[4:5, 0:16] = gain_ref[layer : layer + 1, :]
    note_ref[5:6, 0:16] = shift_ref[layer : layer + 1, :]
    stats_ref[...] = jnp.broadcast_to(note_ref[...][None], stats_ref.shape)


def begin_kernel(x_ref, cache_ref, gain_ref, shift_ref, raw_ref, later_ref, stats_ref, note_ref):
    for r in range(8):
        for t in range(2):
            lanes = slice(128 * t, 128 * (t + 1))
            raw_ref[r, :, lanes] = cache_ref[0, t, r]
            later_ref[r, :, lanes] = cache_ref[1, t, r]
        for t in range(4):
            raw_ref[r, :, 256 + 128 * t : 384 + 128 * t] = x_ref[t, r]
    x = x_ref[...].astype(F32).reshape(32, 2, GROUP, 128)
    put_stats(x, gain_ref, shift_ref, 0, note_ref, stats_ref)


def shift_columns(left, centre, right):
    lane = lax.broadcasted_iota(jnp.int32, left.shape, left.ndim - 1)
    axis = left.ndim - 1
    left = jnp.where(lane == 0, 0.0, pltpu.roll(left, 1, axis))
    right = jnp.where(lane == 127, 0.0, pltpu.roll(right, 127, axis))
    return left + centre + right


def get_affine(stats_ref, affine_ref):
    stats = stats_ref[...].reshape(16, 4, 8, 128)
    number = 32 * GROUP
    means = stats[:, :, 0:2]
    mean = jnp.mean(means, axis=(0, 3), keepdims=True)
    off = means - mean
    total = jnp.sum(stats[:, :, 2:4] + number * (off * off), axis=(0, 3), keepdims=True)
    inverse = lax.rsqrt(total / (number * 16 * 128) + EPS)
    mean = jnp.broadcast_to(mean.reshape(4, 2, 1, 1), (4, 2, GROUP, 128)).reshape(4, 16, 128)
    inverse = jnp.broadcast_to(inverse.reshape(4, 2, 1, 1), (4, 2, GROUP, 128)).reshape(4, 16, 128)
    shape = (4, 16, 128)
    same = lax.broadcasted_iota(jnp.int32, shape, 1) == lax.broadcasted_iota(jnp.int32, shape, 2)
    gain = jnp.sum(jnp.where(same, stats[0, :, 4:5], 0.0), axis=2, keepdims=True)
    shift = jnp.sum(jnp.where(same, stats[0, :, 5:6], 0.0), axis=2, keepdims=True)
    affine_ref[0] = mean
    affine_ref[1] = inverse * gain
    affine_ref[2] = jnp.broadcast_to(shift, shape)


def convolve(layer, place_ref, w_refs, o_ref, slab_ref, held_ref):
    for q, w_ref in enumerate(w_refs):
        for dt in range(3):
            held_ref[dt, q] = w_ref[layer, dt]
    for r in range(8):
        rows = slab_ref[r : r + 3].reshape(192, 768)
        prod = dot(held_ref[0].reshape(192, 192), rows[:, 0:512])
        prod += dot(held_ref[1].reshape(192, 192), rows[:, 128:640])
        prod += dot(held_ref[2].reshape(192, 192), rows[:, 256:768])
        prod = prod.reshape(4, 3, 16, 512)
        for t in range(4):
            lanes = slice(128 * t, 128 * (t + 1))
            part = prod[:, :, :, lanes]
            summed = shift_columns(part[:, 0], part[:, 1], part[:, 2]).astype(BF16)
            for q in range(4):
                o_ref[lax.rem(place_ref[1] + (4 - q), 4), r, :, lanes] = summed[q]


def norm_rows(x_of, place_ref, edge_ref, affine_ref, slab_ref):
    for k in range(4):
        b = place_ref[2 + k]
        mean = affine_ref[0, b]
        gain = affine_ref[1, b]
        shift = affine_ref[2, b]
        for r in range(10):
            for t in range(4):
                y = silu((x_of(k, r, t).astype(F32) - mean) * gain + shift)
                if r == 0:
                    y = y * edge_ref[0]
                if r == 9:
                    y = y * edge_ref[1]
                slab_ref[r, b, :, 256 + 128 * t : 384 + 128 * t] = y.astype(BF16)


def first_kernel(
    place_ref, edge_ref, a_ref, b_ref, c_ref, d_ref, stats_ref, w0, w1, w2, w3, o_ref, affine_ref, slab_ref, held_ref
):
    get_affine(stats_ref, affine_ref)
    refs = (a_ref, b_ref, c_ref, d_ref)
    for k in range(4):
        b = place_ref[2 + k]
        for r in range(10):
            slab_ref[r, b, :, 0:256] = refs[k][r, :, 0:256]

    def x_of(k, r, t):
        return refs[k][r, :, 256 + 128 * t : 384 + 128 * t]

    norm_rows(x_of, place_ref, edge_ref, affine_ref, slab_ref)
    convolve(0, place_ref, (w0, w1, w2, w3), o_ref, slab_ref, held_ref)


def second_kernel(
    place_ref, edge_ref, a_ref, b_ref, c_ref, d_ref, ca_ref, cb_ref, cc_ref, cd_ref,
    stats_ref, w0, w1, w2, w3, o_ref, affine_ref, slab_ref, held_ref,
):
    get_affine(stats_ref, affine_ref)
    refs = (a_ref, b_ref, c_ref, d_ref)
    caches = (ca_ref, cb_ref, cc_ref, cd_ref)
    for k in range(4):
        b = place_ref[2 + k]
        for r in range(10):
            slab_ref[r, b, :, 0:256] = caches[k][r]

    def x_of(k, r, t):
        return refs[k][r, :, 128 * t : 128 * (t + 1)]

    norm_rows(x_of, place_ref, edge_ref, affine_ref, slab_ref)
    convolve(1, place_ref, (w0, w1, w2, w3), o_ref, slab_ref, held_ref)


def merge_kernel(part_ref, bias_ref, gain_ref, shift_ref, mid_ref, stats_ref, note_ref):
    bias = jnp.concatenate([bias_ref[...]] * 4, axis=1)
    for r in range(8):
        summed = part_ref[0, r].astype(F32) + part_ref[1, r].astype(F32)
        summed += part_ref[2, r].astype(F32) + part_ref[3, r].astype(F32)
        mid_ref[r] = (summed + bias).astype(BF16)
    slabs = [mid_ref[:, :, 128 * t : 128 * (t + 1)].astype(F32) for t in range(4)]
    x = jnp.concatenate(slabs, axis=0).reshape(32, 2, GROUP, 128)
    put_stats(x, gain_ref, shift_ref, 1, note_ref, stats_ref)


def last_kernel(x_ref, part_ref, bias_ref, o_ref):
    bias = bias_ref[...]
    for r in range(8):
        for t in range(4):
            lanes = slice(128 * t, 128 * (t + 1))
            branch = part_ref[0, r, :, lanes].astype(F32) + part_ref[1, r, :, lanes].astype(F32)
            branch += part_ref[2, r, :, lanes].astype(F32) + part_ref[3, r, :, lanes].astype(F32)
            o_ref[t, r] = (x_ref[t, r].astype(F32) + (branch + bias)).astype(BF16)


def struct(shape, dtype=BF16):
    return jax.ShapeDtypeStruct(shape, dtype)


def with_rows(x):
    up = [(i, i + 1) for i in range(15)]
    down = [(i + 1, i) for i in range(15)]
    above = lax.ppermute(x[7:8], ROW, up)
    below = lax.ppermute(x[0:1], ROW, down)
    return jnp.concatenate([above, x, below], axis=0)


def near(x):
    return [x] + [lax.ppermute(x, NEAR, [(i, i ^ k) for i in range(4)]) for k in (1, 2, 3)]


def exchange(x, axes):
    return lax.all_to_all(x, axes, 0, 0, tiled=True)


def weights_of(weight):
    me = lax.axis_index("zh")
    weight = weight.reshape(2, 16, 3, 3, 3, 4, 64).transpose(5, 0, 2, 4, 1, 3, 6)
    weight = weight.reshape(4, 2, 3, 3, 16, 192)
    held = [lax.dynamic_index_in_dim(weight, lax.rem(me + d, 4), 0, keepdims=False) for d in range(4)]
    moved = [
        lax.ppermute(held[d], "zh", [(i, (i + d) % 4) for i in range(4)]) for d in range(1, 4)
    ]
    return [held[0]] + moved


def local(frames, cache, norm_gain, norm_shift, conv_weight, conv_bias):
    row = lax.axis_index(ROW)
    here = lax.axis_index(NEAR)
    edge = jnp.stack([row > 0, row < 15]).astype(F32)
    place = jnp.stack([row, lax.axis_index("zh"), here, here ^ 1, here ^ 2, here ^ 3]).astype(jnp.int32)
    note = pltpu.VMEM((8, 128), F32)

    raw, later, stats = call(
        begin_kernel,
        (struct((8, 16, 768)), struct((8, 16, 256)), struct((64, 8, 128), F32)),
        frames, cache, norm_gain, norm_shift,
        scratch=(note,),
    )
    stats = exchange(stats, ROW + NEAR)
    raw = near(with_rows(raw))
    weights = weights_of(conv_weight)
    later = near(with_rows(later))
    bias = jnp.broadcast_to(conv_bias[:, :, None], (2, 16, 128))
    scratch = (
        pltpu.VMEM((3, 4, 16, 128), F32),
        pltpu.VMEM((10, 4, 16, 768), BF16),
        pltpu.VMEM((3, 4, 3, 16, 192), BF16),
    )
    flops = 2 * 192 * 576 * 4096

    partial = call(
        first_kernel, struct((4, 8, 16, 512)), place, edge, *raw, stats, *weights,
        smem=(0, 1), scratch=scratch, flops=flops,
    )
    partial = exchange(partial, "zh")
    middle, stats = call(
        merge_kernel,
        (struct((8, 16, 512)), struct((64, 8, 128), F32)),
        partial, bias[0], norm_gain, norm_shift,
        scratch=(note,),
    )
    stats = exchange(stats, ROW + NEAR)
    middle = near(with_rows(middle))
    partial = call(
        second_kernel, struct((4, 8, 16, 512)), place, edge, *middle, *later, stats, *weights,
        smem=(0, 1), scratch=scratch, flops=flops,
    )
    partial = exchange(partial, "zh")
    return call(last_kernel, struct((4, 8, 16, 128)), frames, partial, bias[1])


def solution(mesh):
    fine = Mesh(mesh.devices.reshape(2, 4, 2, 4, 2, 2), ROW + CHAN)
    placed = (
        P(None, ROW, CHAN, None),
        P(None, None, ROW, CHAN, None),
        P(None, CHAN),
        P(None, CHAN),
        P(None, CHAN, None, None),
        P(None, CHAN),
    )
    return jax.shard_map(
        local, mesh=fine, in_specs=placed, out_specs=P(None, ROW, CHAN, None), check_vma=False
    )
```

```python
import jax
import jax.numpy as jnp
from jax import lax
from jax.experimental import pallas as pl
from jax.experimental.pallas import tpu as pltpu
from jax.sharding import Mesh, PartitionSpec as P

GROUP = 8
EPS = 1e-06
BF16 = jnp.bfloat16
F32 = jnp.float32

ROW = ("xh", "y", "core")
CHAN = ("zh", "zl", "xl")
NEAR = ("zl", "xl")


def dot(a, b):
    return lax.dot_general(a, b, (((1,), (0,)), ((), ())), preferred_element_type=F32)


def silu(u):
    return u / (1.0 + jnp.exp(-u))


def call(kernel, outs, *args, smem=(), scratch=(), flops=0, space=pltpu.VMEM):
    specs = [pl.BlockSpec(memory_space=pltpu.SMEM if i in smem else space) for i in range(len(args))]
    moved = sum(a.size * a.dtype.itemsize for a in args)
    return pl.pallas_call(
        kernel,
        out_shape=outs,
        in_specs=specs,
        out_specs=jax.tree.map(lambda _: pl.BlockSpec(memory_space=pltpu.VMEM), outs),
        scratch_shapes=list(scratch),
        compiler_params=pltpu.CompilerParams(vmem_limit_bytes=(40 if space is pltpu.VMEM else 60) * 1024 * 1024),
        cost_estimate=pl.CostEstimate(flops=flops, bytes_accessed=moved, transcendentals=0),
    )(*args)


def put_stats(x, gain_ref, shift_ref, layer, note_ref, stats_ref):
    number = x.shape[0] * GROUP
    mean = jnp.sum(x, axis=(0, 2), keepdims=True) / number
    off = x - mean
    square = jnp.sum(off * off, axis=(0, 2))
    note_ref[...] = jnp.zeros((8, 128), F32)
    note_ref[0:2] = mean.reshape(2, 128)
    note_ref[2:4] = square
    note_ref[4:5, 0:16] = gain_ref[layer : layer + 1, :]
    note_ref[5:6, 0:16] = shift_ref[layer : layer + 1, :]
    stats_ref[...] = jnp.broadcast_to(note_ref[...][None], stats_ref.shape)


def begin_kernel(
    place_ref, x_hbm, cache_hbm, gain_hbm, shift_hbm, w_hbm,
    raw_ref, later_ref, stats_ref, o_ref, x_ref, cache_ref, gain_ref, shift_ref, w_ref, note_ref, sems,
):
    pairs = (
        (x_hbm, x_ref), (cache_hbm, cache_ref), (gain_hbm, gain_ref), (shift_hbm, shift_ref), (w_hbm, w_ref)
    )
    copies = [pltpu.make_async_copy(src, dst, sems.at[i]) for i, (src, dst) in enumerate(pairs)]
    for copy in copies:
        copy.start()
    for copy in copies:
        copy.wait()
    for r in range(8):
        for t in range(2):
            lanes = slice(128 * t, 128 * (t + 1))
            raw_ref[r, :, lanes] = cache_ref[0, t, r]
            later_ref[r, :, lanes] = cache_ref[1, t, r]
        for t in range(4):
            raw_ref[r, :, 256 + 128 * t : 384 + 128 * t] = x_ref[t, r]
    for q in range(4):
        place = lax.rem(q + 4 - place_ref[1], 4)
        for layer in range(2):
            for dt in range(3):
                for dc in range(3):
                    taps = [
                        w_ref[layer, 9 * dt + 3 * dr + dc, :, 64 * q : 64 * (q + 1)] for dr in range(3)
                    ]
                    o_ref[place, layer, dt, dc] = jnp.concatenate(taps, axis=1)
    x = x_ref[...].astype(F32).reshape(32, 2, GROUP, 128)
    put_stats(x, gain_ref, shift_ref, 0, note_ref, stats_ref)


def shift_columns(left, centre, right):
    lane = lax.broadcasted_iota(jnp.int32, left.shape, left.ndim - 1)
    axis = left.ndim - 1
    left = jnp.where(lane == 0, 0.0, pltpu.roll(left, 1, axis))
    right = jnp.where(lane == 127, 0.0, pltpu.roll(right, 127, axis))
    return left + centre + right


def get_affine(stats_ref, affine_ref):
    stats = stats_ref[...].reshape(16, 4, 8, 128)
    number = 32 * GROUP
    means = stats[:, :, 0:2]
    mean = jnp.mean(means, axis=(0, 3), keepdims=True)
    off = means - mean
    total = jnp.sum(stats[:, :, 2:4] + number * (off * off), axis=(0, 3), keepdims=True)
    inverse = lax.rsqrt(total / (number * 16 * 128) + EPS)
    mean = jnp.broadcast_to(mean.reshape(4, 2, 1, 1), (4, 2, GROUP, 128)).reshape(4, 16, 128)
    inverse = jnp.broadcast_to(inverse.reshape(4, 2, 1, 1), (4, 2, GROUP, 128)).reshape(4, 16, 128)
    shape = (4, 16, 128)
    same = lax.broadcasted_iota(jnp.int32, shape, 1) == lax.broadcasted_iota(jnp.int32, shape, 2)
    gain = jnp.sum(jnp.where(same, stats[0, :, 4:5], 0.0), axis=2, keepdims=True)
    shift = jnp.sum(jnp.where(same, stats[0, :, 5:6], 0.0), axis=2, keepdims=True)
    affine_ref[0] = mean
    affine_ref[1] = inverse * gain
    affine_ref[2] = jnp.broadcast_to(shift, shape)


def convolve(layer, place_ref, w_refs, o_ref, slab_ref, held_ref):
    for q, w_ref in enumerate(w_refs):
        for dt in range(3):
            held_ref[dt, q] = w_ref[layer, dt]
    for r in range(8):
        rows = slab_ref[r : r + 3].reshape(192, 768)
        prod = dot(held_ref[0].reshape(192, 192), rows[:, 0:512])
        prod += dot(held_ref[1].reshape(192, 192), rows[:, 128:640])
        prod += dot(held_ref[2].reshape(192, 192), rows[:, 256:768])
        prod = prod.reshape(4, 3, 16, 512)
        for t in range(4):
            lanes = slice(128 * t, 128 * (t + 1))
            part = prod[:, :, :, lanes]
            summed = shift_columns(part[:, 0], part[:, 1], part[:, 2]).astype(BF16)
            for q in range(4):
                o_ref[lax.rem(place_ref[1] + (4 - q), 4), r, :, lanes] = summed[q]


def norm_rows(x_of, place_ref, edge_ref, affine_ref, slab_ref):
    for k in range(4):
        b = place_ref[2 + k]
        mean = affine_ref[0, b]
        gain = affine_ref[1, b]
        shift = affine_ref[2, b]
        for r in range(10):
            for t in range(4):
                y = silu((x_of(k, r, t).astype(F32) - mean) * gain + shift)
                if r == 0:
                    y = y * edge_ref[0]
                if r == 9:
                    y = y * edge_ref[1]
                slab_ref[r, b, :, 256 + 128 * t : 384 + 128 * t] = y.astype(BF16)


def row_of(refs, above_ref, below_ref, k, r):
    if r == 0:
        return above_ref.at[k]
    return below_ref.at[k] if r == 9 else refs[k].at[r - 1]


def first_kernel(
    place_ref, edge_ref, a_ref, b_ref, c_ref, d_ref, above_ref, below_ref, stats_ref,
    w0, w1, w2, w3, o_ref, affine_ref, slab_ref, held_ref,
):
    get_affine(stats_ref, affine_ref)
    refs = (a_ref, b_ref, c_ref, d_ref)
    for k in range(4):
        b = place_ref[2 + k]
        for r in range(10):
            slab_ref[r, b, :, 0:256] = row_of(refs, above_ref, below_ref, k, r)[:, 0:256]

    def x_of(k, r, t):
        return row_of(refs, above_ref, below_ref, k, r)[:, 256 + 128 * t : 384 + 128 * t]

    norm_rows(x_of, place_ref, edge_ref, affine_ref, slab_ref)
    convolve(0, place_ref, (w0, w1, w2, w3), o_ref, slab_ref, held_ref)


def second_kernel(
    place_ref, edge_ref, a_ref, b_ref, c_ref, d_ref, above_ref, below_ref,
    ca_ref, cb_ref, cc_ref, cd_ref, cabove_ref, cbelow_ref,
    stats_ref, w0, w1, w2, w3, o_ref, affine_ref, slab_ref, held_ref,
):
    get_affine(stats_ref, affine_ref)
    refs = (a_ref, b_ref, c_ref, d_ref)
    caches = (ca_ref, cb_ref, cc_ref, cd_ref)
    for k in range(4):
        b = place_ref[2 + k]
        for r in range(10):
            slab_ref[r, b, :, 0:256] = row_of(caches, cabove_ref, cbelow_ref, k, r)[...]

    def x_of(k, r, t):
        return row_of(refs, above_ref, below_ref, k, r)[:, 128 * t : 128 * (t + 1)]

    norm_rows(x_of, place_ref, edge_ref, affine_ref, slab_ref)
    convolve(1, place_ref, (w0, w1, w2, w3), o_ref, slab_ref, held_ref)


def merge_kernel(part_ref, bias_ref, gain_ref, shift_ref, mid_ref, stats_ref, note_ref):
    bias = jnp.concatenate([bias_ref[...]] * 4, axis=1)
    for r in range(8):
        summed = part_ref[0, r].astype(F32) + part_ref[1, r].astype(F32)
        summed += part_ref[2, r].astype(F32) + part_ref[3, r].astype(F32)
        mid_ref[r] = (summed + bias).astype(BF16)
    slabs = [mid_ref[:, :, 128 * t : 128 * (t + 1)].astype(F32) for t in range(4)]
    x = jnp.concatenate(slabs, axis=0).reshape(32, 2, GROUP, 128)
    put_stats(x, gain_ref, shift_ref, 1, note_ref, stats_ref)


def last_kernel(x_ref, part_ref, bias_ref, o_ref):
    bias = bias_ref[...]
    for r in range(8):
        for t in range(4):
            lanes = slice(128 * t, 128 * (t + 1))
            branch = part_ref[0, r, :, lanes].astype(F32) + part_ref[1, r, :, lanes].astype(F32)
            branch += part_ref[2, r, :, lanes].astype(F32) + part_ref[3, r, :, lanes].astype(F32)
            o_ref[t, r] = (x_ref[t, r].astype(F32) + (branch + bias)).astype(BF16)


def struct(shape, dtype=BF16):
    return jax.ShapeDtypeStruct(shape, dtype)


def rows_beside(blocks):
    up = [(i, i + 1) for i in range(15)]
    down = [(i + 1, i) for i in range(15)]
    above = lax.ppermute(jnp.stack([x[7] for x in blocks]), ROW, up)
    below = lax.ppermute(jnp.stack([x[0] for x in blocks]), ROW, down)
    return [above, below]


def near(x):
    return [x] + [lax.ppermute(x, NEAR, [(i, i ^ k) for i in range(4)]) for k in (1, 2, 3)]


def exchange(x, axes):
    return lax.all_to_all(x, axes, 0, 0, tiled=True)


def local(frames, cache, norm_gain, norm_shift, conv_weight, conv_bias):
    row = lax.axis_index(ROW)
    here = lax.axis_index(NEAR)
    edge = jnp.stack([row > 0, row < 15]).astype(F32)
    place = jnp.stack([row, lax.axis_index("zh"), here, here ^ 1, here ^ 2, here ^ 3]).astype(jnp.int32)
    note = pltpu.VMEM((8, 128), F32)

    raw, later, stats, held = call(
        begin_kernel,
        (
            struct((8, 16, 768)), struct((8, 16, 256)), struct((64, 8, 128), F32),
            struct((4, 2, 3, 3, 16, 192)),
        ),
        place, frames, cache, norm_gain, norm_shift, conv_weight.transpose(0, 2, 1, 3),
        smem=(0,),
        scratch=(
            pltpu.VMEM((4, 8, 16, 128), BF16), pltpu.VMEM((2, 2, 8, 16, 128), BF16),
            pltpu.VMEM((2, 16), F32), pltpu.VMEM((2, 16), F32), pltpu.VMEM((2, 27, 16, 256), BF16),
            note, pltpu.SemaphoreType.DMA((5,)),
        ),
        space=pl.ANY,
    )
    raw = near(raw)
    weights = [held[0]] + [
        lax.ppermute(held[d], "zh", [(i, (i + d) % 4) for i in range(4)]) for d in range(1, 4)
    ]
    stats = exchange(stats, ROW + NEAR)
    raw = raw + rows_beside(raw)
    raw, later = lax.optimization_barrier((raw, later))
    later = near(later)
    later = later + rows_beside(later)
    bias = jnp.broadcast_to(conv_bias[:, :, None], (2, 16, 128))
    scratch = (
        pltpu.VMEM((3, 4, 16, 128), F32),
        pltpu.VMEM((10, 4, 16, 768), BF16),
        pltpu.VMEM((3, 4, 3, 16, 192), BF16),
    )
    flops = 2 * 192 * 576 * 4096

    partial = call(
        first_kernel, struct((4, 8, 16, 512)), place, edge, *raw, stats, *weights,
        smem=(0, 1), scratch=scratch, flops=flops,
    )
    partial = exchange(partial, "zh")
    partial, later = lax.optimization_barrier((partial, later))
    middle, stats = call(
        merge_kernel,
        (struct((8, 16, 512)), struct((64, 8, 128), F32)),
        partial, bias[0], norm_gain, norm_shift,
        scratch=(note,),
    )
    middle = near(middle)
    stats = exchange(stats, ROW + NEAR)
    middle = middle + rows_beside(middle)
    partial = call(
        second_kernel, struct((4, 8, 16, 512)), place, edge, *middle, *later, stats, *weights,
        smem=(0, 1), scratch=scratch, flops=flops,
    )
    partial = exchange(partial, "zh")
    return call(last_kernel, struct((4, 8, 16, 128)), frames, partial, bias[1])


def solution(mesh):
    fine = Mesh(mesh.devices.reshape(2, 4, 2, 4, 2, 2), ROW + CHAN)
    placed = (
        P(None, ROW, CHAN, None),
        P(None, None, ROW, CHAN, None),
        P(None, CHAN),
        P(None, CHAN),
        P(None, CHAN, None, None),
        P(None, CHAN),
    )
    return jax.shard_map(
        local, mesh=fine, in_specs=placed, out_specs=P(None, ROW, CHAN, None), check_vma=False
    )
```

```python
import functools

import jax
import jax.numpy as jnp
from jax import lax
from jax.experimental import pallas as pl
from jax.experimental.pallas import tpu as pltpu
from jax.sharding import Mesh, PartitionSpec as P

GROUP = 8
EPS = 1e-06
BF16 = jnp.bfloat16
F32 = jnp.float32

ROW = ("xh", "y", "core")
CHAN = ("zh", "zl", "xl")
NEAR = ("zl", "xl")


def dot(a, b):
    return lax.dot_general(a, b, (((1,), (0,)), ((), ())), preferred_element_type=F32)


def silu(u):
    return u / (1.0 + jnp.exp(-u))


def call(kernel, outs, *args, far=(), scratch=(), flops=0):
    specs = [pl.BlockSpec(memory_space=pl.ANY if i in far else pltpu.VMEM) for i in range(len(args))]
    moved = sum(a.size * a.dtype.itemsize for a in args)
    return pl.pallas_call(
        kernel,
        out_shape=outs,
        in_specs=specs,
        out_specs=jax.tree.map(lambda _: pl.BlockSpec(memory_space=pltpu.VMEM), outs),
        scratch_shapes=list(scratch),
        compiler_params=pltpu.CompilerParams(vmem_limit_bytes=(60 if far else 40) * 1024 * 1024),
        cost_estimate=pl.CostEstimate(flops=flops, bytes_accessed=moved, transcendentals=0),
    )(*args)


def place():
    return lax.axis_index(ROW), lax.axis_index("zh"), lax.axis_index(NEAR)


def put_stats(rows_ref, note_ref, stats_ref):
    slabs = [rows_ref[:, :, 256 + 128 * t : 384 + 128 * t].astype(F32) for t in range(4)]
    x = jnp.concatenate(slabs, axis=0).reshape(32, 2, GROUP, 128)
    number = x.shape[0] * GROUP
    mean = jnp.sum(x, axis=(0, 2), keepdims=True) / number
    off = x - mean
    square = jnp.sum(off * off, axis=(0, 2))
    note_ref[0:2] = mean.reshape(2, 128)
    note_ref[2:4] = square
    stats_ref[...] = jnp.broadcast_to(note_ref[...][None], stats_ref.shape)


def fetch(pairs, sems):
    copies = [pltpu.make_async_copy(src, dst, sems.at[i]) for i, (src, dst) in enumerate(pairs)]
    for copy in copies:
        copy.start()
    for copy in copies:
        copy.wait()


def rows_kernel(x_hbm, cache_hbm, raw_ref, later_ref, x_ref, cache_ref, sems):
    fetch(((x_hbm, x_ref), (cache_hbm, cache_ref)), sems)
    for r in range(8):
        for t in range(2):
            lanes = slice(128 * t, 128 * (t + 1))
            raw_ref[r, :, lanes] = cache_ref[0, t, r]
            later_ref[r, :, lanes] = cache_ref[1, t, r]
        for t in range(4):
            raw_ref[r, :, 256 + 128 * t : 384 + 128 * t] = x_ref[t, r]


def stats_kernel(
    raw_ref, gain_hbm, shift_hbm, w_hbm, stats_ref, next_ref, w0_ref, w1_ref,
    gain_ref, shift_ref, w_ref, note_ref, sems,
):
    fetch(((gain_hbm, gain_ref), (shift_hbm, shift_ref), (w_hbm, w_ref)), sems)
    _, me, _ = place()
    for q in range(4):
        for dt in range(3):
            for dc in range(3):
                taps = [
                    [
                        w_ref[layer, 9 * dt + 3 * dr + dc, :, 64 * q : 64 * (q + 1)]
                        for dr in range(3)
                    ]
                    for layer in range(2)
                ]
                w0_ref[q, dt, dc] = jnp.concatenate(taps[0], axis=1)
                w1_ref[lax.rem(q + 4 - me, 4), dt, dc] = jnp.concatenate(taps[1], axis=1)
    for layer, ref in ((0, note_ref), (1, next_ref)):
        ref[...] = jnp.zeros((8, 128), F32)
        ref[4:5, 0:16] = gain_ref[layer : layer + 1, :]
        ref[5:6, 0:16] = shift_ref[layer : layer + 1, :]
    put_stats(raw_ref, note_ref, stats_ref)


def second_stats_kernel(mid_ref, next_ref, stats_ref, note_ref):
    note_ref[...] = next_ref[...]
    put_stats(mid_ref, note_ref, stats_ref)


def shift_columns(left, centre, right):
    lane = lax.broadcasted_iota(jnp.int32, left.shape, left.ndim - 1)
    axis = left.ndim - 1
    left = jnp.where(lane == 0, 0.0, pltpu.roll(left, 1, axis))
    right = jnp.where(lane == 127, 0.0, pltpu.roll(right, 127, axis))
    return left + centre + right


def get_affine(stats_ref, affine_ref):
    stats = stats_ref[...].reshape(16, 4, 8, 128)
    number = 32 * GROUP
    means = stats[:, :, 0:2]
    mean = jnp.mean(means, axis=(0, 3), keepdims=True)
    off = means - mean
    total = jnp.sum(stats[:, :, 2:4] + number * (off * off), axis=(0, 3), keepdims=True)
    inverse = lax.rsqrt(total / (number * 16 * 128) + EPS)
    mean = jnp.broadcast_to(mean.reshape(4, 2, 1, 1), (4, 2, GROUP, 128)).reshape(4, 16, 128)
    inverse = jnp.broadcast_to(inverse.reshape(4, 2, 1, 1), (4, 2, GROUP, 128)).reshape(4, 16, 128)
    shape = (4, 16, 128)
    same = lax.broadcasted_iota(jnp.int32, shape, 1) == lax.broadcasted_iota(jnp.int32, shape, 2)
    gain = jnp.sum(jnp.where(same, stats[0, :, 4:5], 0.0), axis=2, keepdims=True)
    shift = jnp.sum(jnp.where(same, stats[0, :, 5:6], 0.0), axis=2, keepdims=True)
    affine_ref[0] = mean
    affine_ref[1] = inverse * gain
    affine_ref[2] = jnp.broadcast_to(shift, shape)


def conv_kernel(
    first, a_ref, b_ref, c_ref, d_ref, chip_ref, next_ref, stats_ref, *refs
):
    *w_refs, o_ref, affine_ref, slab_ref, held_ref = refs
    row, me, here = place()
    get_affine(stats_ref, affine_ref)
    upper = lax.rem(row, 2) == 0
    not_top = (row > 0).astype(F32)
    not_bottom = (row < 15).astype(F32)
    for k, ref in enumerate((a_ref, b_ref, c_ref, d_ref)):
        b = lax.bitwise_xor(here, k)
        mean = affine_ref[0, b]
        gain = affine_ref[1, b]
        shift = affine_ref[2, b]
        for r in range(10):
            for t in range(6):
                lanes = slice(128 * t, 128 * (t + 1))
                if r == 0:
                    x = jnp.where(upper, next_ref[k, :, lanes].astype(F32), chip_ref[k, :, lanes].astype(F32))
                elif r == 9:
                    x = jnp.where(upper, chip_ref[k, :, lanes].astype(F32), next_ref[k, :, lanes].astype(F32))
                elif t < 2:
                    x = ref[r - 1, :, lanes]
                else:
                    x = ref[r - 1, :, lanes].astype(F32)
                if t >= 2:
                    x = silu((x - mean) * gain + shift)
                if r == 0:
                    x = x * not_top
                if r == 9:
                    x = x * not_bottom
                slab_ref[r, b, :, lanes] = x.astype(BF16)
    for q in range(4):
        for dt in range(3):
            held_ref[dt, q] = w_refs[0][q, dt] if first else w_refs[q][dt]
    for r in range(8):
        rows = slab_ref[r : r + 3].reshape(192, 768)
        prod = dot(held_ref[0].reshape(192, 192), rows[:, 0:512])
        prod += dot(held_ref[1].reshape(192, 192), rows[:, 128:640])
        prod += dot(held_ref[2].reshape(192, 192), rows[:, 256:768])
        prod = prod.reshape(4, 3, 16, 512)
        for t in range(4):
            lanes = slice(128 * t, 128 * (t + 1))
            part = prod[:, :, :, lanes]
            summed = shift_columns(part[:, 0], part[:, 1], part[:, 2]).astype(BF16)
            for q in range(4):
                target = q if first else lax.rem(me + (4 - q), 4)
                o_ref[target, r, :, lanes] = summed[q]


def merge_kernel(part_ref, bias_ref, later_ref, mid_ref):
    bias = jnp.concatenate([bias_ref[...]] * 4, axis=1)
    for r in range(8):
        summed = part_ref[0, r].astype(F32) + part_ref[1, r].astype(F32)
        summed += part_ref[2, r].astype(F32) + part_ref[3, r].astype(F32)
        mid_ref[r, :, 0:256] = later_ref[r]
        mid_ref[r, :, 256:768] = (summed + bias).astype(BF16)


def last_kernel(x_ref, part_ref, bias_ref, o_ref):
    bias = bias_ref[...]
    for r in range(8):
        for t in range(4):
            lanes = slice(128 * t, 128 * (t + 1))
            branch = part_ref[0, r, :, lanes].astype(F32) + part_ref[1, r, :, lanes].astype(F32)
            branch += part_ref[2, r, :, lanes].astype(F32) + part_ref[3, r, :, lanes].astype(F32)
            o_ref[t, r] = (x_ref[t, r].astype(F32) + (branch + bias)).astype(BF16)


def struct(shape, dtype=BF16):
    return jax.ShapeDtypeStruct(shape, dtype)


def edge_kernel(a_ref, b_ref, c_ref, d_ref, chip_ref, next_ref):
    upper = lax.rem(lax.axis_index(ROW), 2) == 0
    towards = jnp.where(upper, 7, 0)
    for k, ref in enumerate((a_ref, b_ref, c_ref, d_ref)):
        chip_ref[k] = ref[towards]
        next_ref[k] = ref[7 - towards]


def rows_beside(blocks):
    chip, beyond = call(edge_kernel, (struct((4, 16, 768)), struct((4, 16, 768))), *blocks, flops=2 * 10**10)
    chip = lax.ppermute(chip, ROW, [(i, i ^ 1) for i in range(16)])
    pairs = [(i, i + 1) for i in range(1, 15, 2)] + [(i + 1, i) for i in range(1, 15, 2)]
    beyond = lax.ppermute(beyond, ROW, pairs)
    return [chip, beyond]


def near(x):
    return [x] + [lax.ppermute(x, NEAR, [(i, i ^ k) for i in range(4)]) for k in (1, 2, 3)]


def exchange(x, axes):
    return lax.all_to_all(x, axes, 0, 0, tiled=True)


def local(frames, cache, norm_gain, norm_shift, conv_weight, conv_bias):
    note = pltpu.VMEM((8, 128), F32)
    raw, later = call(
        rows_kernel, (struct((8, 16, 768)), struct((8, 16, 256))), frames, cache,
        scratch=(
            pltpu.VMEM((4, 8, 16, 128), BF16), pltpu.VMEM((2, 2, 8, 16, 128), BF16),
            pltpu.SemaphoreType.DMA((2,)),
        ),
        far=(0, 1),
    )
    stats, note1, w0, w1 = call(
        stats_kernel,
        (
            struct((64, 8, 128), F32), struct((8, 128), F32),
            struct((4, 3, 3, 16, 192)), struct((4, 3, 3, 16, 192)),
        ),
        raw, norm_gain, norm_shift, conv_weight.transpose(0, 2, 1, 3),
        scratch=(
            pltpu.VMEM((2, 16), F32), pltpu.VMEM((2, 16), F32), pltpu.VMEM((2, 27, 16, 256), BF16),
            note, pltpu.SemaphoreType.DMA((3,)),
        ),
        far=(1, 2, 3),
    )
    raw = near(raw)
    w0 = exchange(w0, "zh")
    stats, w0 = lax.optimization_barrier((stats, w0))
    stats = exchange(stats, ROW + NEAR)
    raw = raw + rows_beside(raw)
    bias = jnp.broadcast_to(conv_bias[:, :, None], (2, 16, 128))
    scratch = (
        pltpu.VMEM((3, 4, 16, 128), F32),
        pltpu.VMEM((10, 4, 16, 768), BF16),
        pltpu.VMEM((3, 4, 3, 16, 192), BF16),
    )
    flops = 2 * 192 * 576 * 4096

    partial = call(
        functools.partial(conv_kernel, True), struct((4, 8, 16, 512)), *raw, stats, w0,
        scratch=scratch, flops=flops,
    )
    partial, w1 = lax.optimization_barrier((partial, w1))
    w1 = [w1[0]] + [
        lax.ppermute(w1[d], "zh", [(i, (i + d) % 4) for i in range(4)]) for d in range(1, 4)
    ]
    partial = exchange(partial, "zh")
    partial, w1 = lax.optimization_barrier((partial, w1))
    middle = call(merge_kernel, struct((8, 16, 768)), partial, bias[0], later)
    stats = call(second_stats_kernel, struct((64, 8, 128), F32), middle, note1, scratch=(note,))
    middle = near(middle)
    stats = exchange(stats, ROW + NEAR)
    middle = middle + rows_beside(middle)
    partial = call(
        functools.partial(conv_kernel, False), struct((4, 8, 16, 512)), *middle, stats, *w1,
        scratch=scratch, flops=flops,
    )
    partial = exchange(partial, "zh")
    return call(last_kernel, struct((4, 8, 16, 128)), frames, partial, bias[1])


def solution(mesh):
    fine = Mesh(mesh.devices.reshape(2, 4, 2, 4, 2, 2), ROW + CHAN)
    placed = (
        P(None, ROW, CHAN, None),
        P(None, None, ROW, CHAN, None),
        P(None, CHAN),
        P(None, CHAN),
        P(None, CHAN, None, None),
        P(None, CHAN),
    )
    return jax.shard_map(
        local, mesh=fine, in_specs=placed, out_specs=P(None, ROW, CHAN, None), check_vma=False
    )
```

```python
import functools

import jax
import jax.numpy as jnp
from jax import lax
from jax.experimental import pallas as pl
from jax.experimental.pallas import tpu as pltpu
from jax.sharding import Mesh, PartitionSpec as P

GROUP = 8
EPS = 1e-06
BF16 = jnp.bfloat16
F32 = jnp.float32

ROW = ("xh", "y", "core")
CHAN = ("zh", "zl", "xl")
NEAR = ("zl", "xl")


def dot(a, b):
    return lax.dot_general(a, b, (((1,), (0,)), ((), ())), preferred_element_type=F32)


def silu(u):
    return u / (1.0 + jnp.exp(-u))


def call(kernel, outs, *args, far=(), scratch=(), flops=0):
    specs = [pl.BlockSpec(memory_space=pl.ANY if i in far else pltpu.VMEM) for i in range(len(args))]
    moved = sum(a.size * a.dtype.itemsize for a in args)
    return pl.pallas_call(
        kernel,
        out_shape=outs,
        in_specs=specs,
        out_specs=jax.tree.map(lambda _: pl.BlockSpec(memory_space=pltpu.VMEM), outs),
        scratch_shapes=list(scratch),
        compiler_params=pltpu.CompilerParams(vmem_limit_bytes=(60 if far else 40) * 1024 * 1024),
        cost_estimate=pl.CostEstimate(flops=flops, bytes_accessed=moved, transcendentals=0),
    )(*args)


def place():
    return lax.axis_index(ROW), lax.axis_index("zh"), lax.axis_index(NEAR)


def put_stats(rows_ref, note_ref, stats_ref):
    slabs = [rows_ref[:, :, 256 + 128 * t : 384 + 128 * t].astype(F32) for t in range(4)]
    x = jnp.concatenate(slabs, axis=0).reshape(32, 2, GROUP, 128)
    number = x.shape[0] * GROUP
    mean = jnp.sum(x, axis=(0, 2), keepdims=True) / number
    off = x - mean
    square = jnp.sum(off * off, axis=(0, 2))
    note_ref[0:2] = mean.reshape(2, 128)
    note_ref[2:4] = square
    stats_ref[...] = jnp.broadcast_to(note_ref[...][None], stats_ref.shape)


def fetch(pairs, sems):
    copies = [pltpu.make_async_copy(src, dst, sems.at[i]) for i, (src, dst) in enumerate(pairs)]
    for copy in copies:
        copy.start()
    for copy in copies:
        copy.wait()


def begin_kernel(
    x_hbm, cache_hbm, gain_hbm, shift_hbm, w_hbm,
    raw_ref, later_ref, stats_ref, note1_ref, own_ref, side_ref, far_ref,
    x_ref, cache_ref, gain_ref, shift_ref, w_ref, note_ref, pieces_ref, sems,
):
    fetch(
        (
            (x_hbm, x_ref), (cache_hbm, cache_ref), (gain_hbm, gain_ref), (shift_hbm, shift_ref),
            (w_hbm, w_ref),
        ),
        sems,
    )
    for r in range(8):
        for t in range(2):
            lanes = slice(128 * t, 128 * (t + 1))
            raw_ref[r, :, lanes] = cache_ref[0, t, r]
            later_ref[r, :, lanes] = cache_ref[1, t, r]
        for t in range(4):
            raw_ref[r, :, 256 + 128 * t : 384 + 128 * t] = x_ref[t, r]
    row, me, _ = place()
    core = lax.rem(row, 2)
    for q in range(4):
        ahead = lax.rem(q + 4 - me, 4)
        for layer in range(2):
            for dt in range(3):
                for dc in range(3):
                    taps = [
                        w_ref[layer, 9 * dt + 3 * dr + dc, :, 64 * q : 64 * (q + 1)] for dr in range(3)
                    ]
                    pieces_ref[ahead, layer, dt, dc] = jnp.concatenate(taps, axis=1)
    own_ref[...] = pieces_ref[0]
    side_ref[...] = pieces_ref[1 + 2 * core]
    far_ref[...] = pieces_ref[2, core]
    for layer, ref in ((0, note_ref), (1, note1_ref)):
        ref[...] = jnp.zeros((8, 128), F32)
        ref[4:5, 0:16] = gain_ref[layer : layer + 1, :]
        ref[5:6, 0:16] = shift_ref[layer : layer + 1, :]
    put_stats(raw_ref, note_ref, stats_ref)


def shift_columns(left, centre, right):
    lane = lax.broadcasted_iota(jnp.int32, left.shape, left.ndim - 1)
    axis = left.ndim - 1
    left = jnp.where(lane == 0, 0.0, pltpu.roll(left, 1, axis))
    right = jnp.where(lane == 127, 0.0, pltpu.roll(right, 127, axis))
    return left + centre + right


def get_affine(stats_ref, affine_ref):
    stats = stats_ref[...].reshape(16, 4, 8, 128)
    number = 32 * GROUP
    means = stats[:, :, 0:2]
    mean = jnp.mean(means, axis=(0, 3), keepdims=True)
    off = means - mean
    total = jnp.sum(stats[:, :, 2:4] + number * (off * off), axis=(0, 3), keepdims=True)
    inverse = lax.rsqrt(total / (number * 16 * 128) + EPS)
    mean = jnp.broadcast_to(mean.reshape(4, 2, 1, 1), (4, 2, GROUP, 128)).reshape(4, 16, 128)
    inverse = jnp.broadcast_to(inverse.reshape(4, 2, 1, 1), (4, 2, GROUP, 128)).reshape(4, 16, 128)
    shape = (4, 16, 128)
    same = lax.broadcasted_iota(jnp.int32, shape, 1) == lax.broadcasted_iota(jnp.int32, shape, 2)
    gain = jnp.sum(jnp.where(same, stats[0, :, 4:5], 0.0), axis=2, keepdims=True)
    shift = jnp.sum(jnp.where(same, stats[0, :, 5:6], 0.0), axis=2, keepdims=True)
    affine_ref[0] = mean
    affine_ref[1] = inverse * gain
    affine_ref[2] = jnp.broadcast_to(shift, shape)


def conv_kernel(
    layer, a_ref, b_ref, c_ref, d_ref, chip_ref, next_ref, stats_ref,
    own_ref, side_ref, far_ref, side2_ref, far2_ref, o_ref, affine_ref, slab_ref, held_ref,
):
    row, me, here = place()
    get_affine(stats_ref, affine_ref)
    upper = lax.rem(row, 2) == 0
    not_top = (row > 0).astype(F32)
    not_bottom = (row < 15).astype(F32)
    for k, ref in enumerate((a_ref, b_ref, c_ref, d_ref)):
        b = lax.bitwise_xor(here, k)
        mean = affine_ref[0, b]
        gain = affine_ref[1, b]
        shift = affine_ref[2, b]
        for r in range(10):
            for t in range(6):
                lanes = slice(128 * t, 128 * (t + 1))
                if r == 0:
                    x = jnp.where(upper, next_ref[k, :, lanes].astype(F32), chip_ref[k, :, lanes].astype(F32))
                elif r == 9:
                    x = jnp.where(upper, chip_ref[k, :, lanes].astype(F32), next_ref[k, :, lanes].astype(F32))
                elif t < 2:
                    x = ref[r - 1, :, lanes]
                else:
                    x = ref[r - 1, :, lanes].astype(F32)
                if t >= 2:
                    x = silu((x - mean) * gain + shift)
                if r == 0:
                    x = x * not_top
                if r == 9:
                    x = x * not_bottom
                slab_ref[r, b, :, lanes] = x.astype(BF16)
    core = lax.rem(row, 2)
    sources = (me, lax.rem(me + 3 - 2 * core, 4), lax.rem(me + 1 + 2 * core, 4), lax.rem(me + 2, 4))
    for dt in range(3):
        held_ref[dt, 0] = own_ref[layer, dt]
        held_ref[dt, 1] = side_ref[layer, dt]
        held_ref[dt, 2] = side2_ref[layer, dt]

    @pl.when(core == layer)
    def _():
        for dt in range(3):
            held_ref[dt, 3] = far_ref[dt]

    @pl.when(core != layer)
    def _():
        for dt in range(3):
            held_ref[dt, 3] = far2_ref[dt]

    for r in range(8):
        rows = slab_ref[r : r + 3].reshape(192, 768)
        prod = dot(held_ref[0].reshape(192, 192), rows[:, 0:512])
        prod += dot(held_ref[1].reshape(192, 192), rows[:, 128:640])
        prod += dot(held_ref[2].reshape(192, 192), rows[:, 256:768])
        prod = prod.reshape(4, 3, 16, 512)
        for t in range(4):
            lanes = slice(128 * t, 128 * (t + 1))
            part = prod[:, :, :, lanes]
            summed = shift_columns(part[:, 0], part[:, 1], part[:, 2]).astype(BF16)
            for q in range(4):
                o_ref[sources[q], r, :, lanes] = summed[q]


def merge_kernel(part_ref, bias_ref, later_ref, note1_ref, mid_ref, stats_ref, note_ref):
    bias = jnp.concatenate([bias_ref[...]] * 4, axis=1)
    for r in range(8):
        summed = part_ref[0, r].astype(F32) + part_ref[1, r].astype(F32)
        summed += part_ref[2, r].astype(F32) + part_ref[3, r].astype(F32)
        mid_ref[r, :, 0:256] = later_ref[r]
        mid_ref[r, :, 256:768] = (summed + bias).astype(BF16)
    note_ref[...] = note1_ref[...]
    put_stats(mid_ref, note_ref, stats_ref)


def last_kernel(x_ref, part_ref, bias_ref, o_ref):
    bias = bias_ref[...]
    for r in range(8):
        for t in range(4):
            lanes = slice(128 * t, 128 * (t + 1))
            branch = part_ref[0, r, :, lanes].astype(F32) + part_ref[1, r, :, lanes].astype(F32)
            branch += part_ref[2, r, :, lanes].astype(F32) + part_ref[3, r, :, lanes].astype(F32)
            o_ref[t, r] = (x_ref[t, r].astype(F32) + (branch + bias)).astype(BF16)


def struct(shape, dtype=BF16):
    return jax.ShapeDtypeStruct(shape, dtype)


def edge_kernel(a_ref, b_ref, c_ref, d_ref, chip_ref, next_ref):
    upper = lax.rem(lax.axis_index(ROW), 2) == 0
    towards = jnp.where(upper, 7, 0)
    for k, ref in enumerate((a_ref, b_ref, c_ref, d_ref)):
        chip_ref[k] = ref[towards]
        next_ref[k] = ref[7 - towards]


def rows_beside(blocks):
    chip, beyond = call(edge_kernel, (struct((4, 16, 768)), struct((4, 16, 768))), *blocks, flops=2 * 10**10)
    chip = lax.ppermute(chip, ROW, [(i, i ^ 1) for i in range(16)])
    pairs = [(i, i + 1) for i in range(1, 15, 2)] + [(i + 1, i) for i in range(1, 15, 2)]
    beyond = lax.ppermute(beyond, ROW, pairs)
    return [chip, beyond]


def near(x):
    return [x] + [lax.ppermute(x, NEAR, [(i, i ^ k) for i in range(4)]) for k in (1, 2, 3)]


def exchange(x, axes):
    return lax.all_to_all(x, axes, 0, 0, tiled=True)


def local(frames, cache, norm_gain, norm_shift, conv_weight, conv_bias):
    note = pltpu.VMEM((8, 128), F32)
    piece = (2, 3, 3, 16, 192)
    raw, later, stats, note1, own, side, far = call(
        begin_kernel,
        (
            struct((8, 16, 768)), struct((8, 16, 256)), struct((64, 8, 128), F32), struct((8, 128), F32),
            struct(piece), struct(piece), struct(piece[1:]),
        ),
        frames, cache, norm_gain, norm_shift, conv_weight.transpose(0, 2, 1, 3),
        scratch=(
            pltpu.VMEM((4, 8, 16, 128), BF16), pltpu.VMEM((2, 2, 8, 16, 128), BF16),
            pltpu.VMEM((2, 16), F32), pltpu.VMEM((2, 16), F32), pltpu.VMEM((2, 27, 16, 256), BF16),
            note, pltpu.VMEM((4,) + piece, BF16), pltpu.SemaphoreType.DMA((5,)),
        ),
        far=(0, 1, 2, 3, 4),
    )
    around = [(i, (i + 1) % 4) for i in range(4)] + [(4 + i, 4 + (i + 3) % 4) for i in range(4)]
    side = lax.ppermute(side, ("core", "zh"), around)
    far = lax.ppermute(far, "zh", [(i, (i + 2) % 4) for i in range(4)])
    raw = near(raw)
    stats = exchange(stats, ROW + NEAR)
    raw = raw + rows_beside(raw)
    swap = [(0, 1), (1, 0)]
    weights = [own, side, far, lax.ppermute(side, "core", swap), lax.ppermute(far, "core", swap)]
    bias = jnp.broadcast_to(conv_bias[:, :, None], (2, 16, 128))
    scratch = (
        pltpu.VMEM((3, 4, 16, 128), F32),
        pltpu.VMEM((10, 4, 16, 768), BF16),
        pltpu.VMEM((3, 4, 3, 16, 192), BF16),
    )
    flops = 2 * 192 * 576 * 4096

    partial = call(
        functools.partial(conv_kernel, 0), struct((4, 8, 16, 512)), *raw, stats, *weights,
        scratch=scratch, flops=flops,
    )
    partial = exchange(partial, "zh")
    middle, stats = call(
        merge_kernel, (struct((8, 16, 768)), struct((64, 8, 128), F32)), partial, bias[0], later, note1,
        scratch=(note,),
    )
    middle = near(middle)
    stats = exchange(stats, ROW + NEAR)
    middle = middle + rows_beside(middle)
    partial = call(
        functools.partial(conv_kernel, 1), struct((4, 8, 16, 512)), *middle, stats, *weights,
        scratch=scratch, flops=flops,
    )
    partial = exchange(partial, "zh")
    return call(last_kernel, struct((4, 8, 16, 128)), frames, partial, bias[1])


def solution(mesh):
    fine = Mesh(mesh.devices.reshape(2, 4, 2, 4, 2, 2), ROW + CHAN)
    placed = (
        P(None, ROW, CHAN, None),
        P(None, None, ROW, CHAN, None),
        P(None, CHAN),
        P(None, CHAN),
        P(None, CHAN, None, None),
        P(None, CHAN),
    )
    return jax.shard_map(
        local, mesh=fine, in_specs=placed, out_specs=P(None, ROW, CHAN, None), check_vma=False
    )
```

```python
import functools

import jax
import jax.numpy as jnp
from jax import lax
from jax.experimental import pallas as pl
from jax.experimental.pallas import tpu as pltpu
from jax.sharding import Mesh, PartitionSpec as P

GROUP = 8
EPS = 1e-06
BF16 = jnp.bfloat16
F32 = jnp.float32

ROW = ("xh", "y", "core")
CHAN = ("zh", "zl", "xl")
NEAR = ("zl", "xl")


def dot(a, b):
    return lax.dot_general(a, b, (((1,), (0,)), ((), ())), preferred_element_type=F32)


def silu(u):
    return u / (1.0 + jnp.exp(-u))


def call(kernel, outs, *args, far=(), scratch=(), flops=0):
    specs = [pl.BlockSpec(memory_space=pl.ANY if i in far else pltpu.VMEM) for i in range(len(args))]
    moved = sum(a.size * a.dtype.itemsize for a in args)
    return pl.pallas_call(
        kernel,
        out_shape=outs,
        in_specs=specs,
        out_specs=jax.tree.map(lambda _: pl.BlockSpec(memory_space=pltpu.VMEM), outs),
        scratch_shapes=list(scratch),
        compiler_params=pltpu.CompilerParams(vmem_limit_bytes=(60 if far else 40) * 1024 * 1024),
        cost_estimate=pl.CostEstimate(flops=flops, bytes_accessed=moved, transcendentals=0),
    )(*args)


def place():
    return lax.axis_index(ROW), lax.axis_index("zh"), lax.axis_index(NEAR)


def put_stats(rows_ref, note_ref, stats_ref):
    slabs = [rows_ref[:, :, 256 + 128 * t : 384 + 128 * t].astype(F32) for t in range(4)]
    x = jnp.concatenate(slabs, axis=0).reshape(32, 2, GROUP, 128)
    number = x.shape[0] * GROUP
    mean = jnp.sum(x, axis=(0, 2), keepdims=True) / number
    off = x - mean
    square = jnp.sum(off * off, axis=(0, 2))
    note_ref[0:2] = mean.reshape(2, 128)
    note_ref[2:4] = square
    stats_ref[...] = jnp.broadcast_to(note_ref[...][None], stats_ref.shape)


def fetch(pairs, sems):
    copies = [pltpu.make_async_copy(src, dst, sems.at[i]) for i, (src, dst) in enumerate(pairs)]
    for copy in copies:
        copy.start()
    for copy in copies:
        copy.wait()


def begin_kernel(
    x_hbm, cache_hbm, gain_hbm, shift_hbm, w_hbm,
    raw_ref, later_ref, stats_ref, own_ref, side_ref, far_ref,
    x_ref, cache_ref, gain_ref, shift_ref, w_ref, note_ref, pieces_ref, sems,
):
    fetch(
        (
            (x_hbm, x_ref), (cache_hbm, cache_ref), (gain_hbm, gain_ref), (shift_hbm, shift_ref),
            (w_hbm, w_ref),
        ),
        sems,
    )
    for r in range(8):
        for t in range(2):
            lanes = slice(128 * t, 128 * (t + 1))
            raw_ref[r, :, lanes] = cache_ref[0, t, r]
            later_ref[r, :, lanes] = cache_ref[1, t, r]
        for t in range(4):
            raw_ref[r, :, 256 + 128 * t : 384 + 128 * t] = x_ref[t, r]
    row, me, _ = place()
    core = lax.rem(row, 2)
    for q in range(4):
        ahead = lax.rem(q + 4 - me, 4)
        for layer in range(2):
            for dt in range(3):
                for dc in range(3):
                    taps = [
                        w_ref[layer, 9 * dt + 3 * dr + dc, :, 64 * q : 64 * (q + 1)] for dr in range(3)
                    ]
                    pieces_ref[ahead, layer, dt, dc] = jnp.concatenate(taps, axis=1)
    own_ref[...] = pieces_ref[0]
    side_ref[...] = pieces_ref[1 + 2 * core]
    far_ref[...] = pieces_ref[2, core]
    note_ref[...] = jnp.zeros((8, 128), F32)
    note_ref[4:5, 0:16] = gain_ref[0:1, :]
    note_ref[5:6, 0:16] = shift_ref[0:1, :]
    put_stats(raw_ref, note_ref, stats_ref)


def shift_columns(left, centre, right):
    lane = lax.broadcasted_iota(jnp.int32, left.shape, left.ndim - 1)
    axis = left.ndim - 1
    left = jnp.where(lane == 0, 0.0, pltpu.roll(left, 1, axis))
    right = jnp.where(lane == 127, 0.0, pltpu.roll(right, 127, axis))
    return left + centre + right


def get_affine(stats_ref, affine_ref):
    stats = stats_ref[...].reshape(16, 4, 8, 128)
    number = 32 * GROUP
    means = stats[:, :, 0:2]
    mean = jnp.mean(means, axis=(0, 3), keepdims=True)
    off = means - mean
    total = jnp.sum(stats[:, :, 2:4] + number * (off * off), axis=(0, 3), keepdims=True)
    inverse = lax.rsqrt(total / (number * 16 * 128) + EPS)
    mean = jnp.broadcast_to(mean.reshape(4, 2, 1, 1), (4, 2, GROUP, 128)).reshape(4, 16, 128)
    inverse = jnp.broadcast_to(inverse.reshape(4, 2, 1, 1), (4, 2, GROUP, 128)).reshape(4, 16, 128)
    shape = (4, 16, 128)
    same = lax.broadcasted_iota(jnp.int32, shape, 1) == lax.broadcasted_iota(jnp.int32, shape, 2)
    gain = jnp.sum(jnp.where(same, stats[0, :, 4:5], 0.0), axis=2, keepdims=True)
    shift = jnp.sum(jnp.where(same, stats[0, :, 5:6], 0.0), axis=2, keepdims=True)
    affine_ref[0] = mean
    affine_ref[1] = inverse * gain
    affine_ref[2] = jnp.broadcast_to(shift, shape)


def conv_kernel(
    layer, a_ref, b_ref, c_ref, d_ref, chip_ref, next_ref, stats_ref,
    own_ref, side_ref, far_ref, side2_ref, far2_ref, o0_ref, o1_ref, o2_ref, o3_ref,
    affine_ref, slab_ref, held_ref,
):
    row, _, here = place()
    get_affine(stats_ref, affine_ref)
    upper = lax.rem(row, 2) == 0
    not_top = (row > 0).astype(F32)
    not_bottom = (row < 15).astype(F32)
    for k, ref in enumerate((a_ref, b_ref, c_ref, d_ref)):
        b = lax.bitwise_xor(here, k)
        mean = affine_ref[0, b]
        gain = affine_ref[1, b]
        shift = affine_ref[2, b]
        for r in range(10):
            for t in range(6):
                lanes = slice(128 * t, 128 * (t + 1))
                if r == 0:
                    x = jnp.where(upper, next_ref[k, :, lanes].astype(F32), chip_ref[k, :, lanes].astype(F32))
                elif r == 9:
                    x = jnp.where(upper, chip_ref[k, :, lanes].astype(F32), next_ref[k, :, lanes].astype(F32))
                elif t < 2:
                    x = ref[r - 1, :, lanes]
                else:
                    x = ref[r - 1, :, lanes].astype(F32)
                if t >= 2:
                    x = silu((x - mean) * gain + shift)
                if r == 0:
                    x = x * not_top
                if r == 9:
                    x = x * not_bottom
                slab_ref[r, b, :, lanes] = x.astype(BF16)
    core = lax.rem(row, 2)
    for dt in range(3):
        held_ref[dt, 0] = own_ref[layer, dt]
        held_ref[dt, 1] = side_ref[layer, dt]
        held_ref[dt, 2] = side2_ref[layer, dt]

    @pl.when(core == layer)
    def _():
        for dt in range(3):
            held_ref[dt, 3] = far_ref[dt]

    @pl.when(core != layer)
    def _():
        for dt in range(3):
            held_ref[dt, 3] = far2_ref[dt]

    for r in range(8):
        rows = slab_ref[r : r + 3].reshape(192, 768)
        prod = dot(held_ref[0].reshape(192, 192), rows[:, 0:512])
        prod += dot(held_ref[1].reshape(192, 192), rows[:, 128:640])
        prod += dot(held_ref[2].reshape(192, 192), rows[:, 256:768])
        prod = prod.reshape(4, 3, 16, 512)
        for t in range(4):
            lanes = slice(128 * t, 128 * (t + 1))
            part = prod[:, :, :, lanes]
            summed = shift_columns(part[:, 0], part[:, 1], part[:, 2]).astype(BF16)
            for q, o_ref in enumerate((o0_ref, o1_ref, o2_ref, o3_ref)):
                o_ref[r, :, lanes] = summed[q]


def merge_kernel(a_ref, b_ref, c_ref, d_ref, bias_ref, later_ref, note1_ref, mid_ref, stats_ref, note_ref):
    bias = jnp.concatenate([bias_ref[...]] * 4, axis=1)
    for r in range(8):
        summed = a_ref[r].astype(F32) + b_ref[r].astype(F32)
        summed += c_ref[r].astype(F32) + d_ref[r].astype(F32)
        mid_ref[r, :, 0:256] = later_ref[r]
        mid_ref[r, :, 256:768] = (summed + bias).astype(BF16)
    note_ref[...] = note1_ref[...]
    put_stats(mid_ref, note_ref, stats_ref)


def last_kernel(x_ref, a_ref, b_ref, c_ref, d_ref, bias_ref, o_ref):
    bias = bias_ref[...]
    for r in range(8):
        for t in range(4):
            lanes = slice(128 * t, 128 * (t + 1))
            branch = a_ref[r, :, lanes].astype(F32) + b_ref[r, :, lanes].astype(F32)
            branch += c_ref[r, :, lanes].astype(F32) + d_ref[r, :, lanes].astype(F32)
            o_ref[t, r] = (x_ref[t, r].astype(F32) + (branch + bias)).astype(BF16)


def sides(step):
    return [(i, (i + step) % 4) for i in range(4)] + [(4 + i, 4 + (i - step) % 4) for i in range(4)]


def bring(own, side, other, far):
    far = lax.ppermute(far, "zh", [(i, (i + 2) % 4) for i in range(4)])
    side = lax.ppermute(side, ("core", "zh"), sides(-1))
    other = lax.ppermute(other, ("core", "zh"), sides(1))
    return [own, side, other, far]


def struct(shape, dtype=BF16):
    return jax.ShapeDtypeStruct(shape, dtype)


def edge_kernel(a_ref, b_ref, c_ref, d_ref, chip_ref, next_ref):
    upper = lax.rem(lax.axis_index(ROW), 2) == 0
    towards = jnp.where(upper, 7, 0)
    for k, ref in enumerate((a_ref, b_ref, c_ref, d_ref)):
        chip_ref[k] = ref[towards]
        next_ref[k] = ref[7 - towards]


def rows_beside(blocks):
    chip, beyond = call(edge_kernel, (struct((4, 16, 768)), struct((4, 16, 768))), *blocks, flops=2 * 10**10)
    chip = lax.ppermute(chip, ROW, [(i, i ^ 1) for i in range(16)])
    pairs = [(i, i + 1) for i in range(1, 15, 2)] + [(i + 1, i) for i in range(1, 15, 2)]
    beyond = lax.ppermute(beyond, ROW, pairs)
    return [chip, beyond]


def near(x):
    return [x] + [lax.ppermute(x, NEAR, [(i, i ^ k) for i in range(4)]) for k in (1, 2, 3)]


def exchange(x, axes):
    return lax.all_to_all(x, axes, 0, 0, tiled=True)


def local(frames, cache, norm_gain, norm_shift, conv_weight, conv_bias):
    note = pltpu.VMEM((8, 128), F32)
    piece = (2, 3, 3, 16, 192)
    raw, later, stats, own, side, far = call(
        begin_kernel,
        (
            struct((8, 16, 768)), struct((8, 16, 256)), struct((64, 8, 128), F32), struct(piece),
            struct(piece), struct(piece[1:]),
        ),
        frames, cache, norm_gain, norm_shift, conv_weight.transpose(0, 2, 1, 3),
        scratch=(
            pltpu.VMEM((4, 8, 16, 128), BF16), pltpu.VMEM((2, 2, 8, 16, 128), BF16),
            pltpu.VMEM((2, 16), F32), pltpu.VMEM((2, 16), F32), pltpu.VMEM((2, 27, 16, 256), BF16),
            note, pltpu.VMEM((4,) + piece, BF16), pltpu.SemaphoreType.DMA((5,)),
        ),
        far=(0, 1, 2, 3, 4),
    )
    side = lax.ppermute(side, ("core", "zh"), sides(1))
    far = lax.ppermute(far, "zh", [(i, (i + 2) % 4) for i in range(4)])
    raw = near(raw)
    stats = exchange(stats, ROW + NEAR)
    raw = raw + rows_beside(raw)
    swap = [(0, 1), (1, 0)]
    weights = [own, side, far, lax.ppermute(side, "core", swap), lax.ppermute(far, "core", swap)]
    bias = jnp.broadcast_to(conv_bias[:, :, None], (2, 16, 128))
    note1 = jnp.pad(jnp.stack([norm_gain[1], norm_shift[1]]), ((4, 2), (0, 112)))
    scratch = (
        pltpu.VMEM((3, 4, 16, 128), F32),
        pltpu.VMEM((10, 4, 16, 768), BF16),
        pltpu.VMEM((3, 4, 3, 16, 192), BF16),
    )
    flops = 2 * 192 * 576 * 4096
    parts = (struct((8, 16, 512)),) * 4

    partial = call(
        functools.partial(conv_kernel, 0), parts, *raw, stats, *weights,
        scratch=scratch, flops=flops,
    )
    partial = bring(*partial)
    middle, stats = call(
        merge_kernel, (struct((8, 16, 768)), struct((64, 8, 128), F32)), *partial, bias[0], later, note1,
        scratch=(note,),
    )
    middle = near(middle)
    stats = exchange(stats, ROW + NEAR)
    middle = middle + rows_beside(middle)
    partial = call(
        functools.partial(conv_kernel, 1), parts, *middle, stats, *weights,
        scratch=scratch, flops=flops,
    )
    partial = bring(*partial)
    return call(last_kernel, struct((4, 8, 16, 128)), frames, *partial, bias[1])


def solution(mesh):
    fine = Mesh(mesh.devices.reshape(2, 4, 2, 4, 2, 2), ROW + CHAN)
    placed = (
        P(None, ROW, CHAN, None),
        P(None, None, ROW, CHAN, None),
        P(None, CHAN),
        P(None, CHAN),
        P(None, CHAN, None, None),
        P(None, CHAN),
    )
    return jax.shard_map(
        local, mesh=fine, in_specs=placed, out_specs=P(None, ROW, CHAN, None), check_vma=False
    )
```

```python
import functools

import jax
import jax.numpy as jnp
from jax import lax
from jax.experimental import pallas as pl
from jax.experimental.pallas import tpu as pltpu
from jax.sharding import Mesh, PartitionSpec as P

GROUP = 8
EPS = 1e-06
BF16 = jnp.bfloat16
F32 = jnp.float32

ROW = ("xh", "y", "core")
CHAN = ("zh", "zl", "xl")
NEAR = ("zl", "xl")


def dot(a, b):
    return lax.dot_general(a, b, (((1,), (0,)), ((), ())), preferred_element_type=F32)


def silu(u):
    half = 0.5 * u
    return half + half * jnp.tanh(half)


def call(kernel, outs, *args, far=(), scratch=(), flops=0):
    specs = [pl.BlockSpec(memory_space=pl.ANY if i in far else pltpu.VMEM) for i in range(len(args))]
    moved = sum(a.size * a.dtype.itemsize for a in args)
    return pl.pallas_call(
        kernel,
        out_shape=outs,
        in_specs=specs,
        out_specs=jax.tree.map(lambda _: pl.BlockSpec(memory_space=pltpu.VMEM), outs),
        scratch_shapes=list(scratch),
        compiler_params=pltpu.CompilerParams(vmem_limit_bytes=(60 if far else 40) * 1024 * 1024),
        cost_estimate=pl.CostEstimate(flops=flops, bytes_accessed=moved, transcendentals=0),
    )(*args)


def place():
    return lax.axis_index(ROW), lax.axis_index("zh"), lax.axis_index(NEAR)


def put_stats(rows_ref, note_ref, stats_ref):
    slabs = [rows_ref[:, :, 256 + 128 * t : 384 + 128 * t].astype(F32) for t in range(4)]
    x = jnp.concatenate(slabs, axis=0).reshape(32, 2, GROUP, 128)
    number = x.shape[0] * GROUP
    mean = jnp.sum(x, axis=(0, 2), keepdims=True) / number
    off = x - mean
    square = jnp.sum(off * off, axis=(0, 2))
    note_ref[0:2] = mean.reshape(2, 128)
    note_ref[2:4] = square
    stats_ref[...] = jnp.broadcast_to(note_ref[...][None], stats_ref.shape)


def fetch(pairs, sems):
    copies = [pltpu.make_async_copy(src, dst, sems.at[i]) for i, (src, dst) in enumerate(pairs)]
    for copy in copies:
        copy.start()
    for copy in copies:
        copy.wait()


def begin_kernel(
    x_hbm, cache_hbm, gain_hbm, shift_hbm, w_hbm,
    raw_ref, later_ref, stats_ref, own_ref, side_ref, far_ref,
    x_ref, cache_ref, gain_ref, shift_ref, w_ref, note_ref, pieces_ref, sems,
):
    fetch(
        (
            (x_hbm, x_ref), (cache_hbm, cache_ref), (gain_hbm, gain_ref), (shift_hbm, shift_ref),
            (w_hbm, w_ref),
        ),
        sems,
    )
    for r in range(8):
        for t in range(2):
            lanes = slice(128 * t, 128 * (t + 1))
            raw_ref[r, :, lanes] = cache_ref[0, t, r]
            later_ref[r, :, lanes] = cache_ref[1, t, r]
        for t in range(4):
            raw_ref[r, :, 256 + 128 * t : 384 + 128 * t] = x_ref[t, r]
    row, me, _ = place()
    core = lax.rem(row, 2)
    for q in range(4):
        ahead = lax.rem(q + 4 - me, 4)
        for layer in range(2):
            for dt in range(3):
                for dc in range(3):
                    taps = [
                        w_ref[layer, 9 * dt + 3 * dr + dc, :, 64 * q : 64 * (q + 1)] for dr in range(3)
                    ]
                    pieces_ref[ahead, layer, dt, dc] = jnp.concatenate(taps, axis=1)
    own_ref[...] = pieces_ref[0]
    side_ref[...] = pieces_ref[1 + 2 * core]
    far_ref[...] = pieces_ref[2, core]
    note_ref[...] = jnp.zeros((8, 128), F32)
    note_ref[4:5, 0:16] = gain_ref[0:1, :]
    note_ref[5:6, 0:16] = shift_ref[0:1, :]
    put_stats(raw_ref, note_ref, stats_ref)


def shift_columns(left, centre, right):
    lane = lax.broadcasted_iota(jnp.int32, left.shape, left.ndim - 1)
    axis = left.ndim - 1
    left = jnp.where(lane == 0, 0.0, pltpu.roll(left, 1, axis))
    right = jnp.where(lane == 127, 0.0, pltpu.roll(right, 127, axis))
    return left + centre + right


def get_affine(stats_ref, affine_ref):
    stats = stats_ref[...].reshape(16, 4, 8, 128)
    number = 32 * GROUP
    means = stats[:, :, 0:2]
    mean = jnp.mean(means, axis=(0, 3), keepdims=True)
    off = means - mean
    total = jnp.sum(stats[:, :, 2:4] + number * (off * off), axis=(0, 3), keepdims=True)
    inverse = lax.rsqrt(total / (number * 16 * 128) + EPS)
    mean = jnp.broadcast_to(mean.reshape(4, 2, 1, 1), (4, 2, GROUP, 128)).reshape(4, 16, 128)
    inverse = jnp.broadcast_to(inverse.reshape(4, 2, 1, 1), (4, 2, GROUP, 128)).reshape(4, 16, 128)
    shape = (4, 16, 128)
    same = lax.broadcasted_iota(jnp.int32, shape, 1) == lax.broadcasted_iota(jnp.int32, shape, 2)
    gain = jnp.sum(jnp.where(same, stats[0, :, 4:5], 0.0), axis=2, keepdims=True)
    shift = jnp.sum(jnp.where(same, stats[0, :, 5:6], 0.0), axis=2, keepdims=True)
    affine_ref[0] = mean
    affine_ref[1] = inverse * gain
    affine_ref[2] = jnp.broadcast_to(shift, shape)


def conv_kernel(
    layer, a_ref, b_ref, c_ref, d_ref, chip_ref, next_ref, stats_ref,
    own_ref, side_ref, far_ref, side2_ref, far2_ref, o0_ref, o1_ref, o2_ref, o3_ref,
    affine_ref, slab_ref, held_ref,
):
    row, _, here = place()
    get_affine(stats_ref, affine_ref)
    upper = lax.rem(row, 2) == 0
    not_top = (row > 0).astype(F32)
    not_bottom = (row < 15).astype(F32)
    for k, ref in enumerate((a_ref, b_ref, c_ref, d_ref)):
        b = lax.bitwise_xor(here, k)
        mean = affine_ref[0, b]
        gain = affine_ref[1, b]
        shift = affine_ref[2, b]
        for r in range(10):
            for t in range(6):
                lanes = slice(128 * t, 128 * (t + 1))
                if r == 0:
                    x = jnp.where(upper, next_ref[k, :, lanes].astype(F32), chip_ref[k, :, lanes].astype(F32))
                elif r == 9:
                    x = jnp.where(upper, chip_ref[k, :, lanes].astype(F32), next_ref[k, :, lanes].astype(F32))
                elif t < 2:
                    x = ref[r - 1, :, lanes]
                else:
                    x = ref[r - 1, :, lanes].astype(F32)
                if t >= 2:
                    x = silu((x - mean) * gain + shift)
                if r == 0:
                    x = x * not_top
                if r == 9:
                    x = x * not_bottom
                slab_ref[r, b, :, lanes] = x.astype(BF16)
    core = lax.rem(row, 2)
    for dt in range(3):
        held_ref[dt, 0] = own_ref[layer, dt]
        held_ref[dt, 1] = side_ref[layer, dt]
        held_ref[dt, 2] = side2_ref[layer, dt]

    @pl.when(core == layer)
    def _():
        for dt in range(3):
            held_ref[dt, 3] = far_ref[dt]

    @pl.when(core != layer)
    def _():
        for dt in range(3):
            held_ref[dt, 3] = far2_ref[dt]

    for r in range(8):
        rows = slab_ref[r : r + 3].reshape(192, 768)
        prod = dot(held_ref[0].reshape(192, 192), rows[:, 0:512])
        prod += dot(held_ref[1].reshape(192, 192), rows[:, 128:640])
        prod += dot(held_ref[2].reshape(192, 192), rows[:, 256:768])
        prod = prod.reshape(4, 3, 16, 512)
        for t in range(4):
            lanes = slice(128 * t, 128 * (t + 1))
            part = prod[:, :, :, lanes]
            summed = shift_columns(part[:, 0], part[:, 1], part[:, 2]).astype(BF16)
            for q, o_ref in enumerate((o0_ref, o1_ref, o2_ref, o3_ref)):
                o_ref[r, :, lanes] = summed[q]


def merge_kernel(a_ref, b_ref, c_ref, d_ref, bias_ref, later_ref, note1_ref, mid_ref, stats_ref, note_ref):
    bias = jnp.concatenate([bias_ref[...]] * 4, axis=1)
    for r in range(8):
        summed = a_ref[r].astype(F32) + b_ref[r].astype(F32)
        summed += c_ref[r].astype(F32) + d_ref[r].astype(F32)
        mid_ref[r, :, 0:256] = later_ref[r]
        mid_ref[r, :, 256:768] = (summed + bias).astype(BF16)
    note_ref[...] = note1_ref[...]
    put_stats(mid_ref, note_ref, stats_ref)


def last_kernel(x_ref, a_ref, b_ref, c_ref, d_ref, bias_ref, o_ref):
    bias = bias_ref[...]
    for r in range(8):
        for t in range(4):
            lanes = slice(128 * t, 128 * (t + 1))
            branch = a_ref[r, :, lanes].astype(F32) + b_ref[r, :, lanes].astype(F32)
            branch += c_ref[r, :, lanes].astype(F32) + d_ref[r, :, lanes].astype(F32)
            o_ref[t, r] = (x_ref[t, r].astype(F32) + (branch + bias)).astype(BF16)


def sides(step):
    return [(i, (i + step) % 4) for i in range(4)] + [(4 + i, 4 + (i - step) % 4) for i in range(4)]


def bring(own, side, other, far):
    far = lax.ppermute(far, "zh", [(i, (i + 2) % 4) for i in range(4)])
    side = lax.ppermute(side, ("core", "zh"), sides(-1))
    other = lax.ppermute(other, ("core", "zh"), sides(1))
    return [far, side, other, own]


def struct(shape, dtype=BF16):
    return jax.ShapeDtypeStruct(shape, dtype)


def edge_kernel(a_ref, b_ref, c_ref, d_ref, chip_ref, next_ref):
    upper = lax.rem(lax.axis_index(ROW), 2) == 0
    towards = jnp.where(upper, 7, 0)
    for k, ref in enumerate((a_ref, b_ref, c_ref, d_ref)):
        chip_ref[k] = ref[towards]
        next_ref[k] = ref[7 - towards]


def rows_beside(blocks):
    chip, beyond = call(edge_kernel, (struct((4, 16, 768)), struct((4, 16, 768))), *blocks, flops=2 * 10**10)
    chip = lax.ppermute(chip, ROW, [(i, i ^ 1) for i in range(16)])
    pairs = [(i, i + 1) for i in range(1, 15, 2)] + [(i + 1, i) for i in range(1, 15, 2)]
    beyond = lax.ppermute(beyond, ROW, pairs)
    return [chip, beyond]


def near(x):
    return [x] + [lax.ppermute(x, NEAR, [(i, i ^ k) for i in range(4)]) for k in (1, 2, 3)]


def exchange(x, axes):
    return lax.all_to_all(x, axes, 0, 0, tiled=True)


def local(frames, cache, norm_gain, norm_shift, conv_weight, conv_bias):
    note = pltpu.VMEM((8, 128), F32)
    piece = (2, 3, 3, 16, 192)
    raw, later, stats, own, side, far = call(
        begin_kernel,
        (
            struct((8, 16, 768)), struct((8, 16, 256)), struct((64, 8, 128), F32), struct(piece),
            struct(piece), struct(piece[1:]),
        ),
        frames, cache, norm_gain, norm_shift, conv_weight.transpose(0, 2, 1, 3),
        scratch=(
            pltpu.VMEM((4, 8, 16, 128), BF16), pltpu.VMEM((2, 2, 8, 16, 128), BF16),
            pltpu.VMEM((2, 16), F32), pltpu.VMEM((2, 16), F32), pltpu.VMEM((2, 27, 16, 256), BF16),
            note, pltpu.VMEM((4,) + piece, BF16), pltpu.SemaphoreType.DMA((5,)),
        ),
        far=(0, 1, 2, 3, 4),
    )
    side = lax.ppermute(side, ("core", "zh"), sides(1))
    far = lax.ppermute(lax.ppermute(far, ("core", "zh"), sides(1)), ("core", "zh"), sides(1))
    raw = near(raw)
    stats = exchange(stats, ROW + NEAR)
    raw = raw + rows_beside(raw)
    swap = [(0, 1), (1, 0)]
    weights = [own, side, far, lax.ppermute(side, "core", swap), lax.ppermute(far, "core", swap)]
    bias = jnp.broadcast_to(conv_bias[:, :, None], (2, 16, 128))
    note1 = jnp.pad(jnp.stack([norm_gain[1], norm_shift[1]]), ((4, 2), (0, 112)))
    scratch = (
        pltpu.VMEM((3, 4, 16, 128), F32),
        pltpu.VMEM((10, 4, 16, 768), BF16),
        pltpu.VMEM((3, 4, 3, 16, 192), BF16),
    )
    flops = 2 * 192 * 576 * 4096
    parts = (struct((8, 16, 512)),) * 4

    partial = call(
        functools.partial(conv_kernel, 0), parts, *raw, stats, *weights,
        scratch=scratch, flops=flops,
    )
    partial = bring(*partial)
    middle, stats = call(
        merge_kernel, (struct((8, 16, 768)), struct((64, 8, 128), F32)), *partial, bias[0], later, note1,
        scratch=(note,),
    )
    middle = near(middle)
    stats = exchange(stats, ROW + NEAR)
    middle = middle + rows_beside(middle)
    partial = call(
        functools.partial(conv_kernel, 1), parts, *middle, stats, *weights,
        scratch=scratch, flops=flops,
    )
    partial = bring(*partial)
    return call(last_kernel, struct((4, 8, 16, 128)), frames, *partial, bias[1])


def solution(mesh):
    fine = Mesh(mesh.devices.reshape(2, 4, 2, 4, 2, 2), ROW + CHAN)
    placed = (
        P(None, ROW, CHAN, None),
        P(None, None, ROW, CHAN, None),
        P(None, CHAN),
        P(None, CHAN),
        P(None, CHAN, None, None),
        P(None, CHAN),
    )
    return jax.shard_map(
        local, mesh=fine, in_specs=placed, out_specs=P(None, ROW, CHAN, None), check_vma=False
    )
```

```python
import functools

import jax
import jax.numpy as jnp
from jax import lax
from jax.experimental import pallas as pl
from jax.experimental.pallas import tpu as pltpu
from jax.sharding import Mesh, PartitionSpec as P

GROUP = 8
EPS = 1e-06
BF16 = jnp.bfloat16
F32 = jnp.float32

ROW = ("xh", "y", "core")
CHAN = ("zh", "zl", "xl")
NEAR = ("zl", "xl")


def dot(a, b):
    return lax.dot_general(a, b, (((1,), (0,)), ((), ())), preferred_element_type=F32)


def silu(u):
    return u / (1.0 + jnp.exp(-u))


def call(kernel, outs, *args, far=(), scratch=(), flops=0):
    specs = [pl.BlockSpec(memory_space=pl.ANY if i in far else pltpu.VMEM) for i in range(len(args))]
    moved = sum(a.size * a.dtype.itemsize for a in args)
    return pl.pallas_call(
        kernel,
        out_shape=outs,
        in_specs=specs,
        out_specs=jax.tree.map(lambda _: pl.BlockSpec(memory_space=pltpu.VMEM), outs),
        scratch_shapes=list(scratch),
        compiler_params=pltpu.CompilerParams(vmem_limit_bytes=(60 if far else 40) * 1024 * 1024),
        cost_estimate=pl.CostEstimate(flops=flops, bytes_accessed=moved, transcendentals=0),
    )(*args)


def place():
    return lax.axis_index(ROW), lax.axis_index("zh"), lax.axis_index(NEAR)


def gathered_lanes():
    shape = (256, 256)
    old = lax.broadcasted_iota(jnp.int32, shape, 0)
    new = lax.broadcasted_iota(jnp.int32, shape, 1)
    group, rest = lax.shift_right_logical(old, 6), lax.bitwise_and(old, 15)
    member = lax.bitwise_and(lax.shift_right_logical(old, 4), 3)
    return jnp.where(new == 64 * member + 16 * group + rest, 1.0, 0.0).astype(BF16)


def put_stats(rows_ref, note_ref, stats_ref):
    slabs = [rows_ref[:, :, 256 + 128 * t : 384 + 128 * t].astype(F32) for t in range(4)]
    x = jnp.concatenate(slabs, axis=0).reshape(32, 2, GROUP, 128)
    number = x.shape[0] * GROUP
    mean = jnp.sum(x, axis=(0, 2), keepdims=True) / number
    off = x - mean
    square = jnp.sum(off * off, axis=(0, 2))
    note_ref[0:2] = mean.reshape(2, 128)
    note_ref[2:4] = square
    stats_ref[...] = jnp.broadcast_to(note_ref[...][None], stats_ref.shape)


def fetch(pairs, sems):
    copies = [pltpu.make_async_copy(src, dst, sems.at[i]) for i, (src, dst) in enumerate(pairs)]
    for copy in copies:
        copy.start()
    for copy in copies:
        copy.wait()


def begin_kernel(
    x_hbm, cache_hbm, gain_hbm, shift_hbm, w_hbm,
    raw_ref, later_ref, stats_ref, own_ref, w1_ref, w2_ref, w3_ref,
    x_ref, cache_ref, gain_ref, shift_ref, w_ref, note_ref, pieces_ref, sems,
):
    fetch(
        (
            (x_hbm, x_ref), (cache_hbm, cache_ref), (gain_hbm, gain_ref), (shift_hbm, shift_ref),
            (w_hbm, w_ref),
        ),
        sems,
    )
    for r in range(8):
        for t in range(2):
            lanes = slice(128 * t, 128 * (t + 1))
            raw_ref[r, :, lanes] = cache_ref[0, t, r]
            later_ref[r, :, lanes] = cache_ref[1, t, r]
        for t in range(4):
            raw_ref[r, :, 256 + 128 * t : 384 + 128 * t] = x_ref[t, r]
    _, _, here = place()
    held = dot(w_ref[...].reshape(864, 256), gathered_lanes()).astype(BF16).reshape(2, 27, 16, 256)
    for n in range(4):
        for layer in range(2):
            for dt in range(3):
                for dc in range(3):
                    taps = [
                        held[layer, 9 * dt + 3 * dr + dc, :, 64 * n : 64 * (n + 1)] for dr in range(3)
                    ]
                    pieces_ref[lax.bitwise_xor(here, n), layer, dt, dc] = jnp.concatenate(taps, axis=1)
    for k, ref in enumerate((own_ref, w1_ref, w2_ref, w3_ref)):
        ref[...] = pieces_ref[k]
    note_ref[...] = jnp.zeros((8, 128), F32)
    note_ref[4:5, 0:16] = gain_ref[0:1, :]
    note_ref[5:6, 0:16] = shift_ref[0:1, :]
    put_stats(raw_ref, note_ref, stats_ref)


def shift_columns(left, centre, right):
    lane = lax.broadcasted_iota(jnp.int32, left.shape, left.ndim - 1)
    axis = left.ndim - 1
    left = jnp.where(lane == 0, 0.0, pltpu.roll(left, 1, axis))
    right = jnp.where(lane == 127, 0.0, pltpu.roll(right, 127, axis))
    return left + centre + right


def get_affine(stats_ref, affine_ref):
    stats = stats_ref[...].reshape(16, 4, 8, 128)
    number = 32 * GROUP
    means = stats[:, :, 0:2]
    mean = jnp.mean(means, axis=(0, 3), keepdims=True)
    off = means - mean
    total = jnp.sum(stats[:, :, 2:4] + number * (off * off), axis=(0, 3), keepdims=True)
    inverse = lax.rsqrt(total / (number * 16 * 128) + EPS)
    mean = jnp.broadcast_to(mean.reshape(4, 2, 1, 1), (4, 2, GROUP, 128)).reshape(4, 16, 128)
    inverse = jnp.broadcast_to(inverse.reshape(4, 2, 1, 1), (4, 2, GROUP, 128)).reshape(4, 16, 128)
    shape = (4, 16, 128)
    same = lax.broadcasted_iota(jnp.int32, shape, 1) == lax.broadcasted_iota(jnp.int32, shape, 2)
    gain = jnp.sum(jnp.where(same, stats[0, :, 4:5], 0.0), axis=2, keepdims=True)
    shift = jnp.sum(jnp.where(same, stats[0, :, 5:6], 0.0), axis=2, keepdims=True)
    affine_ref[0] = mean
    affine_ref[1] = inverse * gain
    affine_ref[2] = jnp.broadcast_to(shift, shape)


def conv_kernel(
    layer, a_ref, b_ref, c_ref, d_ref, chip_ref, next_ref, stats_ref,
    w0_ref, w1_ref, w2_ref, w3_ref, o0_ref, o1_ref, o2_ref, o3_ref,
    affine_ref, slab_ref, held_ref,
):
    row, here, _ = place()
    get_affine(stats_ref, affine_ref)
    upper = lax.rem(row, 2) == 0
    not_top = (row > 0).astype(F32)
    not_bottom = (row < 15).astype(F32)
    for k, ref in enumerate((a_ref, b_ref, c_ref, d_ref)):
        b = lax.bitwise_xor(here, k)
        mean = affine_ref[0, b]
        gain = affine_ref[1, b]
        shift = affine_ref[2, b]
        for r in range(10):
            for t in range(6):
                lanes = slice(128 * t, 128 * (t + 1))
                if r == 0:
                    x = jnp.where(upper, next_ref[k, :, lanes].astype(F32), chip_ref[k, :, lanes].astype(F32))
                elif r == 9:
                    x = jnp.where(upper, chip_ref[k, :, lanes].astype(F32), next_ref[k, :, lanes].astype(F32))
                elif t < 2:
                    x = ref[r - 1, :, lanes]
                else:
                    x = ref[r - 1, :, lanes].astype(F32)
                if t >= 2:
                    x = silu((x - mean) * gain + shift)
                if r == 0:
                    x = x * not_top
                if r == 9:
                    x = x * not_bottom
                slab_ref[r, b, :, lanes] = x.astype(BF16)
    for k, w_ref in enumerate((w0_ref, w1_ref, w2_ref, w3_ref)):
        for dt in range(3):
            held_ref[dt, k] = w_ref[layer, dt]
    for r in range(8):
        rows = slab_ref[r : r + 3].reshape(192, 768)
        prod = dot(held_ref[0].reshape(192, 192), rows[:, 0:512])
        prod += dot(held_ref[1].reshape(192, 192), rows[:, 128:640])
        prod += dot(held_ref[2].reshape(192, 192), rows[:, 256:768])
        prod = prod.reshape(4, 3, 16, 512)
        for t in range(4):
            lanes = slice(128 * t, 128 * (t + 1))
            part = prod[:, :, :, lanes]
            summed = shift_columns(part[:, 0], part[:, 1], part[:, 2]).astype(BF16)
            for q, o_ref in enumerate((o0_ref, o1_ref, o2_ref, o3_ref)):
                o_ref[r, :, lanes] = summed[q]


def merge_kernel(a_ref, b_ref, c_ref, d_ref, bias_ref, later_ref, note1_ref, mid_ref, stats_ref, note_ref):
    bias = jnp.concatenate([bias_ref[...]] * 4, axis=1)
    for r in range(8):
        summed = a_ref[r].astype(F32) + b_ref[r].astype(F32)
        summed += c_ref[r].astype(F32) + d_ref[r].astype(F32)
        mid_ref[r, :, 0:256] = later_ref[r]
        mid_ref[r, :, 256:768] = (summed + bias).astype(BF16)
    note_ref[...] = note1_ref[...]
    put_stats(mid_ref, note_ref, stats_ref)


def last_kernel(x_ref, a_ref, b_ref, c_ref, d_ref, bias_ref, o_ref):
    bias = bias_ref[...]
    for r in range(8):
        for t in range(4):
            lanes = slice(128 * t, 128 * (t + 1))
            branch = a_ref[r, :, lanes].astype(F32) + b_ref[r, :, lanes].astype(F32)
            branch += c_ref[r, :, lanes].astype(F32) + d_ref[r, :, lanes].astype(F32)
            o_ref[t, r] = (x_ref[t, r].astype(F32) + (branch + bias)).astype(BF16)


def struct(shape, dtype=BF16):
    return jax.ShapeDtypeStruct(shape, dtype)


def edge_kernel(a_ref, b_ref, c_ref, d_ref, chip_ref, next_ref):
    upper = lax.rem(lax.axis_index(ROW), 2) == 0
    towards = jnp.where(upper, 7, 0)
    for k, ref in enumerate((a_ref, b_ref, c_ref, d_ref)):
        chip_ref[k] = ref[towards]
        next_ref[k] = ref[7 - towards]


def rows_beside(blocks):
    chip, beyond = call(edge_kernel, (struct((4, 16, 768)), struct((4, 16, 768))), *blocks, flops=2 * 10**10)
    chip = lax.ppermute(chip, ROW, [(i, i ^ 1) for i in range(16)])
    pairs = [(i, i + 1) for i in range(1, 15, 2)] + [(i + 1, i) for i in range(1, 15, 2)]
    beyond = lax.ppermute(beyond, ROW, pairs)
    return [chip, beyond]


def gather(x):
    return [x] + [lax.ppermute(x, "zh", [(i, i ^ k) for i in range(4)]) for k in (1, 2, 3)]


def bring(blocks):
    moved = [lax.ppermute(blocks[k], NEAR, [(i, i ^ k) for i in range(4)]) for k in (1, 2, 3)]
    return [blocks[0]] + moved


def exchange(x, axes):
    return lax.all_to_all(x, axes, 0, 0, tiled=True)


def local(frames, cache, norm_gain, norm_shift, conv_weight, conv_bias):
    note = pltpu.VMEM((8, 128), F32)
    piece = (2, 3, 3, 16, 192)
    raw, later, stats, *weights = call(
        begin_kernel,
        (
            struct((8, 16, 768)), struct((8, 16, 256)), struct((64, 8, 128), F32), struct(piece),
            struct(piece), struct(piece), struct(piece),
        ),
        frames, cache, norm_gain, norm_shift, conv_weight.transpose(0, 2, 1, 3),
        scratch=(
            pltpu.VMEM((4, 8, 16, 128), BF16), pltpu.VMEM((2, 2, 8, 16, 128), BF16),
            pltpu.VMEM((2, 16), F32), pltpu.VMEM((2, 16), F32), pltpu.VMEM((2, 27, 16, 256), BF16),
            note, pltpu.VMEM((4,) + piece, BF16), pltpu.SemaphoreType.DMA((5,)),
        ),
        far=(0, 1, 2, 3, 4),
    )
    raw = gather(raw)
    weights = bring(weights)
    stats = exchange(stats, ROW + ("zh",))
    raw = raw + rows_beside(raw)
    bias = jnp.broadcast_to(conv_bias[:, :, None], (2, 16, 128))
    note1 = jnp.pad(jnp.stack([norm_gain[1], norm_shift[1]]), ((4, 2), (0, 112)))
    scratch = (
        pltpu.VMEM((3, 4, 16, 128), F32),
        pltpu.VMEM((10, 4, 16, 768), BF16),
        pltpu.VMEM((3, 4, 3, 16, 192), BF16),
    )
    flops = 2 * 192 * 576 * 4096
    parts = (struct((8, 16, 512)),) * 4

    partial = call(
        functools.partial(conv_kernel, 0), parts, *raw, stats, *weights,
        scratch=scratch, flops=flops,
    )
    partial = bring(partial)
    middle, stats = call(
        merge_kernel, (struct((8, 16, 768)), struct((64, 8, 128), F32)), *partial, bias[0], later, note1,
        scratch=(note,),
    )
    middle = gather(middle)
    stats = exchange(stats, ROW + ("zh",))
    middle = middle + rows_beside(middle)
    partial = call(
        functools.partial(conv_kernel, 1), parts, *middle, stats, *weights,
        scratch=scratch, flops=flops,
    )
    partial = bring(partial)
    return call(last_kernel, struct((4, 8, 16, 128)), frames, *partial, bias[1])


def solution(mesh):
    fine = Mesh(mesh.devices.reshape(2, 4, 2, 4, 2, 2), ROW + CHAN)
    placed = (
        P(None, ROW, CHAN, None),
        P(None, None, ROW, CHAN, None),
        P(None, CHAN),
        P(None, CHAN),
        P(None, CHAN, None, None),
        P(None, CHAN),
    )
    return jax.shard_map(
        local, mesh=fine, in_specs=placed, out_specs=P(None, ROW, CHAN, None), check_vma=False
    )
```

```python
import functools

import jax
import jax.numpy as jnp
from jax import lax
from jax.experimental import pallas as pl
from jax.experimental.pallas import tpu as pltpu
from jax.sharding import Mesh, PartitionSpec as P

GROUP = 8
EPS = 1e-06
BF16 = jnp.bfloat16
F32 = jnp.float32

ROW = ("xh", "y", "core")
CHAN = ("zh", "zl", "xl")
NEAR = ("zl", "xl")


def dot(a, b):
    return lax.dot_general(a, b, (((1,), (0,)), ((), ())), preferred_element_type=F32)


def silu(u):
    return u / (1.0 + jnp.exp(-u))


def call(kernel, outs, *args, far=(), scratch=(), flops=0):
    specs = [pl.BlockSpec(memory_space=pl.ANY if i in far else pltpu.VMEM) for i in range(len(args))]
    moved = sum(a.size * a.dtype.itemsize for a in args)
    return pl.pallas_call(
        kernel,
        out_shape=outs,
        in_specs=specs,
        out_specs=jax.tree.map(lambda _: pl.BlockSpec(memory_space=pltpu.VMEM), outs),
        scratch_shapes=list(scratch),
        compiler_params=pltpu.CompilerParams(vmem_limit_bytes=(60 if far else 40) * 1024 * 1024),
        cost_estimate=pl.CostEstimate(flops=flops, bytes_accessed=moved, transcendentals=0),
    )(*args)


def place():
    return lax.axis_index(ROW), lax.axis_index("zh"), lax.axis_index(NEAR)


def put_stats(rows_ref, note_ref):
    slabs = [rows_ref[:, :, 256 + 128 * t : 384 + 128 * t].astype(F32) for t in range(4)]
    x = jnp.concatenate(slabs, axis=0).reshape(32, 2, GROUP, 128)
    number = x.shape[0] * GROUP
    mean = jnp.sum(x, axis=(0, 2), keepdims=True) / number
    off = x - mean
    square = jnp.sum(off * off, axis=(0, 2))
    note_ref[0:2] = mean.reshape(2, 128)
    note_ref[2:4] = square


def spread_kernel(a_ref, b_ref, c_ref, d_ref, stats_ref):
    for k, ref in enumerate((a_ref, b_ref, c_ref, d_ref)):
        stats_ref[:, k] = jnp.broadcast_to(ref[...][None], (16, 8, 128))


def fetch(pairs, sems):
    copies = [pltpu.make_async_copy(src, dst, sems.at[i]) for i, (src, dst) in enumerate(pairs)]
    for copy in copies:
        copy.start()
    for copy in copies:
        copy.wait()


def begin_kernel(
    x_hbm, cache_hbm, gain_hbm, shift_hbm, w_hbm,
    raw_ref, later_ref, note_ref, own_ref, side_ref, far_ref,
    x_ref, cache_ref, gain_ref, shift_ref, w_ref, pieces_ref, sems,
):
    fetch(
        (
            (x_hbm, x_ref), (cache_hbm, cache_ref), (gain_hbm, gain_ref), (shift_hbm, shift_ref),
            (w_hbm, w_ref),
        ),
        sems,
    )
    for r in range(8):
        for t in range(2):
            lanes = slice(128 * t, 128 * (t + 1))
            raw_ref[r, :, lanes] = cache_ref[0, t, r]
            later_ref[r, :, lanes] = cache_ref[1, t, r]
        for t in range(4):
            raw_ref[r, :, 256 + 128 * t : 384 + 128 * t] = x_ref[t, r]
    row, me, _ = place()
    core = lax.rem(row, 2)
    for q in range(4):
        ahead = lax.rem(q + 4 - me, 4)
        for layer in range(2):
            for dt in range(3):
                for dc in range(3):
                    taps = [
                        w_ref[layer, 9 * dt + 3 * dr + dc, :, 64 * q : 64 * (q + 1)] for dr in range(3)
                    ]
                    pieces_ref[ahead, layer, dt, dc] = jnp.concatenate(taps, axis=1)
    own_ref[...] = pieces_ref[0]
    side_ref[...] = pieces_ref[1 + 2 * core]
    far_ref[...] = pieces_ref[2, core]
    note_ref[...] = jnp.zeros((8, 128), F32)
    note_ref[4:5, 0:16] = gain_ref[0:1, :]
    note_ref[5:6, 0:16] = shift_ref[0:1, :]
    put_stats(raw_ref, note_ref)


def shift_columns(left, centre, right):
    lane = lax.broadcasted_iota(jnp.int32, left.shape, left.ndim - 1)
    axis = left.ndim - 1
    left = jnp.where(lane == 0, 0.0, pltpu.roll(left, 1, axis))
    right = jnp.where(lane == 127, 0.0, pltpu.roll(right, 127, axis))
    return left + centre + right


def get_affine(stats_ref, affine_ref):
    stats = stats_ref[...]
    number = 32 * GROUP
    means = stats[:, :, 0:2]
    mean = jnp.mean(means, axis=(0, 3), keepdims=True)
    off = means - mean
    total = jnp.sum(stats[:, :, 2:4] + number * (off * off), axis=(0, 3), keepdims=True)
    inverse = lax.rsqrt(total / (number * 16 * 128) + EPS)
    mean = jnp.broadcast_to(mean.reshape(4, 2, 1, 1), (4, 2, GROUP, 128)).reshape(4, 16, 128)
    inverse = jnp.broadcast_to(inverse.reshape(4, 2, 1, 1), (4, 2, GROUP, 128)).reshape(4, 16, 128)
    shape = (4, 16, 128)
    same = lax.broadcasted_iota(jnp.int32, shape, 1) == lax.broadcasted_iota(jnp.int32, shape, 2)
    gain = jnp.sum(jnp.where(same, stats[0, :, 4:5], 0.0), axis=2, keepdims=True)
    shift = jnp.sum(jnp.where(same, stats[0, :, 5:6], 0.0), axis=2, keepdims=True)
    affine_ref[0] = mean
    affine_ref[1] = inverse * gain
    affine_ref[2] = jnp.broadcast_to(shift, shape)


def conv_kernel(
    layer, a_ref, b_ref, c_ref, d_ref, chip_ref, next_ref, stats_ref,
    own_ref, side_ref, far_ref, side2_ref, far2_ref, o0_ref, o1_ref, o2_ref, o3_ref,
    affine_ref, slab_ref, held_ref,
):
    row, _, here = place()
    get_affine(stats_ref, affine_ref)
    upper = lax.rem(row, 2) == 0
    not_top = (row > 0).astype(F32)
    not_bottom = (row < 15).astype(F32)
    for k, ref in enumerate((a_ref, b_ref, c_ref, d_ref)):
        b = lax.bitwise_xor(here, k)
        mean = affine_ref[0, k]
        gain = affine_ref[1, k]
        shift = affine_ref[2, k]
        for r in range(10):
            for t in range(6):
                lanes = slice(128 * t, 128 * (t + 1))
                if r == 0:
                    x = jnp.where(upper, next_ref[k, :, lanes].astype(F32), chip_ref[k, :, lanes].astype(F32))
                elif r == 9:
                    x = jnp.where(upper, chip_ref[k, :, lanes].astype(F32), next_ref[k, :, lanes].astype(F32))
                elif t < 2:
                    x = ref[r - 1, :, lanes]
                else:
                    x = ref[r - 1, :, lanes].astype(F32)
                if t >= 2:
                    x = silu((x - mean) * gain + shift)
                if r == 0:
                    x = x * not_top
                if r == 9:
                    x = x * not_bottom
                slab_ref[r, b, :, lanes] = x.astype(BF16)
    core = lax.rem(row, 2)
    for dt in range(3):
        held_ref[dt, 0] = own_ref[layer, dt]
        held_ref[dt, 1] = side_ref[layer, dt]
        held_ref[dt, 2] = side2_ref[layer, dt]

    @pl.when(core == layer)
    def _():
        for dt in range(3):
            held_ref[dt, 3] = far_ref[dt]

    @pl.when(core != layer)
    def _():
        for dt in range(3):
            held_ref[dt, 3] = far2_ref[dt]

    for r in range(8):
        rows = slab_ref[r : r + 3].reshape(192, 768)
        prod = dot(held_ref[0].reshape(192, 192), rows[:, 0:512])
        prod += dot(held_ref[1].reshape(192, 192), rows[:, 128:640])
        prod += dot(held_ref[2].reshape(192, 192), rows[:, 256:768])
        prod = prod.reshape(4, 3, 16, 512)
        for t in range(4):
            lanes = slice(128 * t, 128 * (t + 1))
            part = prod[:, :, :, lanes]
            summed = shift_columns(part[:, 0], part[:, 1], part[:, 2]).astype(BF16)
            for q, o_ref in enumerate((o0_ref, o1_ref, o2_ref, o3_ref)):
                o_ref[r, :, lanes] = summed[q]


def merge_kernel(a_ref, b_ref, c_ref, d_ref, bias_ref, later_ref, note1_ref, mid_ref, note_ref):
    bias = jnp.concatenate([bias_ref[...]] * 4, axis=1)
    for r in range(8):
        summed = a_ref[r].astype(F32) + b_ref[r].astype(F32)
        summed += c_ref[r].astype(F32) + d_ref[r].astype(F32)
        mid_ref[r, :, 0:256] = later_ref[r]
        mid_ref[r, :, 256:768] = (summed + bias).astype(BF16)
    note_ref[...] = note1_ref[...]
    put_stats(mid_ref, note_ref)


def last_kernel(x_ref, a_ref, b_ref, c_ref, d_ref, bias_ref, o_ref):
    bias = bias_ref[...]
    for r in range(8):
        for t in range(4):
            lanes = slice(128 * t, 128 * (t + 1))
            branch = a_ref[r, :, lanes].astype(F32) + b_ref[r, :, lanes].astype(F32)
            branch += c_ref[r, :, lanes].astype(F32) + d_ref[r, :, lanes].astype(F32)
            o_ref[t, r] = (x_ref[t, r].astype(F32) + (branch + bias)).astype(BF16)


def near_and_stats(rows, local_stats):
    notes = near(local_stats)
    rows, notes = lax.optimization_barrier((rows, notes))
    rows = near(rows)
    stats = call(spread_kernel, struct((16, 4, 8, 128), F32), *notes)
    return rows, exchange(stats, ROW)


def sides(step):
    return [(i, (i + step) % 4) for i in range(4)] + [(4 + i, 4 + (i - step) % 4) for i in range(4)]


def bring(own, side, other, far):
    far = lax.ppermute(far, "zh", [(i, (i + 2) % 4) for i in range(4)])
    side = lax.ppermute(side, ("core", "zh"), sides(-1))
    other = lax.ppermute(other, ("core", "zh"), sides(1))
    return [own, side, other, far]


def struct(shape, dtype=BF16):
    return jax.ShapeDtypeStruct(shape, dtype)


def edge_kernel(a_ref, b_ref, c_ref, d_ref, chip_ref, next_ref):
    upper = lax.rem(lax.axis_index(ROW), 2) == 0
    towards = jnp.where(upper, 7, 0)
    for k, ref in enumerate((a_ref, b_ref, c_ref, d_ref)):
        chip_ref[k] = ref[towards]
        next_ref[k] = ref[7 - towards]


def rows_beside(blocks):
    chip, beyond = call(edge_kernel, (struct((4, 16, 768)), struct((4, 16, 768))), *blocks, flops=2 * 10**10)
    chip = lax.ppermute(chip, ROW, [(i, i ^ 1) for i in range(16)])
    pairs = [(i, i + 1) for i in range(1, 15, 2)] + [(i + 1, i) for i in range(1, 15, 2)]
    beyond = lax.ppermute(beyond, ROW, pairs)
    return [chip, beyond]


def near(x):
    return [x] + [lax.ppermute(x, NEAR, [(i, i ^ k) for i in range(4)]) for k in (1, 2, 3)]


def exchange(x, axes):
    return lax.all_to_all(x, axes, 0, 0, tiled=True)


def local(frames, cache, norm_gain, norm_shift, conv_weight, conv_bias):
    note = struct((8, 128), F32)
    piece = (2, 3, 3, 16, 192)
    raw, later, local_stats, own, side, far = call(
        begin_kernel,
        (
            struct((8, 16, 768)), struct((8, 16, 256)), note, struct(piece),
            struct(piece), struct(piece[1:]),
        ),
        frames, cache, norm_gain, norm_shift, conv_weight.transpose(0, 2, 1, 3),
        scratch=(
            pltpu.VMEM((4, 8, 16, 128), BF16), pltpu.VMEM((2, 2, 8, 16, 128), BF16),
            pltpu.VMEM((2, 16), F32), pltpu.VMEM((2, 16), F32), pltpu.VMEM((2, 27, 16, 256), BF16),
            pltpu.VMEM((4,) + piece, BF16), pltpu.SemaphoreType.DMA((5,)),
        ),
        far=(0, 1, 2, 3, 4),
    )
    side = lax.ppermute(side, ("core", "zh"), sides(1))
    far = lax.ppermute(far, "zh", [(i, (i + 2) % 4) for i in range(4)])
    raw, stats = near_and_stats(raw, local_stats)
    raw = raw + rows_beside(raw)
    swap = [(0, 1), (1, 0)]
    weights = [own, side, far, lax.ppermute(side, "core", swap), lax.ppermute(far, "core", swap)]
    bias = jnp.broadcast_to(conv_bias[:, :, None], (2, 16, 128))
    note1 = jnp.pad(jnp.stack([norm_gain[1], norm_shift[1]]), ((4, 2), (0, 112)))
    scratch = (
        pltpu.VMEM((3, 4, 16, 128), F32),
        pltpu.VMEM((10, 4, 16, 768), BF16),
        pltpu.VMEM((3, 4, 3, 16, 192), BF16),
    )
    flops = 2 * 192 * 576 * 4096
    parts = (struct((8, 16, 512)),) * 4

    partial = call(
        functools.partial(conv_kernel, 0), parts, *raw, stats, *weights,
        scratch=scratch, flops=flops,
    )
    partial = bring(*partial)
    middle, local_stats = call(
        merge_kernel, (struct((8, 16, 768)), note), *partial, bias[0], later, note1
    )
    middle, stats = near_and_stats(middle, local_stats)
    middle = middle + rows_beside(middle)
    partial = call(
        functools.partial(conv_kernel, 1), parts, *middle, stats, *weights,
        scratch=scratch, flops=flops,
    )
    partial = bring(*partial)
    return call(last_kernel, struct((4, 8, 16, 128)), frames, *partial, bias[1])


def solution(mesh):
    fine = Mesh(mesh.devices.reshape(2, 4, 2, 4, 2, 2), ROW + CHAN)
    placed = (
        P(None, ROW, CHAN, None),
        P(None, None, ROW, CHAN, None),
        P(None, CHAN),
        P(None, CHAN),
        P(None, CHAN, None, None),
        P(None, CHAN),
    )
    return jax.shard_map(
        local, mesh=fine, in_specs=placed, out_specs=P(None, ROW, CHAN, None), check_vma=False
    )
```

```python
import functools

import jax
import jax.numpy as jnp
from jax import lax
from jax.experimental import pallas as pl
from jax.experimental.pallas import tpu as pltpu
from jax.sharding import Mesh, PartitionSpec as P

GROUP = 8
EPS = 1e-06
BF16 = jnp.bfloat16
F32 = jnp.float32

ROW = ("xh", "y", "core")
CHAN = ("zh", "zl", "xl")
NEAR = ("zl", "xl")


def dot(a, b):
    return lax.dot_general(a, b, (((1,), (0,)), ((), ())), preferred_element_type=F32)


def silu(u):
    return u / (1.0 + jnp.exp(-u))


def call(kernel, outs, *args, far=(), scratch=(), flops=0):
    specs = [pl.BlockSpec(memory_space=pl.ANY if i in far else pltpu.VMEM) for i in range(len(args))]
    moved = sum(a.size * a.dtype.itemsize for a in args)
    return pl.pallas_call(
        kernel,
        out_shape=outs,
        in_specs=specs,
        out_specs=jax.tree.map(lambda _: pl.BlockSpec(memory_space=pltpu.VMEM), outs),
        scratch_shapes=list(scratch),
        compiler_params=pltpu.CompilerParams(vmem_limit_bytes=(60 if far else 40) * 1024 * 1024),
        cost_estimate=pl.CostEstimate(flops=flops, bytes_accessed=moved, transcendentals=0),
    )(*args)


def place():
    return lax.axis_index(ROW), lax.axis_index("zh"), lax.axis_index(NEAR)


def put_stats(rows_ref, note_ref, stats_ref):
    slabs = [rows_ref[:, :, 256 + 128 * t : 384 + 128 * t].astype(F32) for t in range(4)]
    x = jnp.concatenate(slabs, axis=0).reshape(32, 2, GROUP, 128)
    number = x.shape[0] * GROUP
    mean = jnp.sum(x, axis=(0, 2), keepdims=True) / number
    off = x - mean
    square = jnp.sum(off * off, axis=(0, 2))
    note_ref[0:2] = mean.reshape(2, 128)
    note_ref[2:4] = square
    stats_ref[...] = jnp.broadcast_to(note_ref[...][None], stats_ref.shape)


def fetch(pairs, sems):
    copies = [pltpu.make_async_copy(src, dst, sems.at[i]) for i, (src, dst) in enumerate(pairs)]
    for copy in copies:
        copy.start()
    for copy in copies:
        copy.wait()


def begin_kernel(
    x_hbm, cache_hbm, gain_hbm, shift_hbm, w_hbm,
    raw_ref, later_ref, stats_ref, own_ref, side_ref, far_ref,
    x_ref, cache_ref, gain_ref, shift_ref, w_ref, note_ref, pieces_ref, sems,
):
    fetch(
        (
            (x_hbm, x_ref), (cache_hbm, cache_ref), (gain_hbm, gain_ref), (shift_hbm, shift_ref),
            (w_hbm, w_ref),
        ),
        sems,
    )
    for r in range(8):
        for t in range(2):
            lanes = slice(128 * t, 128 * (t + 1))
            raw_ref[r, :, lanes] = cache_ref[0, t, r]
            later_ref[r, :, lanes] = cache_ref[1, t, r]
        for t in range(4):
            raw_ref[r, :, 256 + 128 * t : 384 + 128 * t] = x_ref[t, r]
    row, me, _ = place()
    core = lax.rem(row, 2)
    for q in range(4):
        ahead = lax.rem(q + 4 - me, 4)
        for layer in range(2):
            for dt in range(3):
                for dc in range(3):
                    taps = [
                        w_ref[layer, 9 * dt + 3 * dr + dc, :, 64 * q : 64 * (q + 1)] for dr in range(3)
                    ]
                    pieces_ref[ahead, layer, dt, dc] = jnp.concatenate(taps, axis=1)
    own_ref[...] = pieces_ref[0]
    side_ref[...] = pieces_ref[1 + 2 * core]
    far_ref[...] = pieces_ref[2, core]
    note_ref[...] = jnp.zeros((8, 128), F32)
    note_ref[4:5, 0:16] = gain_ref[0:1, :]
    note_ref[5:6, 0:16] = shift_ref[0:1, :]
    put_stats(raw_ref, note_ref, stats_ref)


def shift_columns(left, centre, right):
    lane = lax.broadcasted_iota(jnp.int32, left.shape, left.ndim - 1)
    axis = left.ndim - 1
    left = jnp.where(lane == 0, 0.0, pltpu.roll(left, 1, axis))
    right = jnp.where(lane == 127, 0.0, pltpu.roll(right, 127, axis))
    return left + centre + right


def get_affine(stats_ref, affine_ref):
    stats = stats_ref[...].reshape(16, 4, 8, 128)
    number = 32 * GROUP
    means = stats[:, :, 0:2]
    mean = jnp.mean(means, axis=(0, 3), keepdims=True)
    off = means - mean
    total = jnp.sum(stats[:, :, 2:4] + number * (off * off), axis=(0, 3), keepdims=True)
    inverse = lax.rsqrt(total / (number * 16 * 128) + EPS)
    mean = jnp.broadcast_to(mean.reshape(4, 2, 1, 1), (4, 2, GROUP, 128)).reshape(4, 16, 128)
    inverse = jnp.broadcast_to(inverse.reshape(4, 2, 1, 1), (4, 2, GROUP, 128)).reshape(4, 16, 128)
    shape = (4, 16, 128)
    same = lax.broadcasted_iota(jnp.int32, shape, 1) == lax.broadcasted_iota(jnp.int32, shape, 2)
    gain = jnp.sum(jnp.where(same, stats[0, :, 4:5], 0.0), axis=2, keepdims=True)
    shift = jnp.sum(jnp.where(same, stats[0, :, 5:6], 0.0), axis=2, keepdims=True)
    affine_ref[0] = mean
    affine_ref[1] = inverse * gain
    affine_ref[2] = jnp.broadcast_to(shift, shape)


def conv_kernel(
    layer, a_ref, b_ref, c_ref, d_ref, chip_ref, next_ref, stats_ref,
    own_ref, side_ref, far_ref, side2_ref, far2_ref, o0_ref, o1_ref, o2_ref, o3_ref,
    affine_ref, slab_ref, held_ref,
):
    row, _, here = place()
    get_affine(stats_ref, affine_ref)
    upper = lax.rem(row, 2) == 0
    not_top = (row > 0).astype(F32)
    not_bottom = (row < 15).astype(F32)
    for k, ref in enumerate((a_ref, b_ref, c_ref, d_ref)):
        b = lax.bitwise_xor(here, k)
        mean = affine_ref[0, b]
        gain = affine_ref[1, b]
        shift = affine_ref[2, b]
        for r in range(10):
            for t in range(6):
                lanes = slice(128 * t, 128 * (t + 1))
                if r == 0:
                    x = jnp.where(upper, next_ref[k, :, lanes].astype(F32), chip_ref[k, :, lanes].astype(F32))
                elif r == 9:
                    x = jnp.where(upper, chip_ref[k, :, lanes].astype(F32), next_ref[k, :, lanes].astype(F32))
                elif t < 2:
                    x = ref[r - 1, :, lanes]
                else:
                    x = ref[r - 1, :, lanes].astype(F32)
                if t >= 2:
                    x = silu((x - mean) * gain + shift)
                if r == 0:
                    x = x * not_top
                if r == 9:
                    x = x * not_bottom
                slab_ref[r, b, :, lanes] = x.astype(BF16)
    core = lax.rem(row, 2)
    for dt in range(3):
        held_ref[dt, 0] = own_ref[layer, dt]
        held_ref[dt, 1] = side_ref[layer, dt]
        held_ref[dt, 2] = side2_ref[layer, dt]

    @pl.when(core == layer)
    def _():
        for dt in range(3):
            held_ref[dt, 3] = far_ref[dt]

    @pl.when(core != layer)
    def _():
        for dt in range(3):
            held_ref[dt, 3] = far2_ref[dt]

    for r in range(8):
        rows = slab_ref[r : r + 3].reshape(192, 768)
        prod = dot(held_ref[0].reshape(192, 192), rows[:, 0:512])
        prod += dot(held_ref[1].reshape(192, 192), rows[:, 128:640])
        prod += dot(held_ref[2].reshape(192, 192), rows[:, 256:768])
        prod = prod.reshape(4, 3, 16, 512)
        for t in range(4):
            lanes = slice(128 * t, 128 * (t + 1))
            part = prod[:, :, :, lanes]
            summed = shift_columns(part[:, 0], part[:, 1], part[:, 2]).astype(BF16)
            for q, o_ref in enumerate((o0_ref, o1_ref, o2_ref, o3_ref)):
                o_ref[r, :, lanes] = summed[q]


def merge_kernel(a_ref, b_ref, c_ref, bias_ref, later_ref, note1_ref, mid_ref, stats_ref, note_ref):
    bias = jnp.concatenate([bias_ref[...]] * 4, axis=1)
    for r in range(8):
        summed = a_ref[r].astype(F32) + b_ref[r].astype(F32) + c_ref[r].astype(F32)
        mid_ref[r, :, 0:256] = later_ref[r]
        mid_ref[r, :, 256:768] = (summed + bias).astype(BF16)
    note_ref[...] = note1_ref[...]
    put_stats(mid_ref, note_ref, stats_ref)


def last_kernel(x_ref, a_ref, b_ref, c_ref, bias_ref, o_ref):
    bias = bias_ref[...]
    for r in range(8):
        for t in range(4):
            lanes = slice(128 * t, 128 * (t + 1))
            branch = a_ref[r, :, lanes].astype(F32) + b_ref[r, :, lanes].astype(F32)
            branch += c_ref[r, :, lanes].astype(F32)
            o_ref[t, r] = (x_ref[t, r].astype(F32) + (branch + bias)).astype(BF16)


def sides(step):
    return [(i, (i + step) % 4) for i in range(4)] + [(4 + i, 4 + (i - step) % 4) for i in range(4)]


def add_kernel(a_ref, b_ref, o_ref):
    o_ref[...] = (a_ref[...].astype(F32) + b_ref[...].astype(F32)).astype(BF16)


def bring(own, side, other, far):
    far = lax.ppermute(far, ("core", "zh"), sides(-1))
    other = lax.ppermute(other, ("core", "zh"), sides(1))
    side = call(add_kernel, struct(side.shape), side, far)
    side = lax.ppermute(side, ("core", "zh"), sides(-1))
    return [own, other, side]


def struct(shape, dtype=BF16):
    return jax.ShapeDtypeStruct(shape, dtype)


def edge_kernel(a_ref, b_ref, c_ref, d_ref, chip_ref, next_ref):
    upper = lax.rem(lax.axis_index(ROW), 2) == 0
    towards = jnp.where(upper, 7, 0)
    for k, ref in enumerate((a_ref, b_ref, c_ref, d_ref)):
        chip_ref[k] = ref[towards]
        next_ref[k] = ref[7 - towards]


def rows_beside(blocks):
    chip, beyond = call(edge_kernel, (struct((4, 16, 768)), struct((4, 16, 768))), *blocks, flops=2 * 10**10)
    chip = lax.ppermute(chip, ROW, [(i, i ^ 1) for i in range(16)])
    pairs = [(i, i + 1) for i in range(1, 15, 2)] + [(i + 1, i) for i in range(1, 15, 2)]
    beyond = lax.ppermute(beyond, ROW, pairs)
    return [chip, beyond]


def near(x):
    return [x] + [lax.ppermute(x, NEAR, [(i, i ^ k) for i in range(4)]) for k in (1, 2, 3)]


def exchange(x, axes):
    return lax.all_to_all(x, axes, 0, 0, tiled=True)


def local(frames, cache, norm_gain, norm_shift, conv_weight, conv_bias):
    note = pltpu.VMEM((8, 128), F32)
    piece = (2, 3, 3, 16, 192)
    raw, later, stats, own, side, far = call(
        begin_kernel,
        (
            struct((8, 16, 768)), struct((8, 16, 256)), struct((64, 8, 128), F32), struct(piece),
            struct(piece), struct(piece[1:]),
        ),
        frames, cache, norm_gain, norm_shift, conv_weight.transpose(0, 2, 1, 3),
        scratch=(
            pltpu.VMEM((4, 8, 16, 128), BF16), pltpu.VMEM((2, 2, 8, 16, 128), BF16),
            pltpu.VMEM((2, 16), F32), pltpu.VMEM((2, 16), F32), pltpu.VMEM((2, 27, 16, 256), BF16),
            note, pltpu.VMEM((4,) + piece, BF16), pltpu.SemaphoreType.DMA((5,)),
        ),
        far=(0, 1, 2, 3, 4),
    )
    side = lax.ppermute(side, ("core", "zh"), sides(1))
    far = lax.ppermute(far, "zh", [(i, (i + 2) % 4) for i in range(4)])
    raw = near(raw)
    stats = exchange(stats, ROW + NEAR)
    raw = raw + rows_beside(raw)
    swap = [(0, 1), (1, 0)]
    weights = [own, side, far, lax.ppermute(side, "core", swap), lax.ppermute(far, "core", swap)]
    bias = jnp.broadcast_to(conv_bias[:, :, None], (2, 16, 128))
    note1 = jnp.pad(jnp.stack([norm_gain[1], norm_shift[1]]), ((4, 2), (0, 112)))
    scratch = (
        pltpu.VMEM((3, 4, 16, 128), F32),
        pltpu.VMEM((10, 4, 16, 768), BF16),
        pltpu.VMEM((3, 4, 3, 16, 192), BF16),
    )
    flops = 2 * 192 * 576 * 4096
    parts = (struct((8, 16, 512)),) * 4

    partial = call(
        functools.partial(conv_kernel, 0), parts, *raw, stats, *weights,
        scratch=scratch, flops=flops,
    )
    partial = bring(*partial)
    middle, stats = call(
        merge_kernel, (struct((8, 16, 768)), struct((64, 8, 128), F32)), *partial, bias[0], later, note1,
        scratch=(note,),
    )
    middle = near(middle)
    stats = exchange(stats, ROW + NEAR)
    middle = middle + rows_beside(middle)
    partial = call(
        functools.partial(conv_kernel, 1), parts, *middle, stats, *weights,
        scratch=scratch, flops=flops,
    )
    partial = bring(*partial)
    return call(last_kernel, struct((4, 8, 16, 128)), frames, *partial, bias[1])


def solution(mesh):
    fine = Mesh(mesh.devices.reshape(2, 4, 2, 4, 2, 2), ROW + CHAN)
    placed = (
        P(None, ROW, CHAN, None),
        P(None, None, ROW, CHAN, None),
        P(None, CHAN),
        P(None, CHAN),
        P(None, CHAN, None, None),
        P(None, CHAN),
    )
    return jax.shard_map(
        local, mesh=fine, in_specs=placed, out_specs=P(None, ROW, CHAN, None), check_vma=False
    )
```

```python
import functools

import jax
import jax.numpy as jnp
from jax import lax
from jax.experimental import pallas as pl
from jax.experimental.pallas import tpu as pltpu
from jax.sharding import Mesh, PartitionSpec as P

GROUP = 8
EPS = 1e-06
BF16 = jnp.bfloat16
F32 = jnp.float32

ROW = ("xh", "y", "core")
CHAN = ("zh", "zl", "xl")
NEAR = ("zl", "xl")


def dot(a, b):
    return lax.dot_general(a, b, (((1,), (0,)), ((), ())), preferred_element_type=F32)


def silu(u):
    half = 0.5 * u
    return half + half * jnp.tanh(half)


def call(kernel, outs, *args, far=(), scratch=(), flops=0):
    specs = [pl.BlockSpec(memory_space=pl.ANY if i in far else pltpu.VMEM) for i in range(len(args))]
    moved = sum(a.size * a.dtype.itemsize for a in args)
    return pl.pallas_call(
        kernel,
        out_shape=outs,
        in_specs=specs,
        out_specs=jax.tree.map(lambda _: pl.BlockSpec(memory_space=pltpu.VMEM), outs),
        scratch_shapes=list(scratch),
        compiler_params=pltpu.CompilerParams(vmem_limit_bytes=(60 if far else 40) * 1024 * 1024),
        cost_estimate=pl.CostEstimate(flops=flops, bytes_accessed=moved, transcendentals=0),
    )(*args)


def place():
    return lax.axis_index(ROW), lax.axis_index("zh"), lax.axis_index(NEAR)


def put_stats(rows_ref, note_ref, stats_ref):
    slabs = [rows_ref[:, :, 256 + 128 * t : 384 + 128 * t].astype(F32) for t in range(4)]
    x = jnp.concatenate(slabs, axis=0).reshape(32, 2, GROUP, 128)
    number = x.shape[0] * GROUP
    mean = jnp.sum(x, axis=(0, 2), keepdims=True) / number
    off = x - mean
    square = jnp.sum(off * off, axis=(0, 2))
    note_ref[0:2] = mean.reshape(2, 128)
    note_ref[2:4] = square
    stats_ref[...] = jnp.broadcast_to(note_ref[...][None], stats_ref.shape)


def fetch(pairs, sems):
    copies = [pltpu.make_async_copy(src, dst, sems.at[i]) for i, (src, dst) in enumerate(pairs)]
    for copy in copies:
        copy.start()
    for copy in copies:
        copy.wait()


def begin_kernel(
    x_hbm, cache_hbm, gain_hbm, shift_hbm, w_hbm,
    raw_ref, later_ref, stats_ref, own_ref, side_ref, far_ref,
    x_ref, cache_ref, gain_ref, shift_ref, w_ref, note_ref, pieces_ref, sems,
):
    fetch(
        (
            (x_hbm, x_ref), (cache_hbm, cache_ref), (gain_hbm, gain_ref), (shift_hbm, shift_ref),
            (w_hbm, w_ref),
        ),
        sems,
    )
    for r in range(8):
        for t in range(2):
            lanes = slice(128 * t, 128 * (t + 1))
            raw_ref[r, :, lanes] = cache_ref[0, t, r]
            later_ref[r, :, lanes] = cache_ref[1, t, r]
        for t in range(4):
            raw_ref[r, :, 256 + 128 * t : 384 + 128 * t] = x_ref[t, r]
    row, me, _ = place()
    core = lax.rem(row, 2)
    for q in range(4):
        ahead = lax.rem(q + 4 - me, 4)
        for layer in range(2):
            for dt in range(3):
                for dc in range(3):
                    taps = [
                        w_ref[layer, 9 * dt + 3 * dr + dc, :, 64 * q : 64 * (q + 1)] for dr in range(3)
                    ]
                    pieces_ref[ahead, layer, dt, dc] = jnp.concatenate(taps, axis=1)
    own_ref[...] = pieces_ref[0]
    side_ref[...] = pieces_ref[1 + 2 * core]
    far_ref[...] = pieces_ref[2, core]
    note_ref[...] = jnp.zeros((8, 128), F32)
    note_ref[4:5, 0:16] = gain_ref[0:1, :]
    note_ref[5:6, 0:16] = shift_ref[0:1, :]
    put_stats(raw_ref, note_ref, stats_ref)


def shift_columns(left, centre, right):
    lane = lax.broadcasted_iota(jnp.int32, left.shape, left.ndim - 1)
    axis = left.ndim - 1
    left = jnp.where(lane == 0, 0.0, pltpu.roll(left, 1, axis))
    right = jnp.where(lane == 127, 0.0, pltpu.roll(right, 127, axis))
    return left + centre + right


def get_affine(stats_ref, affine_ref):
    stats = stats_ref[...].reshape(16, 4, 8, 128)
    number = 32 * GROUP
    means = stats[:, :, 0:2]
    mean = jnp.mean(means, axis=(0, 3), keepdims=True)
    off = means - mean
    total = jnp.sum(stats[:, :, 2:4] + number * (off * off), axis=(0, 3), keepdims=True)
    inverse = lax.rsqrt(total / (number * 16 * 128) + EPS)
    mean = jnp.broadcast_to(mean.reshape(4, 2, 1, 1), (4, 2, GROUP, 128)).reshape(4, 16, 128)
    inverse = jnp.broadcast_to(inverse.reshape(4, 2, 1, 1), (4, 2, GROUP, 128)).reshape(4, 16, 128)
    shape = (4, 16, 128)
    same = lax.broadcasted_iota(jnp.int32, shape, 1) == lax.broadcasted_iota(jnp.int32, shape, 2)
    gain = jnp.sum(jnp.where(same, stats[0, :, 4:5], 0.0), axis=2, keepdims=True)
    shift = jnp.sum(jnp.where(same, stats[0, :, 5:6], 0.0), axis=2, keepdims=True)
    affine_ref[0] = mean
    affine_ref[1] = inverse * gain
    affine_ref[2] = jnp.broadcast_to(shift, shape)


def products(layer, w_refs, o_refs, slab_ref):
    for r in range(8):
        rows = slab_ref[r : r + 3].reshape(192, 768)
        prod = jnp.zeros((96, 512), F32)
        for dt in range(3):
            held = jnp.concatenate([ref(dt).reshape(48, 192) for ref in w_refs], axis=0)
            prod += dot(held, rows[:, 128 * dt : 128 * dt + 512])
        prod = prod.reshape(2, 3, 16, 512)
        for t in range(4):
            lanes = slice(128 * t, 128 * (t + 1))
            part = prod[:, :, :, lanes]
            summed = shift_columns(part[:, 0], part[:, 1], part[:, 2]).astype(BF16)
            for q, o_ref in enumerate(o_refs):
                o_ref[r, :, lanes] = summed[q]


def near_kernel(layer, slab_ref, own_ref, side_ref, o0_ref, o1_ref):
    w_refs = (lambda dt: own_ref[layer, dt], lambda dt: side_ref[layer, dt])
    products(layer, w_refs, (o0_ref, o1_ref), slab_ref)


def conv_kernel(
    layer, a_ref, b_ref, c_ref, d_ref, chip_ref, next_ref, stats_ref, other_ref, far_ref, far2_ref,
    o2_ref, o3_ref, slab_ref, affine_ref, held_ref,
):
    row, _, here = place()
    get_affine(stats_ref, affine_ref)
    upper = lax.rem(row, 2) == 0
    not_top = (row > 0).astype(F32)
    not_bottom = (row < 15).astype(F32)
    for k, ref in enumerate((a_ref, b_ref, c_ref, d_ref)):
        b = lax.bitwise_xor(here, k)
        mean = affine_ref[0, b]
        gain = affine_ref[1, b]
        shift = affine_ref[2, b]
        for r in range(10):
            for t in range(6):
                lanes = slice(128 * t, 128 * (t + 1))
                if r == 0:
                    x = jnp.where(upper, next_ref[k, :, lanes].astype(F32), chip_ref[k, :, lanes].astype(F32))
                elif r == 9:
                    x = jnp.where(upper, chip_ref[k, :, lanes].astype(F32), next_ref[k, :, lanes].astype(F32))
                elif t < 2:
                    x = ref[r - 1, :, lanes]
                else:
                    x = ref[r - 1, :, lanes].astype(F32)
                if t >= 2:
                    x = silu((x - mean) * gain + shift)
                if r == 0:
                    x = x * not_top
                if r == 9:
                    x = x * not_bottom
                slab_ref[r, b, :, lanes] = x.astype(BF16)
    core = lax.rem(row, 2)

    @pl.when(core == layer)
    def _():
        held_ref[...] = far_ref[...]

    @pl.when(core != layer)
    def _():
        held_ref[...] = far2_ref[...]

    w_refs = (lambda dt: other_ref[layer, dt], lambda dt: held_ref[dt])
    products(layer, w_refs, (o2_ref, o3_ref), slab_ref)


def merge_kernel(a_ref, b_ref, c_ref, bias_ref, later_ref, note1_ref, mid_ref, stats_ref, note_ref):
    bias = jnp.concatenate([bias_ref[...]] * 4, axis=1)
    for r in range(8):
        summed = a_ref[r].astype(F32) + b_ref[r].astype(F32) + c_ref[r].astype(F32)
        mid_ref[r, :, 0:256] = later_ref[r]
        mid_ref[r, :, 256:768] = (summed + bias).astype(BF16)
    note_ref[...] = note1_ref[...]
    put_stats(mid_ref, note_ref, stats_ref)


def last_kernel(x_ref, a_ref, b_ref, c_ref, bias_ref, o_ref):
    bias = bias_ref[...]
    for r in range(8):
        for t in range(4):
            lanes = slice(128 * t, 128 * (t + 1))
            branch = a_ref[r, :, lanes].astype(F32) + b_ref[r, :, lanes].astype(F32)
            branch += c_ref[r, :, lanes].astype(F32)
            o_ref[t, r] = (x_ref[t, r].astype(F32) + (branch + bias)).astype(BF16)


def sides(step):
    return [(i, (i + step) % 4) for i in range(4)] + [(4 + i, 4 + (i - step) % 4) for i in range(4)]


def add_kernel(a_ref, b_ref, o_ref):
    o_ref[...] = (a_ref[...].astype(F32) + b_ref[...].astype(F32)).astype(BF16)


def convolve(layer, inputs, own, side, far, other, far2):
    part = struct((8, 16, 512))
    flops = 2 * 96 * 576 * 4096
    other, far, slab = call(
        functools.partial(conv_kernel, layer), (part, part, struct((10, 4, 16, 768))),
        *inputs, other, far, far2,
        scratch=(pltpu.VMEM((3, 4, 16, 128), F32), pltpu.VMEM((3, 3, 16, 192), BF16)), flops=flops,
    )
    far = lax.ppermute(far, ("core", "zh"), sides(-1))
    other = lax.ppermute(other, ("core", "zh"), sides(1))
    own, side = call(
        functools.partial(near_kernel, layer), (part, part), slab, own, side, flops=flops
    )
    side = call(add_kernel, part, side, far)
    side = lax.ppermute(side, ("core", "zh"), sides(-1))
    return [own, other, side]


def struct(shape, dtype=BF16):
    return jax.ShapeDtypeStruct(shape, dtype)


def edge_kernel(a_ref, b_ref, c_ref, d_ref, chip_ref, next_ref):
    upper = lax.rem(lax.axis_index(ROW), 2) == 0
    towards = jnp.where(upper, 7, 0)
    for k, ref in enumerate((a_ref, b_ref, c_ref, d_ref)):
        chip_ref[k] = ref[towards]
        next_ref[k] = ref[7 - towards]


def rows_beside(blocks):
    chip, beyond = call(edge_kernel, (struct((4, 16, 768)), struct((4, 16, 768))), *blocks, flops=2 * 10**10)
    chip = lax.ppermute(chip, ROW, [(i, i ^ 1) for i in range(16)])
    pairs = [(i, i + 1) for i in range(1, 15, 2)] + [(i + 1, i) for i in range(1, 15, 2)]
    beyond = lax.ppermute(beyond, ROW, pairs)
    return [chip, beyond]


def near(x):
    return [x] + [lax.ppermute(x, NEAR, [(i, i ^ k) for i in range(4)]) for k in (1, 2, 3)]


def exchange(x, axes):
    return lax.all_to_all(x, axes, 0, 0, tiled=True)


def local(frames, cache, norm_gain, norm_shift, conv_weight, conv_bias):
    note = pltpu.VMEM((8, 128), F32)
    piece = (2, 3, 3, 16, 192)
    raw, later, stats, own, side, far = call(
        begin_kernel,
        (
            struct((8, 16, 768)), struct((8, 16, 256)), struct((64, 8, 128), F32), struct(piece),
            struct(piece), struct(piece[1:]),
        ),
        frames, cache, norm_gain, norm_shift, conv_weight.transpose(0, 2, 1, 3),
        scratch=(
            pltpu.VMEM((4, 8, 16, 128), BF16), pltpu.VMEM((2, 2, 8, 16, 128), BF16),
            pltpu.VMEM((2, 16), F32), pltpu.VMEM((2, 16), F32), pltpu.VMEM((2, 27, 16, 256), BF16),
            note, pltpu.VMEM((4,) + piece, BF16), pltpu.SemaphoreType.DMA((5,)),
        ),
        far=(0, 1, 2, 3, 4),
    )
    side = lax.ppermute(side, ("core", "zh"), sides(1))
    far = lax.ppermute(far, "zh", [(i, (i + 2) % 4) for i in range(4)])
    raw = near(raw)
    stats = exchange(stats, ROW + NEAR)
    raw = raw + rows_beside(raw)
    swap = [(0, 1), (1, 0)]
    weights = [own, side, far, lax.ppermute(side, "core", swap), lax.ppermute(far, "core", swap)]
    bias = jnp.broadcast_to(conv_bias[:, :, None], (2, 16, 128))
    note1 = jnp.pad(jnp.stack([norm_gain[1], norm_shift[1]]), ((4, 2), (0, 112)))
    partial = convolve(0, [*raw, stats], *weights)
    middle, stats = call(
        merge_kernel, (struct((8, 16, 768)), struct((64, 8, 128), F32)), *partial, bias[0], later, note1,
        scratch=(note,),
    )
    middle = near(middle)
    stats = exchange(stats, ROW + NEAR)
    middle = middle + rows_beside(middle)
    partial = convolve(1, [*middle, stats], *weights)
    return call(last_kernel, struct((4, 8, 16, 128)), frames, *partial, bias[1])


def solution(mesh):
    fine = Mesh(mesh.devices.reshape(2, 4, 2, 4, 2, 2), ROW + CHAN)
    placed = (
        P(None, ROW, CHAN, None),
        P(None, None, ROW, CHAN, None),
        P(None, CHAN),
        P(None, CHAN),
        P(None, CHAN, None, None),
        P(None, CHAN),
    )
    return jax.shard_map(
        local, mesh=fine, in_specs=placed, out_specs=P(None, ROW, CHAN, None), check_vma=False
    )
```

```python
import functools

import jax
import jax.numpy as jnp
from jax import lax
from jax.experimental import pallas as pl
from jax.experimental.pallas import tpu as pltpu
from jax.sharding import Mesh, PartitionSpec as P

GROUP = 8
EPS = 1e-06
BF16 = jnp.bfloat16
F32 = jnp.float32

ROW = ("xh", "y", "core")
CHAN = ("zh", "zl", "xl")
NEAR = ("zl", "xl")


def dot(a, b):
    return lax.dot_general(a, b, (((1,), (0,)), ((), ())), preferred_element_type=F32)


def silu(u):
    half = 0.5 * u
    return half + half * jnp.tanh(half)


def call(kernel, outs, *args, far=(), scratch=(), flops=0):
    specs = [pl.BlockSpec(memory_space=pl.ANY if i in far else pltpu.VMEM) for i in range(len(args))]
    moved = sum(a.size * a.dtype.itemsize for a in args)
    return pl.pallas_call(
        kernel,
        out_shape=outs,
        in_specs=specs,
        out_specs=jax.tree.map(lambda _: pl.BlockSpec(memory_space=pltpu.VMEM), outs),
        scratch_shapes=list(scratch),
        compiler_params=pltpu.CompilerParams(vmem_limit_bytes=(60 if far else 40) * 1024 * 1024),
        cost_estimate=pl.CostEstimate(flops=flops, bytes_accessed=moved, transcendentals=0),
    )(*args)


def place():
    return lax.axis_index(ROW), lax.axis_index("zh"), lax.axis_index(NEAR)


def put_stats(rows_ref, note_ref):
    slabs = [rows_ref[:, :, 256 + 128 * t : 384 + 128 * t].astype(F32) for t in range(4)]
    x = jnp.concatenate(slabs, axis=0).reshape(32, 2, GROUP, 128)
    number = x.shape[0] * GROUP
    mean = jnp.sum(x, axis=(0, 2), keepdims=True) / number
    off = x - mean
    square = jnp.sum(off * off, axis=(0, 2))
    note_ref[0:2] = mean.reshape(2, 128)
    note_ref[2:4] = square


def spread_kernel(a_ref, b_ref, stats_ref, note_ref):
    note_ref[...] = a_ref[...]
    off = a_ref[0:2] - b_ref[0:2]
    note_ref[0:2] = 0.5 * (a_ref[0:2] + b_ref[0:2])
    note_ref[2:4] = a_ref[2:4] + b_ref[2:4] + (16.0 * GROUP) * (off * off)
    stats_ref[...] = jnp.broadcast_to(note_ref[...][None], stats_ref.shape)


def fetch(pairs, sems):
    copies = [pltpu.make_async_copy(src, dst, sems.at[i]) for i, (src, dst) in enumerate(pairs)]
    for copy in copies:
        copy.start()
    for copy in copies:
        copy.wait()


def begin_kernel(
    x_hbm, cache_hbm, gain_hbm, shift_hbm, w_hbm,
    raw_ref, later_ref, note_ref, own_ref, side_ref, far_ref,
    x_ref, cache_ref, gain_ref, shift_ref, w_ref, pieces_ref, sems,
):
    fetch(
        (
            (x_hbm, x_ref), (cache_hbm, cache_ref), (gain_hbm, gain_ref), (shift_hbm, shift_ref),
            (w_hbm, w_ref),
        ),
        sems,
    )
    for r in range(8):
        for t in range(2):
            lanes = slice(128 * t, 128 * (t + 1))
            raw_ref[r, :, lanes] = cache_ref[0, t, r]
            later_ref[r, :, lanes] = cache_ref[1, t, r]
        for t in range(4):
            raw_ref[r, :, 256 + 128 * t : 384 + 128 * t] = x_ref[t, r]
    row, me, _ = place()
    core = lax.rem(row, 2)
    for q in range(4):
        ahead = lax.rem(q + 4 - me, 4)
        for layer in range(2):
            for dt in range(3):
                for dc in range(3):
                    taps = [
                        w_ref[layer, 9 * dt + 3 * dr + dc, :, 64 * q : 64 * (q + 1)] for dr in range(3)
                    ]
                    pieces_ref[ahead, layer, dt, dc] = jnp.concatenate(taps, axis=1)
    own_ref[...] = pieces_ref[0]
    side_ref[...] = pieces_ref[1 + 2 * core]
    far_ref[...] = pieces_ref[2, core]
    note_ref[...] = jnp.zeros((8, 128), F32)
    note_ref[4:5, 0:16] = gain_ref[0:1, :]
    note_ref[5:6, 0:16] = shift_ref[0:1, :]
    put_stats(raw_ref, note_ref)


def shift_columns(left, centre, right):
    lane = lax.broadcasted_iota(jnp.int32, left.shape, left.ndim - 1)
    axis = left.ndim - 1
    left = jnp.where(lane == 0, 0.0, pltpu.roll(left, 1, axis))
    right = jnp.where(lane == 127, 0.0, pltpu.roll(right, 127, axis))
    return left + centre + right


def get_affine(stats_ref, affine_ref):
    stats = stats_ref[...].reshape(8, 4, 8, 128)
    number = 64 * GROUP
    means = stats[:, :, 0:2]
    mean = jnp.mean(means, axis=(0, 3), keepdims=True)
    off = means - mean
    total = jnp.sum(stats[:, :, 2:4] + number * (off * off), axis=(0, 3), keepdims=True)
    inverse = lax.rsqrt(total / (number * 8 * 128) + EPS)
    mean = jnp.broadcast_to(mean.reshape(4, 2, 1, 1), (4, 2, GROUP, 128)).reshape(4, 16, 128)
    inverse = jnp.broadcast_to(inverse.reshape(4, 2, 1, 1), (4, 2, GROUP, 128)).reshape(4, 16, 128)
    shape = (4, 16, 128)
    same = lax.broadcasted_iota(jnp.int32, shape, 1) == lax.broadcasted_iota(jnp.int32, shape, 2)
    gain = jnp.sum(jnp.where(same, stats[0, :, 4:5], 0.0), axis=2, keepdims=True)
    shift = jnp.sum(jnp.where(same, stats[0, :, 5:6], 0.0), axis=2, keepdims=True)
    affine_ref[0] = mean
    affine_ref[1] = inverse * gain
    affine_ref[2] = jnp.broadcast_to(shift, shape)


def products(layer, w_refs, o_refs, slab_ref):
    for r in range(8):
        rows = slab_ref[r : r + 3].reshape(192, 768)
        prod = jnp.zeros((96, 512), F32)
        for dt in range(3):
            held = jnp.concatenate([ref(dt).reshape(48, 192) for ref in w_refs], axis=0)
            prod += dot(held, rows[:, 128 * dt : 128 * dt + 512])
        prod = prod.reshape(2, 3, 16, 512)
        for t in range(4):
            lanes = slice(128 * t, 128 * (t + 1))
            part = prod[:, :, :, lanes]
            summed = shift_columns(part[:, 0], part[:, 1], part[:, 2]).astype(BF16)
            for q, o_ref in enumerate(o_refs):
                o_ref[r, :, lanes] = summed[q]


def near_kernel(layer, slab_ref, own_ref, side_ref, o0_ref, o1_ref):
    w_refs = (lambda dt: own_ref[layer, dt], lambda dt: side_ref[layer, dt])
    products(layer, w_refs, (o0_ref, o1_ref), slab_ref)


def conv_kernel(
    layer, a_ref, b_ref, c_ref, d_ref, chip_ref, next_ref, stats_ref, other_ref, far_ref, far2_ref,
    o2_ref, o3_ref, slab_ref, affine_ref, held_ref,
):
    row, _, here = place()
    get_affine(stats_ref, affine_ref)
    upper = lax.rem(row, 2) == 0
    not_top = (row > 0).astype(F32)
    not_bottom = (row < 15).astype(F32)
    for k, ref in enumerate((a_ref, b_ref, c_ref, d_ref)):
        b = lax.bitwise_xor(here, k)
        mean = affine_ref[0, b]
        gain = affine_ref[1, b]
        shift = affine_ref[2, b]
        for r in range(10):
            for t in range(6):
                lanes = slice(128 * t, 128 * (t + 1))
                if r == 0:
                    x = jnp.where(upper, next_ref[k, :, lanes].astype(F32), chip_ref[k, :, lanes].astype(F32))
                elif r == 9:
                    x = jnp.where(upper, chip_ref[k, :, lanes].astype(F32), next_ref[k, :, lanes].astype(F32))
                elif t < 2:
                    x = ref[r - 1, :, lanes]
                else:
                    x = ref[r - 1, :, lanes].astype(F32)
                if t >= 2:
                    x = silu((x - mean) * gain + shift)
                if r == 0:
                    x = x * not_top
                if r == 9:
                    x = x * not_bottom
                slab_ref[r, b, :, lanes] = x.astype(BF16)
    core = lax.rem(row, 2)

    @pl.when(core == layer)
    def _():
        held_ref[...] = far_ref[...]

    @pl.when(core != layer)
    def _():
        held_ref[...] = far2_ref[...]

    w_refs = (lambda dt: other_ref[layer, dt], lambda dt: held_ref[dt])
    products(layer, w_refs, (o2_ref, o3_ref), slab_ref)


def merge_kernel(a_ref, b_ref, c_ref, bias_ref, later_ref, note1_ref, mid_ref, note_ref):
    bias = jnp.concatenate([bias_ref[...]] * 4, axis=1)
    for r in range(8):
        summed = a_ref[r].astype(F32) + b_ref[r].astype(F32) + c_ref[r].astype(F32)
        mid_ref[r, :, 0:256] = later_ref[r]
        mid_ref[r, :, 256:768] = (summed + bias).astype(BF16)
    note_ref[...] = note1_ref[...]
    put_stats(mid_ref, note_ref)


def last_kernel(x_ref, a_ref, b_ref, c_ref, bias_ref, o_ref):
    bias = bias_ref[...]
    for r in range(8):
        for t in range(4):
            lanes = slice(128 * t, 128 * (t + 1))
            branch = a_ref[r, :, lanes].astype(F32) + b_ref[r, :, lanes].astype(F32)
            branch += c_ref[r, :, lanes].astype(F32)
            o_ref[t, r] = (x_ref[t, r].astype(F32) + (branch + bias)).astype(BF16)


def all_stats(note):
    other = lax.ppermute(note, "core", [(0, 1), (1, 0)])
    return exchange(call(spread_kernel, struct((32, 8, 128), F32), note, other,
                         scratch=(pltpu.VMEM((8, 128), F32),)), ("xh", "y") + NEAR)


def sides(step):
    return [(i, (i + step) % 4) for i in range(4)] + [(4 + i, 4 + (i - step) % 4) for i in range(4)]


def add_kernel(a_ref, b_ref, o_ref):
    o_ref[...] = (a_ref[...].astype(F32) + b_ref[...].astype(F32)).astype(BF16)


def convolve(layer, inputs, own, side, far, other, far2):
    part = struct((8, 16, 512))
    flops = 2 * 96 * 576 * 4096
    other, far, slab = call(
        functools.partial(conv_kernel, layer), (part, part, struct((10, 4, 16, 768))),
        *inputs, other, far, far2,
        scratch=(pltpu.VMEM((3, 4, 16, 128), F32), pltpu.VMEM((3, 3, 16, 192), BF16)), flops=flops,
    )
    far = lax.ppermute(far, ("core", "zh"), sides(-1))
    other = lax.ppermute(other, ("core", "zh"), sides(1))
    own, side = call(
        functools.partial(near_kernel, layer), (part, part), slab, own, side, flops=flops
    )
    side = call(add_kernel, part, side, far)
    side = lax.ppermute(side, ("core", "zh"), sides(-1))
    return [own, other, side]


def struct(shape, dtype=BF16):
    return jax.ShapeDtypeStruct(shape, dtype)


def edge_kernel(a_ref, b_ref, c_ref, d_ref, chip_ref, next_ref):
    upper = lax.rem(lax.axis_index(ROW), 2) == 0
    towards = jnp.where(upper, 7, 0)
    for k, ref in enumerate((a_ref, b_ref, c_ref, d_ref)):
        chip_ref[k] = ref[towards]
        next_ref[k] = ref[7 - towards]


def rows_beside(blocks):
    chip, beyond = call(edge_kernel, (struct((4, 16, 768)), struct((4, 16, 768))), *blocks, flops=2 * 10**10)
    chip = lax.ppermute(chip, ROW, [(i, i ^ 1) for i in range(16)])
    pairs = [(i, i + 1) for i in range(1, 15, 2)] + [(i + 1, i) for i in range(1, 15, 2)]
    beyond = lax.ppermute(beyond, ROW, pairs)
    return [chip, beyond]


def near(x):
    return [x] + [lax.ppermute(x, NEAR, [(i, i ^ k) for i in range(4)]) for k in (1, 2, 3)]


def exchange(x, axes):
    return lax.all_to_all(x, axes, 0, 0, tiled=True)


def local(frames, cache, norm_gain, norm_shift, conv_weight, conv_bias):
    note = struct((8, 128), F32)
    piece = (2, 3, 3, 16, 192)
    raw, later, stats, own, side, far = call(
        begin_kernel,
        (
            struct((8, 16, 768)), struct((8, 16, 256)), note, struct(piece),
            struct(piece), struct(piece[1:]),
        ),
        frames, cache, norm_gain, norm_shift, conv_weight.transpose(0, 2, 1, 3),
        scratch=(
            pltpu.VMEM((4, 8, 16, 128), BF16), pltpu.VMEM((2, 2, 8, 16, 128), BF16),
            pltpu.VMEM((2, 16), F32), pltpu.VMEM((2, 16), F32), pltpu.VMEM((2, 27, 16, 256), BF16),
            pltpu.VMEM((4,) + piece, BF16), pltpu.SemaphoreType.DMA((5,)),
        ),
        far=(0, 1, 2, 3, 4),
    )
    side = lax.ppermute(side, ("core", "zh"), sides(1))
    far = lax.ppermute(far, "zh", [(i, (i + 2) % 4) for i in range(4)])
    raw = near(raw)
    stats = all_stats(stats)
    raw = raw + rows_beside(raw)
    swap = [(0, 1), (1, 0)]
    weights = [own, side, far, lax.ppermute(side, "core", swap), lax.ppermute(far, "core", swap)]
    bias = jnp.broadcast_to(conv_bias[:, :, None], (2, 16, 128))
    note1 = jnp.pad(jnp.stack([norm_gain[1], norm_shift[1]]), ((4, 2), (0, 112)))
    partial = convolve(0, [*raw, stats], *weights)
    middle, stats = call(
        merge_kernel, (struct((8, 16, 768)), note), *partial, bias[0], later, note1
    )
    middle = near(middle)
    stats = all_stats(stats)
    middle = middle + rows_beside(middle)
    partial = convolve(1, [*middle, stats], *weights)
    return call(last_kernel, struct((4, 8, 16, 128)), frames, *partial, bias[1])


def solution(mesh):
    fine = Mesh(mesh.devices.reshape(2, 4, 2, 4, 2, 2), ROW + CHAN)
    placed = (
        P(None, ROW, CHAN, None),
        P(None, None, ROW, CHAN, None),
        P(None, CHAN),
        P(None, CHAN),
        P(None, CHAN, None, None),
        P(None, CHAN),
    )
    return jax.shard_map(
        local, mesh=fine, in_specs=placed, out_specs=P(None, ROW, CHAN, None), check_vma=False
    )
```

```python
import functools

import jax
import jax.numpy as jnp
from jax import lax
from jax.experimental import pallas as pl
from jax.experimental.pallas import tpu as pltpu
from jax.sharding import Mesh, PartitionSpec as P

GROUP = 8
EPS = 1e-06
BF16 = jnp.bfloat16
F32 = jnp.float32

ROW = ("xh", "y", "core")
CHAN = ("zh", "zl", "xl")
NEAR = ("zl", "xl")


def dot(a, b):
    return lax.dot_general(a, b, (((1,), (0,)), ((), ())), preferred_element_type=F32)


def silu(u):
    half = 0.5 * u
    return half + half * jnp.tanh(half)


def call(kernel, outs, *args, far=(), scratch=(), flops=0):
    specs = [pl.BlockSpec(memory_space=pl.ANY if i in far else pltpu.VMEM) for i in range(len(args))]
    moved = sum(a.size * a.dtype.itemsize for a in args)
    return pl.pallas_call(
        kernel,
        out_shape=outs,
        in_specs=specs,
        out_specs=jax.tree.map(lambda _: pl.BlockSpec(memory_space=pltpu.VMEM), outs),
        scratch_shapes=list(scratch),
        compiler_params=pltpu.CompilerParams(vmem_limit_bytes=(60 if far else 40) * 1024 * 1024),
        cost_estimate=pl.CostEstimate(flops=flops, bytes_accessed=moved, transcendentals=0),
    )(*args)


def place():
    return lax.axis_index(ROW), lax.axis_index("zh"), lax.axis_index(NEAR)


def put_stats(rows_ref, note_ref, stats_ref):
    slabs = [rows_ref[:, :, 256 + 128 * t : 384 + 128 * t].astype(F32) for t in range(4)]
    x = jnp.concatenate(slabs, axis=0).reshape(32, 2, GROUP, 128)
    number = x.shape[0] * GROUP
    mean = jnp.sum(x, axis=(0, 2), keepdims=True) / number
    off = x - mean
    square = jnp.sum(off * off, axis=(0, 2))
    note_ref[0:2] = mean.reshape(2, 128)
    note_ref[2:4] = square
    stats_ref[...] = jnp.broadcast_to(note_ref[...][None], stats_ref.shape)


def fetch(pairs, sems):
    copies = [pltpu.make_async_copy(src, dst, sems.at[i]) for i, (src, dst) in enumerate(pairs)]
    for copy in copies:
        copy.start()
    for copy in copies:
        copy.wait()


def begin_kernel(
    x_hbm, cache_hbm, gain_hbm, shift_hbm, w_hbm,
    raw_ref, later_ref, stats_ref, own_ref, side_ref, far_ref,
    x_ref, cache_ref, gain_ref, shift_ref, w_ref, note_ref, pieces_ref, sems,
):
    fetch(
        (
            (x_hbm, x_ref), (cache_hbm, cache_ref), (gain_hbm, gain_ref), (shift_hbm, shift_ref),
            (w_hbm, w_ref),
        ),
        sems,
    )
    for r in range(8):
        for t in range(2):
            lanes = slice(128 * t, 128 * (t + 1))
            raw_ref[r, :, lanes] = cache_ref[0, t, r]
            later_ref[r, :, lanes] = cache_ref[1, t, r]
        for t in range(4):
            raw_ref[r, :, 256 + 128 * t : 384 + 128 * t] = x_ref[t, r]
    row, me, _ = place()
    core = lax.rem(row, 2)
    for q in range(4):
        ahead = lax.rem(q + 4 - me, 4)
        for layer in range(2):
            for dt in range(3):
                for dc in range(3):
                    taps = [
                        w_ref[layer, 9 * dt + 3 * dr + dc, :, 64 * q : 64 * (q + 1)] for dr in range(3)
                    ]
                    pieces_ref[ahead, layer, dt, dc] = jnp.concatenate(taps, axis=1)
    own_ref[...] = pieces_ref[0]
    side_ref[...] = pieces_ref[1 + 2 * core]
    far_ref[...] = pieces_ref[2, core]
    note_ref[...] = jnp.zeros((8, 128), F32)
    note_ref[4:5, 0:16] = gain_ref[0:1, :]
    note_ref[5:6, 0:16] = shift_ref[0:1, :]
    put_stats(raw_ref, note_ref, stats_ref)


def shift_columns(left, centre, right):
    lane = lax.broadcasted_iota(jnp.int32, left.shape, left.ndim - 1)
    axis = left.ndim - 1
    left = jnp.where(lane == 0, 0.0, pltpu.roll(left, 1, axis))
    right = jnp.where(lane == 127, 0.0, pltpu.roll(right, 127, axis))
    return left + centre + right


def get_affine(stats_ref, affine_ref):
    stats = stats_ref[...].reshape(16, 4, 8, 128)
    number = 32 * GROUP
    means = stats[:, :, 0:2]
    mean = jnp.mean(means, axis=(0, 3), keepdims=True)
    off = means - mean
    total = jnp.sum(stats[:, :, 2:4] + number * (off * off), axis=(0, 3), keepdims=True)
    inverse = lax.rsqrt(total / (number * 16 * 128) + EPS)
    mean = jnp.broadcast_to(mean.reshape(4, 2, 1, 1), (4, 2, GROUP, 128)).reshape(4, 16, 128)
    inverse = jnp.broadcast_to(inverse.reshape(4, 2, 1, 1), (4, 2, GROUP, 128)).reshape(4, 16, 128)
    shape = (4, 16, 128)
    same = lax.broadcasted_iota(jnp.int32, shape, 1) == lax.broadcasted_iota(jnp.int32, shape, 2)
    gain = jnp.sum(jnp.where(same, stats[0, :, 4:5], 0.0), axis=2, keepdims=True)
    shift = jnp.sum(jnp.where(same, stats[0, :, 5:6], 0.0), axis=2, keepdims=True)
    affine_ref[0] = mean
    affine_ref[1] = inverse * gain
    affine_ref[2] = jnp.broadcast_to(shift, shape)


def window(slab_ref, edge_ref, r):
    if r == 0:
        rows = jnp.concatenate([edge_ref[0:1], slab_ref[0:2]], axis=0)
    elif r == 7:
        rows = jnp.concatenate([slab_ref[6:8], edge_ref[1:2]], axis=0)
    else:
        rows = slab_ref[r - 1 : r + 2]
    return rows.reshape(192, 768)


def products(which, w_refs, o_refs, slab_ref, edge_ref):
    for r in which:
        rows = window(slab_ref, edge_ref, r)
        prod = jnp.zeros((96, 512), F32)
        for dt in range(3):
            held = jnp.concatenate([ref(dt).reshape(48, 192) for ref in w_refs], axis=0)
            prod += dot(held, rows[:, 128 * dt : 128 * dt + 512])
        prod = prod.reshape(2, 3, 16, 512)
        for t in range(4):
            lanes = slice(128 * t, 128 * (t + 1))
            part = prod[:, :, :, lanes]
            summed = shift_columns(part[:, 0], part[:, 1], part[:, 2]).astype(BF16)
            for q, o_ref in enumerate(o_refs):
                o_ref[r, :, lanes] = summed[q]


def near_kernel(layer, slab_ref, edge_ref, own_ref, side_ref, o0_ref, o1_ref):
    w_refs = (lambda dt: own_ref[layer, dt], lambda dt: side_ref[layer, dt])
    products(range(8), w_refs, (o0_ref, o1_ref), slab_ref, edge_ref)


def hold(layer, far_ref, far2_ref, held_ref):
    core = lax.rem(lax.axis_index(ROW), 2)

    @pl.when(core == layer)
    def _():
        held_ref[...] = far_ref[...]

    @pl.when(core != layer)
    def _():
        held_ref[...] = far2_ref[...]


def inner_kernel(
    layer, a_ref, b_ref, c_ref, d_ref, stats_ref, other_ref, far_ref, far2_ref,
    o2_ref, o3_ref, slab_ref, affine_ref, held_ref,
):
    here = lax.axis_index(NEAR)
    get_affine(stats_ref, affine_ref)
    for k, ref in enumerate((a_ref, b_ref, c_ref, d_ref)):
        b = lax.bitwise_xor(here, k)
        mean = affine_ref[0, b]
        gain = affine_ref[1, b]
        shift = affine_ref[2, b]
        for r in range(8):
            slab_ref[r, b, :, 0:256] = ref[r, :, 0:256]
            for t in range(2, 6):
                lanes = slice(128 * t, 128 * (t + 1))
                x = silu((ref[r, :, lanes].astype(F32) - mean) * gain + shift)
                slab_ref[r, b, :, lanes] = x.astype(BF16)
    hold(layer, far_ref, far2_ref, held_ref)
    w_refs = (lambda dt: other_ref[layer, dt], lambda dt: held_ref[dt])
    for o_ref in (o2_ref, o3_ref):
        o_ref[0] = jnp.zeros((16, 512), BF16)
        o_ref[7] = jnp.zeros((16, 512), BF16)
    products(range(1, 7), w_refs, (o2_ref, o3_ref), slab_ref, None)


def outer_kernel(
    layer, chip_ref, next_ref, affine_ref, slab_ref, other_ref, far_ref, far2_ref, i2_ref, i3_ref,
    o2_ref, o3_ref, edge_ref, held_ref,
):
    row, _, here = place()
    upper = lax.rem(row, 2) == 0
    inside = ((row > 0).astype(F32), (row < 15).astype(F32))
    for k in range(4):
        b = lax.bitwise_xor(here, k)
        mean = affine_ref[0, b]
        gain = affine_ref[1, b]
        shift = affine_ref[2, b]
        for t in range(6):
            lanes = slice(128 * t, 128 * (t + 1))
            chip = chip_ref[k, :, lanes].astype(F32)
            beyond = next_ref[k, :, lanes].astype(F32)
            for end, x in enumerate((jnp.where(upper, beyond, chip), jnp.where(upper, chip, beyond))):
                if t >= 2:
                    x = silu((x - mean) * gain + shift)
                edge_ref[end, b, :, lanes] = (x * inside[end]).astype(BF16)
    hold(layer, far_ref, far2_ref, held_ref)
    w_refs = (lambda dt: other_ref[layer, dt], lambda dt: held_ref[dt])
    for i_ref, o_ref in ((i2_ref, o2_ref), (i3_ref, o3_ref)):
        o_ref[1:7] = i_ref[1:7]
    products((0, 7), w_refs, (o2_ref, o3_ref), slab_ref, edge_ref)


def merge_kernel(a_ref, b_ref, c_ref, bias_ref, later_ref, note1_ref, mid_ref, stats_ref, note_ref):
    bias = jnp.concatenate([bias_ref[...]] * 4, axis=1)
    for r in range(8):
        summed = a_ref[r].astype(F32) + b_ref[r].astype(F32) + c_ref[r].astype(F32)
        mid_ref[r, :, 0:256] = later_ref[r]
        mid_ref[r, :, 256:768] = (summed + bias).astype(BF16)
    note_ref[...] = note1_ref[...]
    put_stats(mid_ref, note_ref, stats_ref)


def last_kernel(x_ref, a_ref, b_ref, c_ref, bias_ref, o_ref):
    bias = bias_ref[...]
    for r in range(8):
        for t in range(4):
            lanes = slice(128 * t, 128 * (t + 1))
            branch = a_ref[r, :, lanes].astype(F32) + b_ref[r, :, lanes].astype(F32)
            branch += c_ref[r, :, lanes].astype(F32)
            o_ref[t, r] = (x_ref[t, r].astype(F32) + (branch + bias)).astype(BF16)


def sides(step):
    return [(i, (i + step) % 4) for i in range(4)] + [(4 + i, 4 + (i - step) % 4) for i in range(4)]


def add_kernel(a_ref, b_ref, o_ref):
    o_ref[...] = (a_ref[...].astype(F32) + b_ref[...].astype(F32)).astype(BF16)


def convolve(layer, inputs, own, side, far, other, far2):
    part = struct((8, 16, 512))
    flops = 2 * 96 * 576 * 4096
    held = pltpu.VMEM((3, 3, 16, 192), BF16)
    *blocks, chip, beyond, stats = inputs
    other_part, far_part, slab, affine = call(
        functools.partial(inner_kernel, layer),
        (part, part, struct((8, 4, 16, 768)), struct((3, 4, 16, 128), F32)),
        *blocks, stats, other, far, far2,
        scratch=(held,), flops=flops,
    )
    other, far, edge = call(
        functools.partial(outer_kernel, layer), (part, part, struct((2, 4, 16, 768))),
        chip, beyond, affine, slab, other, far, far2, other_part, far_part,
        scratch=(held,), flops=flops // 4,
    )
    far = lax.ppermute(far, ("core", "zh"), sides(-1))
    other = lax.ppermute(other, ("core", "zh"), sides(1))
    own, side = call(
        functools.partial(near_kernel, layer), (part, part), slab, edge, own, side, flops=flops
    )
    side = call(add_kernel, part, side, far)
    side = lax.ppermute(side, ("core", "zh"), sides(-1))
    return [own, other, side]


def struct(shape, dtype=BF16):
    return jax.ShapeDtypeStruct(shape, dtype)


def edge_kernel(a_ref, b_ref, c_ref, d_ref, chip_ref, next_ref):
    upper = lax.rem(lax.axis_index(ROW), 2) == 0
    towards = jnp.where(upper, 7, 0)
    for k, ref in enumerate((a_ref, b_ref, c_ref, d_ref)):
        chip_ref[k] = ref[towards]
        next_ref[k] = ref[7 - towards]


def rows_beside(blocks):
    chip, beyond = call(edge_kernel, (struct((4, 16, 768)), struct((4, 16, 768))), *blocks, flops=2 * 10**10)
    chip = lax.ppermute(chip, ROW, [(i, i ^ 1) for i in range(16)])
    pairs = [(i, i + 1) for i in range(1, 15, 2)] + [(i + 1, i) for i in range(1, 15, 2)]
    beyond = lax.ppermute(beyond, ROW, pairs)
    return [chip, beyond]


def near(x):
    return [x] + [lax.ppermute(x, NEAR, [(i, i ^ k) for i in range(4)]) for k in (1, 2, 3)]


def exchange(x, axes):
    return lax.all_to_all(x, axes, 0, 0, tiled=True)


def local(frames, cache, norm_gain, norm_shift, conv_weight, conv_bias):
    note = pltpu.VMEM((8, 128), F32)
    piece = (2, 3, 3, 16, 192)
    raw, later, stats, own, side, far = call(
        begin_kernel,
        (
            struct((8, 16, 768)), struct((8, 16, 256)), struct((64, 8, 128), F32), struct(piece),
            struct(piece), struct(piece[1:]),
        ),
        frames, cache, norm_gain, norm_shift, conv_weight.transpose(0, 2, 1, 3),
        scratch=(
            pltpu.VMEM((4, 8, 16, 128), BF16), pltpu.VMEM((2, 2, 8, 16, 128), BF16),
            pltpu.VMEM((2, 16), F32), pltpu.VMEM((2, 16), F32), pltpu.VMEM((2, 27, 16, 256), BF16),
            note, pltpu.VMEM((4,) + piece, BF16), pltpu.SemaphoreType.DMA((5,)),
        ),
        far=(0, 1, 2, 3, 4),
    )
    side = lax.ppermute(side, ("core", "zh"), sides(1))
    far = lax.ppermute(far, "zh", [(i, (i + 2) % 4) for i in range(4)])
    raw = near(raw)
    stats = exchange(stats, ROW + NEAR)
    raw = raw + rows_beside(raw)
    swap = [(0, 1), (1, 0)]
    weights = [own, side, far, lax.ppermute(side, "core", swap), lax.ppermute(far, "core", swap)]
    bias = jnp.broadcast_to(conv_bias[:, :, None], (2, 16, 128))
    note1 = jnp.pad(jnp.stack([norm_gain[1], norm_shift[1]]), ((4, 2), (0, 112)))
    partial = convolve(0, [*raw, stats], *weights)
    middle, stats = call(
        merge_kernel, (struct((8, 16, 768)), struct((64, 8, 128), F32)), *partial, bias[0], later, note1,
        scratch=(note,),
    )
    middle = near(middle)
    stats = exchange(stats, ROW + NEAR)
    middle = middle + rows_beside(middle)
    partial = convolve(1, [*middle, stats], *weights)
    return call(last_kernel, struct((4, 8, 16, 128)), frames, *partial, bias[1])


def solution(mesh):
    fine = Mesh(mesh.devices.reshape(2, 4, 2, 4, 2, 2), ROW + CHAN)
    placed = (
        P(None, ROW, CHAN, None),
        P(None, None, ROW, CHAN, None),
        P(None, CHAN),
        P(None, CHAN),
        P(None, CHAN, None, None),
        P(None, CHAN),
    )
    return jax.shard_map(
        local, mesh=fine, in_specs=placed, out_specs=P(None, ROW, CHAN, None), check_vma=False
    )
```

```python
import functools

import jax
import jax.numpy as jnp
from jax import lax
from jax.experimental import pallas as pl
from jax.experimental.pallas import tpu as pltpu
from jax.sharding import Mesh, PartitionSpec as P

GROUP = 8
EPS = 1e-06
BF16 = jnp.bfloat16
F32 = jnp.float32

ROW = ("xh", "y", "core")
CHAN = ("zh", "zl", "xl")
NEAR = ("zl", "xl")


def dot(a, b):
    return lax.dot_general(a, b, (((1,), (0,)), ((), ())), preferred_element_type=F32)


def silu(u):
    half = 0.5 * u
    return half + half * jnp.tanh(half)


def call(kernel, outs, *args, far=(), scratch=(), flops=0):
    specs = [pl.BlockSpec(memory_space=pl.ANY if i in far else pltpu.VMEM) for i in range(len(args))]
    moved = sum(a.size * a.dtype.itemsize for a in args)
    return pl.pallas_call(
        kernel,
        out_shape=outs,
        in_specs=specs,
        out_specs=jax.tree.map(lambda _: pl.BlockSpec(memory_space=pltpu.VMEM), outs),
        scratch_shapes=list(scratch),
        compiler_params=pltpu.CompilerParams(vmem_limit_bytes=(60 if far else 40) * 1024 * 1024),
        cost_estimate=pl.CostEstimate(flops=flops, bytes_accessed=moved, transcendentals=0),
    )(*args)


def place():
    return lax.axis_index(ROW), lax.axis_index("zh"), lax.axis_index(NEAR)


def put_stats(rows_ref, note_ref, stats_ref):
    slabs = [rows_ref[:, :, 256 + 128 * t : 384 + 128 * t].astype(F32) for t in range(4)]
    x = jnp.concatenate(slabs, axis=0).reshape(32, 2, GROUP, 128)
    number = x.shape[0] * GROUP
    mean = jnp.sum(x, axis=(0, 2), keepdims=True) / number
    off = x - mean
    square = jnp.sum(off * off, axis=(0, 2))
    note_ref[0:2] = mean.reshape(2, 128)
    note_ref[2:4] = square
    stats_ref[...] = jnp.broadcast_to(note_ref[...][None], stats_ref.shape)


def fetch(pairs, sems):
    copies = [pltpu.make_async_copy(src, dst, sems.at[i]) for i, (src, dst) in enumerate(pairs)]
    for copy in copies:
        copy.start()
    for copy in copies:
        copy.wait()


def begin_kernel(
    x_hbm, cache_hbm, gain_hbm, shift_hbm, w_hbm,
    raw_ref, later_ref, stats_ref, own_ref, side_ref, far_ref,
    x_ref, cache_ref, gain_ref, shift_ref, w_ref, note_ref, pieces_ref, sems,
):
    fetch(
        (
            (x_hbm, x_ref), (cache_hbm, cache_ref), (gain_hbm, gain_ref), (shift_hbm, shift_ref),
            (w_hbm, w_ref),
        ),
        sems,
    )
    for r in range(8):
        for t in range(2):
            lanes = slice(128 * t, 128 * (t + 1))
            raw_ref[r, :, lanes] = cache_ref[0, t, r]
            later_ref[r, :, lanes] = cache_ref[1, t, r]
        for t in range(4):
            raw_ref[r, :, 256 + 128 * t : 384 + 128 * t] = x_ref[t, r]
    row, me, _ = place()
    core = lax.rem(row, 2)
    for q in range(4):
        ahead = lax.rem(q + 4 - me, 4)
        for layer in range(2):
            for dt in range(3):
                for dc in range(3):
                    taps = [
                        w_ref[layer, 9 * dt + 3 * dr + dc, :, 64 * q : 64 * (q + 1)] for dr in range(3)
                    ]
                    pieces_ref[ahead, layer, dt, dc] = jnp.concatenate(taps, axis=1)
    own_ref[...] = pieces_ref[0]
    side_ref[...] = pieces_ref[1 + 2 * core]
    far_ref[...] = pieces_ref[2, core]
    note_ref[...] = jnp.zeros((8, 128), F32)
    note_ref[4:5, 0:16] = gain_ref[0:1, :]
    note_ref[5:6, 0:16] = shift_ref[0:1, :]
    put_stats(raw_ref, note_ref, stats_ref)


def shift_columns(left, centre, right):
    lane = lax.broadcasted_iota(jnp.int32, left.shape, left.ndim - 1)
    axis = left.ndim - 1
    left = jnp.where(lane == 0, 0.0, pltpu.roll(left, 1, axis))
    right = jnp.where(lane == 127, 0.0, pltpu.roll(right, 127, axis))
    return left + centre + right


def get_affine(stats_ref, affine_ref):
    stats = stats_ref[...].reshape(16, 4, 8, 128)
    number = 32 * GROUP
    means = stats[:, :, 0:2]
    mean = jnp.mean(means, axis=(0, 3), keepdims=True)
    off = means - mean
    total = jnp.sum(stats[:, :, 2:4] + number * (off * off), axis=(0, 3), keepdims=True)
    inverse = lax.rsqrt(total / (number * 16 * 128) + EPS)
    mean = jnp.broadcast_to(mean.reshape(4, 2, 1, 1), (4, 2, GROUP, 128)).reshape(4, 16, 128)
    inverse = jnp.broadcast_to(inverse.reshape(4, 2, 1, 1), (4, 2, GROUP, 128)).reshape(4, 16, 128)
    shape = (4, 16, 128)
    same = lax.broadcasted_iota(jnp.int32, shape, 1) == lax.broadcasted_iota(jnp.int32, shape, 2)
    gain = jnp.sum(jnp.where(same, stats[0, :, 4:5], 0.0), axis=2, keepdims=True)
    shift = jnp.sum(jnp.where(same, stats[0, :, 5:6], 0.0), axis=2, keepdims=True)
    affine_ref[0] = mean
    affine_ref[1] = inverse * gain
    affine_ref[2] = jnp.broadcast_to(shift, shape)


def products(layer, w_refs, o_refs, slab_ref):
    count = len(w_refs)
    for r in range(8):
        rows = slab_ref[r : r + 3].reshape(192, 768)
        prod = jnp.zeros((48 * count, 512), F32)
        for dt in range(3):
            held = [ref(dt).reshape(48, 192) for ref in w_refs]
            held = held[0] if count == 1 else jnp.concatenate(held, axis=0)
            prod += dot(held, rows[:, 128 * dt : 128 * dt + 512])
        prod = prod.reshape(count, 3, 16, 512)
        for t in range(4):
            lanes = slice(128 * t, 128 * (t + 1))
            part = prod[:, :, :, lanes]
            summed = shift_columns(part[:, 0], part[:, 1], part[:, 2]).astype(BF16)
            for q, o_ref in enumerate(o_refs):
                o_ref[r, :, lanes] = summed[q]


def near_kernel(layer, slab_ref, own_ref, side_ref, other_ref, o0_ref, o1_ref, o2_ref):
    w_refs = tuple(functools.partial(lambda ref, dt: ref[layer, dt], ref) for ref in (own_ref, side_ref, other_ref))
    products(layer, w_refs, (o0_ref, o1_ref, o2_ref), slab_ref)


def conv_kernel(
    layer, a_ref, b_ref, c_ref, d_ref, chip_ref, next_ref, stats_ref, far_ref, far2_ref,
    o3_ref, slab_ref, affine_ref, held_ref,
):
    row, _, here = place()
    get_affine(stats_ref, affine_ref)
    upper = lax.rem(row, 2) == 0
    not_top = (row > 0).astype(F32)
    not_bottom = (row < 15).astype(F32)
    for k, ref in enumerate((a_ref, b_ref, c_ref, d_ref)):
        b = lax.bitwise_xor(here, k)
        mean = affine_ref[0, b]
        gain = affine_ref[1, b]
        shift = affine_ref[2, b]
        for r in range(10):
            for t in range(6):
                lanes = slice(128 * t, 128 * (t + 1))
                if r == 0:
                    x = jnp.where(upper, next_ref[k, :, lanes].astype(F32), chip_ref[k, :, lanes].astype(F32))
                elif r == 9:
                    x = jnp.where(upper, chip_ref[k, :, lanes].astype(F32), next_ref[k, :, lanes].astype(F32))
                elif t < 2:
                    x = ref[r - 1, :, lanes]
                else:
                    x = ref[r - 1, :, lanes].astype(F32)
                if t >= 2:
                    x = silu((x - mean) * gain + shift)
                if r == 0:
                    x = x * not_top
                if r == 9:
                    x = x * not_bottom
                slab_ref[r, b, :, lanes] = x.astype(BF16)
    core = lax.rem(row, 2)

    @pl.when(core == layer)
    def _():
        held_ref[...] = far_ref[...]

    @pl.when(core != layer)
    def _():
        held_ref[...] = far2_ref[...]

    products(layer, (lambda dt: held_ref[dt],), (o3_ref,), slab_ref)


def merge_kernel(a_ref, b_ref, c_ref, bias_ref, later_ref, note1_ref, mid_ref, stats_ref, note_ref):
    bias = jnp.concatenate([bias_ref[...]] * 4, axis=1)
    for r in range(8):
        summed = a_ref[r].astype(F32) + b_ref[r].astype(F32) + c_ref[r].astype(F32)
        mid_ref[r, :, 0:256] = later_ref[r]
        mid_ref[r, :, 256:768] = (summed + bias).astype(BF16)
    note_ref[...] = note1_ref[...]
    put_stats(mid_ref, note_ref, stats_ref)


def last_kernel(x_ref, a_ref, b_ref, c_ref, bias_ref, o_ref):
    bias = bias_ref[...]
    for r in range(8):
        for t in range(4):
            lanes = slice(128 * t, 128 * (t + 1))
            branch = a_ref[r, :, lanes].astype(F32) + b_ref[r, :, lanes].astype(F32)
            branch += c_ref[r, :, lanes].astype(F32)
            o_ref[t, r] = (x_ref[t, r].astype(F32) + (branch + bias)).astype(BF16)


def sides(step):
    return [(i, (i + step) % 4) for i in range(4)] + [(4 + i, 4 + (i - step) % 4) for i in range(4)]


def add_kernel(a_ref, b_ref, o_ref):
    o_ref[...] = (a_ref[...].astype(F32) + b_ref[...].astype(F32)).astype(BF16)


def convolve(layer, inputs, own, side, far, other, far2):
    part = struct((8, 16, 512))
    flops = 2 * 48 * 576 * 4096
    far, slab = call(
        functools.partial(conv_kernel, layer), (part, struct((10, 4, 16, 768))), *inputs, far, far2,
        scratch=(pltpu.VMEM((3, 4, 16, 128), F32), pltpu.VMEM((3, 3, 16, 192), BF16)), flops=flops,
    )
    far = lax.ppermute(far, ("core", "zh"), sides(-1))
    own, side, other = call(
        functools.partial(near_kernel, layer), (part,) * 3, slab, own, side, other, flops=3 * flops
    )
    other = lax.ppermute(other, ("core", "zh"), sides(1))
    side = call(add_kernel, part, side, far)
    side = lax.ppermute(side, ("core", "zh"), sides(-1))
    return [own, other, side]


def struct(shape, dtype=BF16):
    return jax.ShapeDtypeStruct(shape, dtype)


def edge_kernel(a_ref, b_ref, c_ref, d_ref, chip_ref, next_ref):
    upper = lax.rem(lax.axis_index(ROW), 2) == 0
    towards = jnp.where(upper, 7, 0)
    for k, ref in enumerate((a_ref, b_ref, c_ref, d_ref)):
        chip_ref[k] = ref[towards]
        next_ref[k] = ref[7 - towards]


def rows_beside(blocks):
    chip, beyond = call(edge_kernel, (struct((4, 16, 768)), struct((4, 16, 768))), *blocks, flops=2 * 10**10)
    chip = lax.ppermute(chip, ROW, [(i, i ^ 1) for i in range(16)])
    pairs = [(i, i + 1) for i in range(1, 15, 2)] + [(i + 1, i) for i in range(1, 15, 2)]
    beyond = lax.ppermute(beyond, ROW, pairs)
    return [chip, beyond]


def near(x):
    return [x] + [lax.ppermute(x, NEAR, [(i, i ^ k) for i in range(4)]) for k in (1, 2, 3)]


def exchange(x, axes):
    return lax.all_to_all(x, axes, 0, 0, tiled=True)


def local(frames, cache, norm_gain, norm_shift, conv_weight, conv_bias):
    note = pltpu.VMEM((8, 128), F32)
    piece = (2, 3, 3, 16, 192)
    raw, later, stats, own, side, far = call(
        begin_kernel,
        (
            struct((8, 16, 768)), struct((8, 16, 256)), struct((64, 8, 128), F32), struct(piece),
            struct(piece), struct(piece[1:]),
        ),
        frames, cache, norm_gain, norm_shift, conv_weight.transpose(0, 2, 1, 3),
        scratch=(
            pltpu.VMEM((4, 8, 16, 128), BF16), pltpu.VMEM((2, 2, 8, 16, 128), BF16),
            pltpu.VMEM((2, 16), F32), pltpu.VMEM((2, 16), F32), pltpu.VMEM((2, 27, 16, 256), BF16),
            note, pltpu.VMEM((4,) + piece, BF16), pltpu.SemaphoreType.DMA((5,)),
        ),
        far=(0, 1, 2, 3, 4),
    )
    side = lax.ppermute(side, ("core", "zh"), sides(1))
    far = lax.ppermute(far, "zh", [(i, (i + 2) % 4) for i in range(4)])
    raw = near(raw)
    stats = exchange(stats, ROW + NEAR)
    raw = raw + rows_beside(raw)
    swap = [(0, 1), (1, 0)]
    weights = [own, side, far, lax.ppermute(side, "core", swap), lax.ppermute(far, "core", swap)]
    bias = jnp.broadcast_to(conv_bias[:, :, None], (2, 16, 128))
    note1 = jnp.pad(jnp.stack([norm_gain[1], norm_shift[1]]), ((4, 2), (0, 112)))
    partial = convolve(0, [*raw, stats], *weights)
    middle, stats = call(
        merge_kernel, (struct((8, 16, 768)), struct((64, 8, 128), F32)), *partial, bias[0], later, note1,
        scratch=(note,),
    )
    middle = near(middle)
    stats = exchange(stats, ROW + NEAR)
    middle = middle + rows_beside(middle)
    partial = convolve(1, [*middle, stats], *weights)
    return call(last_kernel, struct((4, 8, 16, 128)), frames, *partial, bias[1])


def solution(mesh):
    fine = Mesh(mesh.devices.reshape(2, 4, 2, 4, 2, 2), ROW + CHAN)
    placed = (
        P(None, ROW, CHAN, None),
        P(None, None, ROW, CHAN, None),
        P(None, CHAN),
        P(None, CHAN),
        P(None, CHAN, None, None),
        P(None, CHAN),
    )
    return jax.shard_map(
        local, mesh=fine, in_specs=placed, out_specs=P(None, ROW, CHAN, None), check_vma=False
    )
```

```python
import functools

import jax
import jax.numpy as jnp
from jax import lax
from jax.experimental import pallas as pl
from jax.experimental.pallas import tpu as pltpu
from jax.sharding import Mesh, PartitionSpec as P

GROUP = 8
EPS = 1e-06
BF16 = jnp.bfloat16
F32 = jnp.float32

ROW = ("xh", "y", "core")
CHAN = ("zh", "zl", "xl")
NEAR = ("zl", "xl")


def dot(a, b):
    return lax.dot_general(a, b, (((1,), (0,)), ((), ())), preferred_element_type=F32)


def silu(u):
    half = 0.5 * u
    return half + half * jnp.tanh(half)


def call(kernel, outs, *args, far=(), scratch=(), flops=0):
    specs = [pl.BlockSpec(memory_space=pl.ANY if i in far else pltpu.VMEM) for i in range(len(args))]
    moved = sum(a.size * a.dtype.itemsize for a in args)
    return pl.pallas_call(
        kernel,
        out_shape=outs,
        in_specs=specs,
        out_specs=jax.tree.map(lambda _: pl.BlockSpec(memory_space=pltpu.VMEM), outs),
        scratch_shapes=list(scratch),
        compiler_params=pltpu.CompilerParams(vmem_limit_bytes=(60 if far else 40) * 1024 * 1024),
        cost_estimate=pl.CostEstimate(flops=flops, bytes_accessed=moved, transcendentals=0),
    )(*args)


def place():
    return lax.axis_index(ROW), lax.axis_index("zh"), lax.axis_index(NEAR)


def put_stats(rows_ref, note_ref):
    slabs = [rows_ref[:, :, 256 + 128 * t : 384 + 128 * t].astype(F32) for t in range(4)]
    x = jnp.concatenate(slabs, axis=0).reshape(32, 2, GROUP, 128)
    mean = jnp.sum(x, axis=(0, 2), keepdims=True) / (32 * GROUP)
    off = x - mean
    note_ref[0:2] = mean.reshape(2, 128)
    note_ref[2:4] = jnp.sum(off * off, axis=(0, 2))


def fetch(pairs, sems):
    copies = [pltpu.make_async_copy(src, dst, sems.at[i]) for i, (src, dst) in enumerate(pairs)]
    for copy in copies:
        copy.start()
    for copy in copies:
        copy.wait()


def begin_kernel(
    x_hbm, cache_hbm, gain_hbm, shift_hbm, w_hbm,
    raw_ref, later_ref, stats_ref, own_ref, side_ref, far_ref,
    x_ref, cache_ref, gain_ref, shift_ref, w_ref, note_ref, pieces_ref, sems,
):
    fetch(
        (
            (x_hbm, x_ref), (cache_hbm, cache_ref), (gain_hbm, gain_ref), (shift_hbm, shift_ref),
            (w_hbm, w_ref),
        ),
        sems,
    )
    for r in range(8):
        for t in range(2):
            lanes = slice(128 * t, 128 * (t + 1))
            raw_ref[r, :, lanes] = cache_ref[0, t, r]
            later_ref[r, :, lanes] = cache_ref[1, t, r]
        for t in range(4):
            raw_ref[r, :, 256 + 128 * t : 384 + 128 * t] = x_ref[t, r]
    row, me, _ = place()
    core = lax.rem(row, 2)
    for q in range(4):
        ahead = lax.rem(q + 4 - me, 4)
        for layer in range(2):
            for dt in range(3):
                for dc in range(3):
                    taps = [
                        w_ref[layer, 9 * dt + 3 * dr + dc, :, 64 * q : 64 * (q + 1)] for dr in range(3)
                    ]
                    pieces_ref[ahead, layer, dt, dc] = jnp.concatenate(taps, axis=1)
    own_ref[...] = pieces_ref[0]
    side_ref[...] = pieces_ref[1 + 2 * core]
    far_ref[...] = pieces_ref[2, core]
    note_ref[...] = jnp.zeros((8, 128), F32)
    for layer in range(2):
        note_ref[4 + layer : 5 + layer, 0:16] = gain_ref[layer : layer + 1, :]
        note_ref[6 + layer : 7 + layer, 0:16] = shift_ref[layer : layer + 1, :]
    put_stats(raw_ref, note_ref)
    stats_ref[...] = jnp.broadcast_to(note_ref[...][None], stats_ref.shape)


def shift_columns(left, centre, right):
    lane = lax.broadcasted_iota(jnp.int32, left.shape, left.ndim - 1)
    axis = left.ndim - 1
    left = jnp.where(lane == 0, 0.0, pltpu.roll(left, 1, axis))
    right = jnp.where(lane == 127, 0.0, pltpu.roll(right, 127, axis))
    return left + centre + right


def get_affine(layer, stats_ref, notes_ref, affine_ref):
    stats = stats_ref[...]
    stats = stats.reshape(16, 4, stats.shape[1], 128)
    number = 32 * GROUP
    means = stats[:, :, 0:2]
    mean = jnp.mean(means, axis=(0, 3), keepdims=True)
    off = means - mean
    total = jnp.sum(stats[:, :, 2:4] + number * (off * off), axis=(0, 3), keepdims=True)
    inverse = lax.rsqrt(total / (number * 16 * 128) + EPS)
    mean = jnp.broadcast_to(mean.reshape(4, 2, 1, 1), (4, 2, GROUP, 128)).reshape(4, 16, 128)
    inverse = jnp.broadcast_to(inverse.reshape(4, 2, 1, 1), (4, 2, GROUP, 128)).reshape(4, 16, 128)
    shape = (4, 16, 128)
    same = lax.broadcasted_iota(jnp.int32, shape, 1) == lax.broadcasted_iota(jnp.int32, shape, 2)
    gain = jnp.sum(jnp.where(same, notes_ref[0:4, 4 + layer : 5 + layer], 0.0), axis=2, keepdims=True)
    shift = jnp.sum(jnp.where(same, notes_ref[0:4, 6 + layer : 7 + layer], 0.0), axis=2, keepdims=True)
    affine_ref[0] = mean
    affine_ref[1] = inverse * gain
    affine_ref[2] = jnp.broadcast_to(shift, shape)


def products(layer, w_refs, o_refs, slab_ref):
    for r in range(8):
        rows = slab_ref[r : r + 3].reshape(192, 768)
        prod = jnp.zeros((96, 512), F32)
        for dt in range(3):
            held = jnp.concatenate([ref(dt).reshape(48, 192) for ref in w_refs], axis=0)
            prod += dot(held, rows[:, 128 * dt : 128 * dt + 512])
        prod = prod.reshape(2, 3, 16, 512)
        for t in range(4):
            lanes = slice(128 * t, 128 * (t + 1))
            part = prod[:, :, :, lanes]
            summed = shift_columns(part[:, 0], part[:, 1], part[:, 2]).astype(BF16)
            for q, o_ref in enumerate(o_refs):
                o_ref[r, :, lanes] = summed[q]


def near_kernel(layer, slab_ref, own_ref, side_ref, o0_ref, o1_ref):
    w_refs = (lambda dt: own_ref[layer, dt], lambda dt: side_ref[layer, dt])
    products(layer, w_refs, (o0_ref, o1_ref), slab_ref)


def conv_kernel(
    layer, a_ref, b_ref, c_ref, d_ref, chip_ref, next_ref, stats_ref, notes_ref, other_ref, far_ref, far2_ref,
    o2_ref, o3_ref, slab_ref, affine_ref, held_ref,
):
    row, _, here = place()
    get_affine(layer, stats_ref, notes_ref, affine_ref)
    upper = lax.rem(row, 2) == 0
    not_top = (row > 0).astype(F32)
    not_bottom = (row < 15).astype(F32)
    for k, ref in enumerate((a_ref, b_ref, c_ref, d_ref)):
        b = lax.bitwise_xor(here, k)
        mean = affine_ref[0, b]
        gain = affine_ref[1, b]
        shift = affine_ref[2, b]
        for r in range(10):
            for t in range(6):
                lanes = slice(128 * t, 128 * (t + 1))
                if r == 0:
                    x = jnp.where(upper, next_ref[k, :, lanes].astype(F32), chip_ref[k, :, lanes].astype(F32))
                elif r == 9:
                    x = jnp.where(upper, chip_ref[k, :, lanes].astype(F32), next_ref[k, :, lanes].astype(F32))
                elif t < 2:
                    x = ref[r - 1, :, lanes]
                else:
                    x = ref[r - 1, :, lanes].astype(F32)
                if t >= 2:
                    x = silu((x - mean) * gain + shift)
                if r == 0:
                    x = x * not_top
                if r == 9:
                    x = x * not_bottom
                slab_ref[r, b, :, lanes] = x.astype(BF16)
    core = lax.rem(row, 2)

    @pl.when(core == layer)
    def _():
        held_ref[...] = far_ref[...]

    @pl.when(core != layer)
    def _():
        held_ref[...] = far2_ref[...]

    w_refs = (lambda dt: other_ref[layer, dt], lambda dt: held_ref[dt])
    products(layer, w_refs, (o2_ref, o3_ref), slab_ref)


def merge_kernel(a_ref, b_ref, c_ref, bias_ref, later_ref, mid_ref, stats_ref, note_ref):
    bias = jnp.concatenate([bias_ref[...]] * 4, axis=1)
    for r in range(8):
        summed = a_ref[r].astype(F32) + b_ref[r].astype(F32) + c_ref[r].astype(F32)
        mid_ref[r, :, 0:256] = later_ref[r]
        mid_ref[r, :, 256:768] = (summed + bias).astype(BF16)
    put_stats(mid_ref, note_ref)
    stats_ref[...] = jnp.broadcast_to(note_ref[...][None], stats_ref.shape)


def last_kernel(x_ref, a_ref, b_ref, c_ref, bias_ref, o_ref):
    bias = bias_ref[...]
    for r in range(8):
        for t in range(4):
            lanes = slice(128 * t, 128 * (t + 1))
            branch = a_ref[r, :, lanes].astype(F32) + b_ref[r, :, lanes].astype(F32)
            branch += c_ref[r, :, lanes].astype(F32)
            o_ref[t, r] = (x_ref[t, r].astype(F32) + (branch + bias)).astype(BF16)


def sides(step):
    return [(i, (i + step) % 4) for i in range(4)] + [(4 + i, 4 + (i - step) % 4) for i in range(4)]


def add_kernel(a_ref, b_ref, o_ref):
    o_ref[...] = (a_ref[...].astype(F32) + b_ref[...].astype(F32)).astype(BF16)


def convolve(layer, inputs, own, side, far, other, far2):
    part = struct((8, 16, 512))
    flops = 2 * 96 * 576 * 4096
    other, far, slab = call(
        functools.partial(conv_kernel, layer), (part, part, struct((10, 4, 16, 768))),
        *inputs, other, far, far2,
        scratch=(pltpu.VMEM((3, 4, 16, 128), F32), pltpu.VMEM((3, 3, 16, 192), BF16)), flops=flops,
    )
    far = lax.ppermute(far, ("core", "zh"), sides(-1))
    other = lax.ppermute(other, ("core", "zh"), sides(1))
    own, side = call(
        functools.partial(near_kernel, layer), (part, part), slab, own, side, flops=flops
    )
    side = call(add_kernel, part, side, far)
    side = lax.ppermute(side, ("core", "zh"), sides(-1))
    return [own, other, side]


def struct(shape, dtype=BF16):
    return jax.ShapeDtypeStruct(shape, dtype)


def edge_kernel(a_ref, b_ref, c_ref, d_ref, chip_ref, next_ref):
    upper = lax.rem(lax.axis_index(ROW), 2) == 0
    towards = jnp.where(upper, 7, 0)
    for k, ref in enumerate((a_ref, b_ref, c_ref, d_ref)):
        chip_ref[k] = ref[towards]
        next_ref[k] = ref[7 - towards]


def rows_beside(blocks):
    chip, beyond = call(edge_kernel, (struct((4, 16, 768)), struct((4, 16, 768))), *blocks, flops=2 * 10**10)
    chip = lax.ppermute(chip, ROW, [(i, i ^ 1) for i in range(16)])
    pairs = [(i, i + 1) for i in range(1, 15, 2)] + [(i + 1, i) for i in range(1, 15, 2)]
    beyond = lax.ppermute(beyond, ROW, pairs)
    return [chip, beyond]


def near(x):
    return [x] + [lax.ppermute(x, NEAR, [(i, i ^ k) for i in range(4)]) for k in (1, 2, 3)]


def exchange(x, axes):
    return lax.all_to_all(x, axes, 0, 0, tiled=True)


def local(frames, cache, norm_gain, norm_shift, conv_weight, conv_bias):
    note = pltpu.VMEM((8, 128), F32)
    piece = (2, 3, 3, 16, 192)
    raw, later, stats, own, side, far = call(
        begin_kernel,
        (
            struct((8, 16, 768)), struct((8, 16, 256)), struct((64, 8, 128), F32), struct(piece),
            struct(piece), struct(piece[1:]),
        ),
        frames, cache, norm_gain, norm_shift, conv_weight.transpose(0, 2, 1, 3),
        scratch=(
            pltpu.VMEM((4, 8, 16, 128), BF16), pltpu.VMEM((2, 2, 8, 16, 128), BF16),
            pltpu.VMEM((2, 16), F32), pltpu.VMEM((2, 16), F32), pltpu.VMEM((2, 27, 16, 256), BF16),
            note, pltpu.VMEM((4,) + piece, BF16), pltpu.SemaphoreType.DMA((5,)),
        ),
        far=(0, 1, 2, 3, 4),
    )
    side = lax.ppermute(side, ("core", "zh"), sides(1))
    far = lax.ppermute(far, "zh", [(i, (i + 2) % 4) for i in range(4)])
    raw = near(raw)
    stats = exchange(stats, ROW + NEAR)
    raw = raw + rows_beside(raw)
    swap = [(0, 1), (1, 0)]
    weights = [own, side, far, lax.ppermute(side, "core", swap), lax.ppermute(far, "core", swap)]
    bias = jnp.broadcast_to(conv_bias[:, :, None], (2, 16, 128))
    notes = stats
    partial = convolve(0, [*raw, stats, notes], *weights)
    middle, stats = call(
        merge_kernel, (struct((8, 16, 768)), struct((64, 4, 128), F32)), *partial, bias[0], later,
        scratch=(pltpu.VMEM((4, 128), F32),),
    )
    middle = near(middle)
    stats = exchange(stats, ROW + NEAR)
    middle = middle + rows_beside(middle)
    partial = convolve(1, [*middle, stats, notes], *weights)
    return call(last_kernel, struct((4, 8, 16, 128)), frames, *partial, bias[1])


def solution(mesh):
    fine = Mesh(mesh.devices.reshape(2, 4, 2, 4, 2, 2), ROW + CHAN)
    placed = (
        P(None, ROW, CHAN, None),
        P(None, None, ROW, CHAN, None),
        P(None, CHAN),
        P(None, CHAN),
        P(None, CHAN, None, None),
        P(None, CHAN),
    )
    return jax.shard_map(
        local, mesh=fine, in_specs=placed, out_specs=P(None, ROW, CHAN, None), check_vma=False
    )
```

```python
import functools

import jax
import jax.numpy as jnp
from jax import lax
from jax.experimental import pallas as pl
from jax.experimental.pallas import tpu as pltpu
from jax.sharding import Mesh, PartitionSpec as P

GROUP = 8
EPS = 1e-06
BF16 = jnp.bfloat16
F32 = jnp.float32

ROW = ("xh", "y", "core")
CHAN = ("zh", "zl", "xl")
NEAR = ("zl", "xl")


def dot(a, b):
    return lax.dot_general(a, b, (((1,), (0,)), ((), ())), preferred_element_type=F32)


def silu(u):
    half = 0.5 * u
    return half + half * jnp.tanh(half)


def call(kernel, outs, *args, far=(), scratch=(), flops=0):
    specs = [pl.BlockSpec(memory_space=pl.ANY if i in far else pltpu.VMEM) for i in range(len(args))]
    moved = sum(a.size * a.dtype.itemsize for a in args)
    return pl.pallas_call(
        kernel,
        out_shape=outs,
        in_specs=specs,
        out_specs=jax.tree.map(lambda _: pl.BlockSpec(memory_space=pltpu.VMEM), outs),
        scratch_shapes=list(scratch),
        compiler_params=pltpu.CompilerParams(vmem_limit_bytes=(60 if far else 40) * 1024 * 1024),
        cost_estimate=pl.CostEstimate(flops=flops, bytes_accessed=moved, transcendentals=0),
    )(*args)


def place():
    return lax.axis_index(ROW), lax.axis_index("zh"), lax.axis_index(NEAR)


def put_stats(rows_ref, note_ref):
    slabs = [rows_ref[:, :, 256 + 128 * t : 384 + 128 * t].astype(F32) for t in range(4)]
    x = jnp.concatenate(slabs, axis=0).reshape(32, 2, GROUP, 128)
    mean = jnp.sum(x, axis=(0, 2), keepdims=True) / (32 * GROUP)
    off = x - mean
    note_ref[0:2] = mean.reshape(2, 128)
    note_ref[2:4] = jnp.sum(off * off, axis=(0, 2))


def fetch(pairs, sems):
    copies = [pltpu.make_async_copy(src, dst, sems.at[i]) for i, (src, dst) in enumerate(pairs)]
    for copy in copies:
        copy.start()
    for copy in copies:
        copy.wait()


def begin_kernel(
    x_hbm, cache_hbm, gain_hbm, shift_hbm, w_hbm,
    raw_ref, later_ref, stats_ref, own_ref, side_ref, far_ref,
    x_ref, cache_ref, gain_ref, shift_ref, w_ref, note_ref, pieces_ref, sems,
):
    fetch(
        (
            (x_hbm, x_ref), (cache_hbm, cache_ref), (gain_hbm, gain_ref), (shift_hbm, shift_ref),
            (w_hbm, w_ref),
        ),
        sems,
    )
    for r in range(8):
        for t in range(2):
            lanes = slice(128 * t, 128 * (t + 1))
            raw_ref[r, :, lanes] = cache_ref[0, t, r]
            later_ref[r, :, lanes] = cache_ref[1, t, r]
        for t in range(4):
            raw_ref[r, :, 256 + 128 * t : 384 + 128 * t] = x_ref[t, r]
    row, me, _ = place()
    core = lax.rem(row, 2)
    for q in range(4):
        ahead = lax.rem(q + 4 - me, 4)
        for layer in range(2):
            for dt in range(3):
                for dc in range(3):
                    taps = [
                        w_ref[layer, 9 * dt + 3 * dr + dc, :, 64 * q : 64 * (q + 1)] for dr in range(3)
                    ]
                    pieces_ref[ahead, layer, dt, dc] = jnp.concatenate(taps, axis=1)
    own_ref[...] = pieces_ref[0]
    side_ref[...] = pieces_ref[1 + 2 * core]
    far_ref[...] = pieces_ref[2, core]
    note_ref[...] = jnp.zeros((8, 128), F32)
    for layer in range(2):
        note_ref[4 + layer : 5 + layer, 0:16] = gain_ref[layer : layer + 1, :]
        note_ref[6 + layer : 7 + layer, 0:16] = shift_ref[layer : layer + 1, :]
    put_stats(raw_ref, note_ref)
    stats_ref[...] = jnp.broadcast_to(note_ref[...][None], stats_ref.shape)


def shift_columns(left, centre, right):
    lane = lax.broadcasted_iota(jnp.int32, left.shape, left.ndim - 1)
    axis = left.ndim - 1
    left = jnp.where(lane == 0, 0.0, pltpu.roll(left, 1, axis))
    right = jnp.where(lane == 127, 0.0, pltpu.roll(right, 127, axis))
    return left + centre + right


def get_affine(layer, stats_ref, notes_ref, affine_ref):
    stats = stats_ref[...]
    stats = stats.reshape(16, 4, stats.shape[1], 128)
    number = 32 * GROUP
    means = stats[:, :, 0:2]
    mean = jnp.mean(means, axis=(0, 3), keepdims=True)
    off = means - mean
    total = jnp.sum(stats[:, :, 2:4] + number * (off * off), axis=(0, 3), keepdims=True)
    inverse = lax.rsqrt(total / (number * 16 * 128) + EPS)
    mean = jnp.broadcast_to(mean.reshape(4, 2, 1, 1), (4, 2, GROUP, 128)).reshape(4, 16, 128)
    inverse = jnp.broadcast_to(inverse.reshape(4, 2, 1, 1), (4, 2, GROUP, 128)).reshape(4, 16, 128)
    shape = (4, 16, 128)
    same = lax.broadcasted_iota(jnp.int32, shape, 1) == lax.broadcasted_iota(jnp.int32, shape, 2)
    gain = jnp.sum(jnp.where(same, notes_ref[0:4, 4 + layer : 5 + layer], 0.0), axis=2, keepdims=True)
    shift = jnp.sum(jnp.where(same, notes_ref[0:4, 6 + layer : 7 + layer], 0.0), axis=2, keepdims=True)
    affine_ref[0] = mean
    affine_ref[1] = inverse * gain
    affine_ref[2] = jnp.broadcast_to(shift, shape)


def products(layer, w_refs, o_refs, slab_ref):
    for r in range(8):
        rows = slab_ref[r : r + 3].reshape(192, 768)
        prod = jnp.zeros((96, 512), F32)
        for dt in range(3):
            held = jnp.concatenate([ref(dt).reshape(48, 192) for ref in w_refs], axis=0)
            prod += dot(held, rows[:, 128 * dt : 128 * dt + 512])
        prod = prod.reshape(2, 3, 16, 512)
        for t in range(4):
            lanes = slice(128 * t, 128 * (t + 1))
            part = prod[:, :, :, lanes]
            summed = shift_columns(part[:, 0], part[:, 1], part[:, 2]).astype(BF16)
            for q, o_ref in enumerate(o_refs):
                o_ref[r, :, lanes] = summed[q]


def near_kernel(layer, slab_ref, own_ref, side_ref, o0_ref, o1_ref):
    w_refs = (lambda dt: own_ref[layer, dt], lambda dt: side_ref[layer, dt])
    products(layer, w_refs, (o0_ref, o1_ref), slab_ref)


def conv_kernel(
    layer, a_ref, b_ref, c_ref, d_ref, next_ref, chip_ref, stats_ref, notes_ref, other_ref, far_ref, far2_ref,
    o2_ref, o3_ref, slab_ref, affine_ref, held_ref,
):
    row, _, here = place()
    get_affine(layer, stats_ref, notes_ref, affine_ref)
    upper = lax.rem(row, 2) == 0
    not_top = (row > 0).astype(F32)
    not_bottom = (row < 15).astype(F32)
    for k, ref in enumerate((a_ref, b_ref, c_ref, d_ref)):
        b = lax.bitwise_xor(here, k)
        mean = affine_ref[0, b]
        gain = affine_ref[1, b]
        shift = affine_ref[2, b]
        for r in range(10):
            for t in range(6):
                lanes = slice(128 * t, 128 * (t + 1))
                if r == 0:
                    x = jnp.where(upper, next_ref[k, :, lanes].astype(F32), chip_ref[k, :, lanes].astype(F32))
                elif r == 9:
                    x = jnp.where(upper, chip_ref[k, :, lanes].astype(F32), next_ref[k, :, lanes].astype(F32))
                elif t < 2:
                    x = ref[r - 1, :, lanes]
                else:
                    x = ref[r - 1, :, lanes].astype(F32)
                if t >= 2:
                    x = silu((x - mean) * gain + shift)
                if r == 0:
                    x = x * not_top
                if r == 9:
                    x = x * not_bottom
                slab_ref[r, b, :, lanes] = x.astype(BF16)
    core = lax.rem(row, 2)

    @pl.when(core == layer)
    def _():
        held_ref[...] = far_ref[...]

    @pl.when(core != layer)
    def _():
        held_ref[...] = far2_ref[...]

    w_refs = (lambda dt: other_ref[layer, dt], lambda dt: held_ref[dt])
    products(layer, w_refs, (o2_ref, o3_ref), slab_ref)


def merge_kernel(a_ref, b_ref, c_ref, bias_ref, later_ref, mid_ref, stats_ref, note_ref):
    bias = jnp.concatenate([bias_ref[...]] * 4, axis=1)
    for r in range(8):
        summed = a_ref[r].astype(F32) + b_ref[r].astype(F32) + c_ref[r].astype(F32)
        mid_ref[r, :, 0:256] = later_ref[r]
        mid_ref[r, :, 256:768] = (summed + bias).astype(BF16)
    put_stats(mid_ref, note_ref)
    stats_ref[...] = jnp.broadcast_to(note_ref[...][None], stats_ref.shape)


def last_kernel(x_ref, a_ref, b_ref, c_ref, bias_ref, o_ref):
    bias = bias_ref[...]
    for r in range(8):
        for t in range(4):
            lanes = slice(128 * t, 128 * (t + 1))
            branch = a_ref[r, :, lanes].astype(F32) + b_ref[r, :, lanes].astype(F32)
            branch += c_ref[r, :, lanes].astype(F32)
            o_ref[t, r] = (x_ref[t, r].astype(F32) + (branch + bias)).astype(BF16)


def sides(step):
    return [(i, (i + step) % 4) for i in range(4)] + [(4 + i, 4 + (i - step) % 4) for i in range(4)]


def add_kernel(a_ref, b_ref, o_ref):
    o_ref[...] = (a_ref[...].astype(F32) + b_ref[...].astype(F32)).astype(BF16)


def convolve(layer, inputs, own, side, far, other, far2):
    part = struct((8, 16, 512))
    flops = 2 * 96 * 576 * 4096
    other, far, slab = call(
        functools.partial(conv_kernel, layer), (part, part, struct((10, 4, 16, 768))),
        *inputs, other, far, far2,
        scratch=(pltpu.VMEM((3, 4, 16, 128), F32), pltpu.VMEM((3, 3, 16, 192), BF16)), flops=flops,
    )
    far = lax.ppermute(far, ("core", "zh"), sides(-1))
    other = lax.ppermute(other, ("core", "zh"), sides(1))
    own, side = call(
        functools.partial(near_kernel, layer), (part, part), slab, own, side, flops=flops
    )
    side = call(add_kernel, part, side, far)
    side = lax.ppermute(side, ("core", "zh"), sides(-1))
    return [own, other, side]


def struct(shape, dtype=BF16):
    return jax.ShapeDtypeStruct(shape, dtype)


def edge_kernel(a_ref, b_ref, c_ref, d_ref, chip_ref, next_ref):
    upper = lax.rem(lax.axis_index(ROW), 2) == 0
    towards = jnp.where(upper, 7, 0)
    for k, ref in enumerate((a_ref, b_ref, c_ref, d_ref)):
        chip_ref[k] = ref[towards]
        next_ref[k] = ref[7 - towards]


def rows_beside(blocks):
    chip, beyond = call(edge_kernel, (struct((4, 16, 768)), struct((4, 16, 768))), *blocks, flops=2 * 10**10)
    pairs = [(i, i + 1) for i in range(1, 15, 2)] + [(i + 1, i) for i in range(1, 15, 2)]
    beyond = lax.ppermute(beyond, ROW, pairs)
    chip = lax.ppermute(chip, ROW, [(i, i ^ 1) for i in range(16)])
    return [beyond, chip]


def near(x):
    return [x] + [lax.ppermute(x, NEAR, [(i, i ^ k) for i in range(4)]) for k in (1, 2, 3)]


def exchange(x, axes):
    return lax.all_to_all(x, axes, 0, 0, tiled=True)


def local(frames, cache, norm_gain, norm_shift, conv_weight, conv_bias):
    note = pltpu.VMEM((8, 128), F32)
    piece = (2, 3, 3, 16, 192)
    raw, later, stats, own, side, far = call(
        begin_kernel,
        (
            struct((8, 16, 768)), struct((8, 16, 256)), struct((64, 8, 128), F32), struct(piece),
            struct(piece), struct(piece[1:]),
        ),
        frames, cache, norm_gain, norm_shift, conv_weight.transpose(0, 2, 1, 3),
        scratch=(
            pltpu.VMEM((4, 8, 16, 128), BF16), pltpu.VMEM((2, 2, 8, 16, 128), BF16),
            pltpu.VMEM((2, 16), F32), pltpu.VMEM((2, 16), F32), pltpu.VMEM((2, 27, 16, 256), BF16),
            note, pltpu.VMEM((4,) + piece, BF16), pltpu.SemaphoreType.DMA((5,)),
        ),
        far=(0, 1, 2, 3, 4),
    )
    side = lax.ppermute(side, ("core", "zh"), sides(1))
    far = lax.ppermute(far, "zh", [(i, (i + 2) % 4) for i in range(4)])
    raw = near(raw)
    stats = exchange(stats, ROW + NEAR)
    raw = raw + rows_beside(raw)
    swap = [(0, 1), (1, 0)]
    weights = [own, side, far, lax.ppermute(side, "core", swap), lax.ppermute(far, "core", swap)]
    bias = jnp.broadcast_to(conv_bias[:, :, None], (2, 16, 128))
    notes = stats
    partial = convolve(0, [*raw, stats, notes], *weights)
    middle, stats = call(
        merge_kernel, (struct((8, 16, 768)), struct((64, 4, 128), F32)), *partial, bias[0], later,
        scratch=(pltpu.VMEM((4, 128), F32),),
    )
    middle = near(middle)
    stats = exchange(stats, ROW + NEAR)
    middle = middle + rows_beside(middle)
    partial = convolve(1, [*middle, stats, notes], *weights)
    return call(last_kernel, struct((4, 8, 16, 128)), frames, *partial, bias[1])


def solution(mesh):
    fine = Mesh(mesh.devices.reshape(2, 4, 2, 4, 2, 2), ROW + CHAN)
    placed = (
        P(None, ROW, CHAN, None),
        P(None, None, ROW, CHAN, None),
        P(None, CHAN),
        P(None, CHAN),
        P(None, CHAN, None, None),
        P(None, CHAN),
    )
    return jax.shard_map(
        local, mesh=fine, in_specs=placed, out_specs=P(None, ROW, CHAN, None), check_vma=False
    )
```

```python
import functools

import jax
import jax.numpy as jnp
from jax import lax
from jax.experimental import pallas as pl
from jax.experimental.pallas import tpu as pltpu
from jax.sharding import Mesh, PartitionSpec as P

GROUP = 8
EPS = 1e-06
BF16 = jnp.bfloat16
F32 = jnp.float32

ROW = ("xh", "y", "core")
CHAN = ("zh", "zl", "xl")
NEAR = ("zl", "xl")


def dot(a, b):
    return lax.dot_general(a, b, (((1,), (0,)), ((), ())), preferred_element_type=F32)


def silu(u):
    half = 0.5 * u
    return half + half * jnp.tanh(half)


def call(kernel, outs, *args, far=(), scratch=(), flops=0):
    specs = [pl.BlockSpec(memory_space=pl.ANY if i in far else pltpu.VMEM) for i in range(len(args))]
    moved = sum(a.size * a.dtype.itemsize for a in args)
    return pl.pallas_call(
        kernel,
        out_shape=outs,
        in_specs=specs,
        out_specs=jax.tree.map(lambda _: pl.BlockSpec(memory_space=pltpu.VMEM), outs),
        scratch_shapes=list(scratch),
        compiler_params=pltpu.CompilerParams(vmem_limit_bytes=(60 if far else 40) * 1024 * 1024),
        cost_estimate=pl.CostEstimate(flops=flops, bytes_accessed=moved, transcendentals=0),
    )(*args)


def place():
    return lax.axis_index(ROW), lax.axis_index("zh"), lax.axis_index(NEAR)


def put_stats(rows_ref, note_ref):
    slabs = [rows_ref[:, :, 256 + 128 * t : 384 + 128 * t].astype(F32) for t in range(4)]
    x = jnp.concatenate(slabs, axis=0).reshape(32, 2, GROUP, 128)
    mean = jnp.sum(x, axis=(0, 2), keepdims=True) / (32 * GROUP)
    off = x - mean
    note_ref[0:2] = mean.reshape(2, 128)
    note_ref[2:4] = jnp.sum(off * off, axis=(0, 2))


def fetch(pairs, sems):
    copies = [pltpu.make_async_copy(src, dst, sems.at[i]) for i, (src, dst) in enumerate(pairs)]
    for copy in copies:
        copy.start()
    return copies


def begin_kernel(
    x_hbm, cache_hbm, gain_hbm, shift_hbm, w_hbm,
    raw_ref, later_ref, stats_ref, own_ref, side_ref, far_ref,
    x_ref, cache_ref, gain_ref, shift_ref, w_ref, note_ref, pieces_ref, sems,
):
    copies = fetch(
        (
            (x_hbm, x_ref), (cache_hbm, cache_ref), (gain_hbm, gain_ref), (shift_hbm, shift_ref),
            (w_hbm, w_ref),
        ),
        sems,
    )
    copies[0].wait()
    copies[1].wait()
    for r in range(8):
        for t in range(2):
            lanes = slice(128 * t, 128 * (t + 1))
            raw_ref[r, :, lanes] = cache_ref[0, t, r]
            later_ref[r, :, lanes] = cache_ref[1, t, r]
        for t in range(4):
            raw_ref[r, :, 256 + 128 * t : 384 + 128 * t] = x_ref[t, r]
    for copy in copies[2:]:
        copy.wait()
    row, me, _ = place()
    core = lax.rem(row, 2)
    for q in range(4):
        ahead = lax.rem(q + 4 - me, 4)
        for layer in range(2):
            for dt in range(3):
                for dc in range(3):
                    taps = [
                        w_ref[layer, 9 * dt + 3 * dr + dc, :, 64 * q : 64 * (q + 1)] for dr in range(3)
                    ]
                    pieces_ref[ahead, layer, dt, dc] = jnp.concatenate(taps, axis=1)
    own_ref[...] = pieces_ref[0]
    side_ref[...] = pieces_ref[1 + 2 * core]
    far_ref[...] = pieces_ref[2, core]
    note_ref[...] = jnp.zeros((8, 128), F32)
    for layer in range(2):
        note_ref[4 + layer : 5 + layer, 0:16] = gain_ref[layer : layer + 1, :]
        note_ref[6 + layer : 7 + layer, 0:16] = shift_ref[layer : layer + 1, :]
    put_stats(raw_ref, note_ref)
    stats_ref[...] = jnp.broadcast_to(note_ref[...][None], stats_ref.shape)


def shift_columns(left, centre, right):
    lane = lax.broadcasted_iota(jnp.int32, left.shape, left.ndim - 1)
    axis = left.ndim - 1
    left = jnp.where(lane == 0, 0.0, pltpu.roll(left, 1, axis))
    right = jnp.where(lane == 127, 0.0, pltpu.roll(right, 127, axis))
    return left + centre + right


def get_affine(layer, stats_ref, notes_ref, affine_ref):
    stats = stats_ref[...]
    stats = stats.reshape(16, 4, stats.shape[1], 128)
    number = 32 * GROUP
    means = stats[:, :, 0:2]
    mean = jnp.mean(means, axis=(0, 3), keepdims=True)
    off = means - mean
    total = jnp.sum(stats[:, :, 2:4] + number * (off * off), axis=(0, 3), keepdims=True)
    inverse = lax.rsqrt(total / (number * 16 * 128) + EPS)
    mean = jnp.broadcast_to(mean.reshape(4, 2, 1, 1), (4, 2, GROUP, 128)).reshape(4, 16, 128)
    inverse = jnp.broadcast_to(inverse.reshape(4, 2, 1, 1), (4, 2, GROUP, 128)).reshape(4, 16, 128)
    shape = (4, 16, 128)
    same = lax.broadcasted_iota(jnp.int32, shape, 1) == lax.broadcasted_iota(jnp.int32, shape, 2)
    gain = jnp.sum(jnp.where(same, notes_ref[0:4, 4 + layer : 5 + layer], 0.0), axis=2, keepdims=True)
    shift = jnp.sum(jnp.where(same, notes_ref[0:4, 6 + layer : 7 + layer], 0.0), axis=2, keepdims=True)
    affine_ref[0] = mean
    affine_ref[1] = inverse * gain
    affine_ref[2] = jnp.broadcast_to(shift, shape)


def products(layer, w_refs, o_refs, slab_ref):
    for r in range(8):
        rows = slab_ref[r : r + 3].reshape(192, 768)
        prod = jnp.zeros((96, 512), F32)
        for dt in range(3):
            held = jnp.concatenate([ref(dt).reshape(48, 192) for ref in w_refs], axis=0)
            prod += dot(held, rows[:, 128 * dt : 128 * dt + 512])
        prod = prod.reshape(2, 3, 16, 512)
        for t in range(4):
            lanes = slice(128 * t, 128 * (t + 1))
            part = prod[:, :, :, lanes]
            summed = shift_columns(part[:, 0], part[:, 1], part[:, 2]).astype(BF16)
            for q, o_ref in enumerate(o_refs):
                o_ref[r, :, lanes] = summed[q]


def near_kernel(layer, slab_ref, own_ref, side_ref, o0_ref, o1_ref):
    w_refs = (lambda dt: own_ref[layer, dt], lambda dt: side_ref[layer, dt])
    products(layer, w_refs, (o0_ref, o1_ref), slab_ref)


def conv_kernel(
    layer, a_ref, b_ref, c_ref, d_ref, next_ref, chip_ref, stats_ref, notes_ref, other_ref, far_ref, far2_ref,
    o2_ref, o3_ref, slab_ref, affine_ref, held_ref,
):
    row, _, here = place()
    get_affine(layer, stats_ref, notes_ref, affine_ref)
    upper = lax.rem(row, 2) == 0
    not_top = (row > 0).astype(F32)
    not_bottom = (row < 15).astype(F32)
    for k, ref in enumerate((a_ref, b_ref, c_ref, d_ref)):
        b = lax.bitwise_xor(here, k)
        mean = affine_ref[0, b]
        gain = affine_ref[1, b]
        shift = affine_ref[2, b]
        for r in range(10):
            for t in range(6):
                lanes = slice(128 * t, 128 * (t + 1))
                if r == 0:
                    x = jnp.where(upper, next_ref[k, :, lanes].astype(F32), chip_ref[k, :, lanes].astype(F32))
                elif r == 9:
                    x = jnp.where(upper, chip_ref[k, :, lanes].astype(F32), next_ref[k, :, lanes].astype(F32))
                elif t < 2:
                    x = ref[r - 1, :, lanes]
                else:
                    x = ref[r - 1, :, lanes].astype(F32)
                if t >= 2:
                    x = silu((x - mean) * gain + shift)
                if r == 0:
                    x = x * not_top
                if r == 9:
                    x = x * not_bottom
                slab_ref[r, b, :, lanes] = x.astype(BF16)
    core = lax.rem(row, 2)

    @pl.when(core == layer)
    def _():
        held_ref[...] = far_ref[...]

    @pl.when(core != layer)
    def _():
        held_ref[...] = far2_ref[...]

    w_refs = (lambda dt: other_ref[layer, dt], lambda dt: held_ref[dt])
    products(layer, w_refs, (o2_ref, o3_ref), slab_ref)


def merge_kernel(a_ref, b_ref, c_ref, bias_ref, later_ref, mid_ref, stats_ref, note_ref):
    bias = jnp.concatenate([bias_ref[...]] * 4, axis=1)
    for r in range(8):
        summed = a_ref[r].astype(F32) + b_ref[r].astype(F32) + c_ref[r].astype(F32)
        mid_ref[r, :, 0:256] = later_ref[r]
        mid_ref[r, :, 256:768] = (summed + bias).astype(BF16)
    put_stats(mid_ref, note_ref)
    stats_ref[...] = jnp.broadcast_to(note_ref[...][None], stats_ref.shape)


def last_kernel(x_ref, a_ref, b_ref, c_ref, bias_ref, o_ref):
    bias = bias_ref[...]
    for r in range(8):
        for t in range(4):
            lanes = slice(128 * t, 128 * (t + 1))
            branch = a_ref[r, :, lanes].astype(F32) + b_ref[r, :, lanes].astype(F32)
            branch += c_ref[r, :, lanes].astype(F32)
            o_ref[t, r] = (x_ref[t, r].astype(F32) + (branch + bias)).astype(BF16)


def sides(step):
    return [(i, (i + step) % 4) for i in range(4)] + [(4 + i, 4 + (i - step) % 4) for i in range(4)]


def add_kernel(a_ref, b_ref, o_ref):
    o_ref[...] = (a_ref[...].astype(F32) + b_ref[...].astype(F32)).astype(BF16)


def convolve(layer, inputs, own, side, far, other, far2):
    part = struct((8, 16, 512))
    flops = 2 * 96 * 576 * 4096
    other, far, slab = call(
        functools.partial(conv_kernel, layer), (part, part, struct((10, 4, 16, 768))),
        *inputs, other, far, far2,
        scratch=(pltpu.VMEM((3, 4, 16, 128), F32), pltpu.VMEM((3, 3, 16, 192), BF16)), flops=flops,
    )
    far = lax.ppermute(far, ("core", "zh"), sides(-1))
    other = lax.ppermute(other, ("core", "zh"), sides(1))
    own, side = call(
        functools.partial(near_kernel, layer), (part, part), slab, own, side, flops=flops
    )
    side = call(add_kernel, part, side, far)
    side = lax.ppermute(side, ("core", "zh"), sides(-1))
    return [own, other, side]


def struct(shape, dtype=BF16):
    return jax.ShapeDtypeStruct(shape, dtype)


def edge_kernel(a_ref, b_ref, c_ref, d_ref, chip_ref, next_ref):
    upper = lax.rem(lax.axis_index(ROW), 2) == 0
    towards = jnp.where(upper, 7, 0)
    for k, ref in enumerate((a_ref, b_ref, c_ref, d_ref)):
        chip_ref[k] = ref[towards]
        next_ref[k] = ref[7 - towards]


def rows_beside(blocks):
    chip, beyond = call(edge_kernel, (struct((4, 16, 768)), struct((4, 16, 768))), *blocks, flops=2 * 10**10)
    pairs = [(i, i + 1) for i in range(1, 15, 2)] + [(i + 1, i) for i in range(1, 15, 2)]
    beyond = lax.ppermute(beyond, ROW, pairs)
    chip = lax.ppermute(chip, ROW, [(i, i ^ 1) for i in range(16)])
    return [beyond, chip]


def near(x):
    return [x] + [lax.ppermute(x, NEAR, [(i, i ^ k) for i in range(4)]) for k in (1, 2, 3)]


def exchange(x, axes):
    return lax.all_to_all(x, axes, 0, 0, tiled=True)


def local(frames, cache, norm_gain, norm_shift, conv_weight, conv_bias):
    note = pltpu.VMEM((8, 128), F32)
    piece = (2, 3, 3, 16, 192)
    raw, later, stats, own, side, far = call(
        begin_kernel,
        (
            struct((8, 16, 768)), struct((8, 16, 256)), struct((64, 8, 128), F32), struct(piece),
            struct(piece), struct(piece[1:]),
        ),
        frames, cache, norm_gain, norm_shift, conv_weight.transpose(0, 2, 1, 3),
        scratch=(
            pltpu.VMEM((4, 8, 16, 128), BF16), pltpu.VMEM((2, 2, 8, 16, 128), BF16),
            pltpu.VMEM((2, 16), F32), pltpu.VMEM((2, 16), F32), pltpu.VMEM((2, 27, 16, 256), BF16),
            note, pltpu.VMEM((4,) + piece, BF16), pltpu.SemaphoreType.DMA((5,)),
        ),
        far=(0, 1, 2, 3, 4),
    )
    side = lax.ppermute(side, ("core", "zh"), sides(1))
    far = lax.ppermute(far, "zh", [(i, (i + 2) % 4) for i in range(4)])
    raw = near(raw)
    stats = exchange(stats, ROW + NEAR)
    raw = raw + rows_beside(raw)
    swap = [(0, 1), (1, 0)]
    weights = [own, side, far, lax.ppermute(side, "core", swap), lax.ppermute(far, "core", swap)]
    bias = jnp.broadcast_to(conv_bias[:, :, None], (2, 16, 128))
    notes = stats
    partial = convolve(0, [*raw, stats, notes], *weights)
    middle, stats = call(
        merge_kernel, (struct((8, 16, 768)), struct((64, 4, 128), F32)), *partial, bias[0], later,
        scratch=(pltpu.VMEM((4, 128), F32),),
    )
    middle = near(middle)
    stats = exchange(stats, ROW + NEAR)
    middle = middle + rows_beside(middle)
    partial = convolve(1, [*middle, stats, notes], *weights)
    return call(last_kernel, struct((4, 8, 16, 128)), frames, *partial, bias[1])


def solution(mesh):
    fine = Mesh(mesh.devices.reshape(2, 4, 2, 4, 2, 2), ROW + CHAN)
    placed = (
        P(None, ROW, CHAN, None),
        P(None, None, ROW, CHAN, None),
        P(None, CHAN),
        P(None, CHAN),
        P(None, CHAN, None, None),
        P(None, CHAN),
    )
    return jax.shard_map(
        local, mesh=fine, in_specs=placed, out_specs=P(None, ROW, CHAN, None), check_vma=False
    )
```
